32 devices in a mesh: rows: 4 (over z), cols: 8 (over y, x, core).
Axes of the slice: x: 2, y: 2, z: 4, core: 2. Of those that a mesh axis runs over, the one named last changes fastest.
Arguments:
- observed: float32 [426, 64, 1024], P(None, 'rows', 'cols'), may hold values from 0.05 to 3
- nonlin: float32 [64, 1024], P('rows', 'cols'), may hold values from -0.3 to 0.3
- abundance: float32 [64, 64, 1024], P(None, 'rows', 'cols'), may hold values from 0 to 2
- spectra: float32 [426, 64], replicated, may hold values from 0.1 to 1
- kernels: float32 [8, 9, 9], replicated, may hold values from 0.003 to 0.03
- tile_family: int32 [4, 8], P('rows', 'cols'), may hold values from 0 to 7
Outputs:
- abundance_out: float32 [64, 64, 1024], P(None, 'rows', 'cols')
- spectra_out: float32 [426, 64], replicated
The draws below stay inside these ranges and needn't reach their ends.
All inputs are finite; a program needn't handle non-finite values.
Results may differ from the reference program's by a relative error of at most 0.0003.
Values sent between devices are 32-bit elements; how exact they have to be, the bound alone decides.
No kernel may reach another device: no remote copies, remote signals or barrier semaphores. Data moves between devices by JAX's collectives and lax.ppermute only.
A program may use at most 64 MiB of HBM per device.

```python
import math
import jax
import jax.numpy as jnp
from jax import lax

L = 426
P_SIZE = 64
KS = 9
FAMILIES = 8
ITERS = 3
CH = 16
CW = 128
NH = 64
NW = 1024
TILE_ROWS = 4
TILE_COLS = 8


def draw_observed(key, part):
    row_ramp = jnp.arange(NH, dtype=jnp.float32)[:, None] / NH
    col_ramp = jnp.arange(NW, dtype=jnp.float32)[None, :] / NW
    shading = 1.0 + row_ramp + col_ramp
    base = jnp.exp(jax.random.uniform(key, (L, NH, NW), jnp.float32, math.log(0.05), 0.0))
    return base * shading[None]


def plant(values, key, low, high):
    extent = values.shape
    spot = [jax.random.randint(jax.random.fold_in(key, axis), (), 0, extent[axis]) for axis in range(len(extent))]
    values = values.at[tuple(spot)].set(low)
    longest = extent.index(max(extent))
    spot[longest] = (spot[longest] + 1) % extent[longest]
    return values.at[tuple(spot)].set(high)


def block_levels(key, dims, split, smallest, largest):
    def one(position, shards_of):
        draws = jax.random.uniform(jax.random.fold_in(jax.random.fold_in(key, 6), position), (shards_of,), jnp.float32, smallest / len(split), largest / len(split))
        return jnp.repeat(jnp.exp(draws), dims[position] // shards_of).reshape((-1,) + (1,) * (len(dims) - position - 1))

    loudness = one(*split[0])
    for cut in split[1:]:
        loudness = loudness * one(*cut)
    return loudness


def setup_inputs(seed: int = 0) -> dict:
    key_list = jax.random.split(jax.random.key(seed), 7)
    return {
        "observed": draw_observed(jax.random.fold_in(key_list[6], 71), 0),
        "nonlin": jnp.clip(jax.random.uniform(key_list[1], (NH, NW), jnp.float32, -0.3, 0.3) * block_levels(key_list[1], (NH, NW), ((0, 4), (1, 8)), -0.4, 0.0), -0.3, 0.3),
        "abundance": jnp.clip(2.0 * jax.random.uniform(key_list[2], (P_SIZE, NH, NW), jnp.float32) ** block_levels(key_list[2], (P_SIZE, NH, NW), ((1, 4), (2, 8)), -0.2, 0.2), 0.0, 2.0),
        "spectra": jnp.clip(jax.random.uniform(key_list[3], (L, P_SIZE), jnp.float32, 0.1, 1.0), 0.1, 1.0),
        "kernels": jnp.clip(jnp.exp(jax.random.uniform(key_list[4], (FAMILIES, KS, KS), jnp.float32, math.log(0.003), math.log(0.03))), 0.003, 0.03),
        "tile_family": plant(jax.random.randint(key_list[5], (TILE_ROWS, TILE_COLS), 0, FAMILIES), jax.random.fold_in(key_list[5], 1), 0, FAMILIES - 1).astype(jnp.int32),
    }


def blur(abundance, tile_family, kernels):
    radius = KS // 2
    family_map = jnp.repeat(jnp.repeat(tile_family, CH, axis=0), CW, axis=1)
    table = kernels.reshape(kernels.shape[0], KS * KS)
    padded = jnp.pad(abundance, ((0, 0), (radius, radius), (radius, radius)))

    def add_tap(total, tap):
        row_shift = tap // KS
        col_shift = tap % KS
        column = lax.dynamic_slice_in_dim(table, tap, 1, 1)[:, 0]
        weight_map = jnp.take(column, family_map, axis=0)
        window = lax.dynamic_slice(padded, (jnp.int32(0), row_shift, col_shift), (P_SIZE, NH, NW))
        return (total + weight_map[None] * window, None)
    start = jnp.zeros((P_SIZE, NH, NW), jnp.float32)
    total, _ = lax.scan(add_tap, start, jnp.arange(KS * KS, dtype=jnp.int32))
    return total

def spectral(observed, nonlin, blurred, spectra):
    highest = lax.Precision.HIGHEST

    def strip(carry, index):
        start = index * CH
        pixels = lax.dynamic_slice_in_dim(observed, start, CH, 1).reshape(L, CH * NW)
        maps = lax.dynamic_slice_in_dim(blurred, start, CH, 1).reshape(P_SIZE, CH * NW)
        bend = lax.dynamic_slice_in_dim(nonlin, start, CH, 0).reshape(CH * NW)
        linear = jnp.dot(spectra, maps, precision=highest, preferred_element_type=jnp.float32) / P_SIZE
        resid = linear + bend[None] * linear * linear - pixels
        weighted = resid * (1.0 + 2.0 * bend[None] * linear)
        grad_flat = jnp.dot(spectra.T, weighted, precision=highest, preferred_element_type=jnp.float32) / P_SIZE
        part = jnp.dot(weighted, maps.T, precision=highest, preferred_element_type=jnp.float32) / P_SIZE
        return (carry + part, grad_flat.reshape(P_SIZE, CH, NW))
    start = jnp.zeros((L, P_SIZE), jnp.float32)
    total, strips = lax.scan(strip, start, jnp.arange(NH // CH, dtype=jnp.int32))
    grad_blur = jnp.transpose(strips, (1, 0, 2, 3)).reshape(P_SIZE, NH, NW)
    return (grad_blur, total)

def reference(observed, nonlin, abundance, spectra, kernels, tile_family):
    current = abundance
    endmembers = spectra
    pixel_count = NH * NW
    for step in range(ITERS):
        blurred, adjoint_fn = jax.vjp(lambda maps: blur(maps, tile_family, kernels), current)
        grad_blur, grad_spectra = spectral(observed, nonlin, blurred, endmembers)
        grad_abund = adjoint_fn(grad_blur)[0]
        current = jnp.maximum(current - 0.5 * grad_abund, 0.0)
        endmembers = jnp.maximum(endmembers - 40.0 * (grad_spectra / pixel_count), 0.0)
    return (current, endmembers)
```

```python
import functools

import jax
import jax.numpy as jnp
import numpy as np
from jax import lax
from jax.experimental import pallas as pl
from jax.experimental.pallas import tpu as pltpu
from jax.sharding import PartitionSpec as P

KS = 9
RADIUS = KS // 2
EDGE = 2 * RADIUS
ITERS = 3
F32 = jnp.float32
BF16 = jnp.bfloat16
VMEM = pl.BlockSpec(memory_space=pltpu.VMEM)
SMEM = pl.BlockSpec(memory_space=pltpu.SMEM)
PARAMS = pltpu.CompilerParams(vmem_limit_bytes=52 * 1024 * 1024)
ROW_ODD, COL_ODD, UP, DOWN, LEFT, RIGHT, HALF = range(7)


def split(x):
    high = x.astype(BF16)
    return high, (x - high.astype(F32)).astype(BF16)


def mm(a, b):
    return jnp.dot(a, b, preferred_element_type=F32)


def mm_nt(a, b):
    return lax.dot_general(a, b, (((1,), (1,)), ((), ())), preferred_element_type=F32)


def lanes(shape):
    return lax.broadcasted_iota(jnp.int32, shape, len(shape) - 1)


def edges(rows, swapped):
    count = len(rows)
    lane = lanes(rows[0].shape)
    width = rows[0].shape[1]
    out = jnp.zeros_like(rows[0])
    for i, row in enumerate(rows):
        place = (i + count // 2) % count if swapped else i
        first = 0 if swapped else width - EDGE
        moved = pltpu.roll(row, (place * EDGE - first) % width, 1)
        out = jnp.where(lane // EDGE == place, moved, out)
    return out


def wide(x, total, shift):
    padded = jnp.concatenate([x, jnp.zeros((x.shape[0], total - x.shape[1]), x.dtype)], axis=1)
    return pltpu.roll(padded, shift % total, 1)


def assemble_side(left, right, above, below, height):
    total = 2 * left.shape[1]
    lane = lanes((left.shape[0], total))
    row, col = lane // EDGE, lane % EDGE
    on_left = col < RADIUS
    own = (row >= RADIUS) & (row < RADIUS + height)
    top = row < RADIUS
    bottom = (row >= RADIUS + height) & (row < 2 * RADIUS + height)
    half = EDGE * height // 2
    lo = RADIUS * EDGE - RADIUS
    hi = RADIUS * EDGE + RADIUS
    base = (RADIUS + height) * EDGE
    out = jnp.zeros((left.shape[0], total), F32)
    out = jnp.where(own & on_left, wide(left, total, lo), out)
    first = (row - RADIUS) < height // 2
    out = jnp.where(own & ~on_left & first, wide(right, total, hi - half), out)
    out = jnp.where(own & ~on_left & ~first, wide(right, total, hi + half), out)
    out = jnp.where(top & ~on_left, wide(above, total, RADIUS - RADIUS * EDGE), out)
    out = jnp.where(top & on_left, wide(above, total, -half - RADIUS * EDGE - RADIUS), out)
    out = jnp.where(bottom & on_left, wide(below, total, base - RADIUS), out)
    out = jnp.where(bottom & ~on_left, wide(below, total, base + RADIUS - half), out)
    return out


def add_rim(row, contrib, index):
    width = row.shape[1]
    start = index * EDGE
    part = contrib[:, start // width * width : start // width * width + width]
    moved = pltpu.roll(part, (-(start % width) - RADIUS) % width, 1)
    lane = lanes(row.shape)
    near = (lane < RADIUS) | (lane >= width - RADIUS)
    return row + jnp.where(near, moved, 0.0)


def first_kernel(family, a_ref, place, rows_ref, e_core, e_cross):
    channels, height, width = a_ref.shape
    rows = []
    for i in range(height):
        row = a_ref[:, i, :]
        rows_ref[i] = row
        rows.append(row)
    low, high = edges(rows, True), edges(rows, False)
    odd = place[COL_ODD] == 1
    e_core[:channels] = jnp.where(odd, low, high)
    e_cross[:channels] = jnp.where(odd, high, low)
    mark = jnp.full((8, width), family[0, 0].astype(F32), F32)
    e_core[channels:] = mark
    e_cross[channels:] = mark


def band_sum(taps, delta):
    total = jnp.zeros(delta.shape, F32)
    for v in range(KS):
        total = jnp.where(delta == v, taps[v], total)
    return total


def build_main(taps, w_high, w_low, index, width):
    shape = (width, width)
    delta = lax.broadcasted_iota(jnp.int32, shape, 0) - lax.broadcasted_iota(jnp.int32, shape, 1) + RADIUS
    blank = jnp.zeros(shape, BF16)
    for u in range(-1, KS + 1):
        if 0 <= u < KS:
            high, low = split(band_sum([taps(u, v) for v in range(KS)], delta))
        else:
            high, low = blank, blank
        for r in range(2):
            for ro in range(2):
                if (u + ro - r) % 2 == 0:
                    d = (u + ro - r) // 2
                    if 0 <= d <= RADIUS:
                        at = index + (d, slice(r * width, r * width + width), slice(ro * width, ro * width + width))
                        w_high[at] = high
                        w_low[at] = low


def rim_column(lane, width):
    c = lane % EDGE
    return jnp.where(c < RADIUS, width - RADIUS + c, c - RADIUS)


def side_column(lane, width):
    c = lane % EDGE
    return jnp.where(c < RADIUS, c - RADIUS, width + c - RADIUS)


def forward_weights(k9, w_high, w_low, s_high, s_low, height, width):
    own = lambda u, v: k9[4, u * KS + v]
    build_main(own, w_high, w_low, (), width)
    n = height * EDGE
    shape = (EDGE, n)
    lane = lanes(shape)
    c = lax.broadcasted_iota(jnp.int32, shape, 0)
    delta = side_column(c, width) - rim_column(lane, width) + RADIUS
    out_row = lane // EDGE
    bands = [band_sum([own(u, v) for v in range(KS)], delta) for u in range(KS)]
    rows = s_high.shape[0] // EDGE
    for a in range(0, rows, 2):
        blocks = []
        for b in (a, a + 1):
            total = jnp.zeros(shape, F32)
            for u in range(KS):
                total = jnp.where(out_row == b - u, bands[u], total)
            blocks.append(total)
        high, low = split(jnp.concatenate(blocks, axis=0))
        s_high[a * EDGE : a * EDGE + 2 * EDGE] = high
        s_low[a * EDGE : a * EDGE + 2 * EDGE] = low


def adjoint_weights_kernel(k9, w_high, w_low, s_high, s_low, scratch, *, height, width):
    for b in range(3):
        build_main(lambda u, v, b=b: k9[3 * b + 1, (KS - 1 - u) * KS + KS - 1 - v], w_high, w_low, (b,), width)
    n = s_high.shape[1]
    half = n // 2
    shape = (EDGE, n)
    lane = lanes(shape)
    c = lax.broadcasted_iota(jnp.int32, shape, 0)
    to_side = lane < half
    column = jnp.where(to_side, side_column(lane, width), rim_column(lane, width))
    out_row = jnp.where(to_side, lane, lane - half) // EDGE
    out_row = jnp.where(out_row < height + EDGE, out_row, -KS - 1)
    sources = (c - EDGE, width + c, rim_column(c, width))
    chunk = height * EDGE
    mid = chunk // 2

    def place_of(kind, q):
        i = q - EDGE
        if kind == 2:
            return 4 * chunk + q * EDGE
        if 0 <= i < height:
            return i * EDGE if kind == 0 else chunk + (i + height // 2) % height * EDGE
        if i < 0:
            return 2 * chunk + (mid if kind == 0 else 0) + q * EDGE
        return 3 * chunk + (0 if kind == 0 else mid) + (i - height) * EDGE

    for kind in range(3):
        delta = sources[kind] - column + RADIUS
        if kind == 2:
            delta = jnp.where(to_side, delta, -1)
        for b in range(3):
            tile = 3 * b + (0, 2, 1)[kind]
            bands = [
                band_sum([k9[tile, (KS - 1 - u) * KS + KS - 1 - v] for v in range(KS)], delta) for u in range(KS)
            ]
            q_range = (range(0, EDGE), range(EDGE, EDGE + height), range(EDGE + height, 2 * EDGE + height))[b]
            for q in q_range:
                total = jnp.zeros(shape, F32)
                for u in range(KS):
                    if 0 <= q - u < height + EDGE:
                        total = jnp.where(out_row == q - u, bands[u], total)
                at = place_of(kind, q)
                scratch[at : at + EDGE] = total
    for start in range(0, scratch.shape[0], 64):
        high, low = split(scratch[start : start + 64])
        s_high[start : start + 64] = high
        s_low[start : start + 64] = low


def blur_into(b_ref, a2_high, a2_low, side, w_high, w_low, s_high, s_low, acc):
    pairs, channels, double = acc.shape
    width = double // 2
    for d in range(RADIUS + 1):
        high = a2_high[d : d + pairs].reshape(pairs * channels, double)
        low = a2_low[d : d + pairs].reshape(pairs * channels, double)
        part = mm(high, w_high[d]) + mm(low, w_high[d]) + mm(high, w_low[d])
        part = part.reshape(pairs, channels, double)
        if d == 0:
            acc[...] = part
        else:
            acc[...] += part
    side_high, side_low = split(side)
    rim = mm(side_high, s_high[...]) + mm(side_low, s_high[...]) + mm(side_high, s_low[...])
    for i in range(2 * pairs):
        row = acc[i // 2, :, i % 2 * width : i % 2 * width + width]
        b_ref[i] = add_rim(row, rim, i)


def start_kernel(
    rows_ref, p1, p2, left, right, above, below, k9, place,
    ext_ref, side_ref, b_ref, w_high, w_low, s_high, s_low,
    a2_high, a2_low, acc,
):
    height, channels, width = rows_ref.shape
    forward_weights(k9, w_high, w_low, s_high, s_low, height, width)
    odd = place[ROW_ODD] == 1
    for a in range(height + EDGE):
        if a < RADIUS:
            row = jnp.where(odd, p1[a * channels : a * channels + channels], p2[a * channels : a * channels + channels])
        elif a < RADIUS + height:
            row = rows_ref[a - RADIUS]
        else:
            k = (a - RADIUS - height) * channels
            row = jnp.where(odd, p2[k : k + channels], p1[k : k + channels])
        ext_ref[a] = row
        high, low = split(row)
        a2_high[a // 2, :, a % 2 * width : a % 2 * width + width] = high
        a2_low[a // 2, :, a % 2 * width : a % 2 * width + width] = low
    side = assemble_side(left[...], right[...], above[...], below[...], height)
    side_ref[...] = side
    blur_into(b_ref, a2_high, a2_low, side, w_high, w_low, s_high, s_low, acc)


def spectral_kernel(
    obs_ref, bend_ref, b_ref, mine, other, place,
    g_mine, core_ref, main1, main2, cross_ref, rows_ref,
    total, *, scale,
):
    height, channels, width = b_ref.shape
    bands = obs_ref.shape[1]
    quarter = bands // 4
    second = place[HALF] == 1
    m0 = jnp.where(second, other[...], mine[...])
    m1 = jnp.where(second, mine[...], other[...])
    spectra = jnp.concatenate([m0[:, :channels], m0[:, channels:], m1[:, :channels], m1[:, channels:]], axis=0)
    m_high, m_low = split(spectra)
    m_cat = jnp.concatenate([m_high, m_low, m_high], axis=1)
    t_high, t_low = split(spectra.T)
    t_cat = jnp.concatenate([t_high, t_low], axis=0)
    rows = []
    for pair in range(height // 2):
        b_pair = jnp.concatenate([b_ref[2 * pair], b_ref[2 * pair + 1]], axis=1)
        b_high, b_low = split(b_pair)
        b_cat = jnp.concatenate([b_high, b_high, b_low], axis=0)
        linear = mm(m_cat, b_cat) * scale
        seen = jnp.concatenate([obs_ref[2 * pair], obs_ref[2 * pair + 1]], axis=1)
        bend = jnp.concatenate([bend_ref[2 * pair : 2 * pair + 1], bend_ref[2 * pair + 1 : 2 * pair + 2]], axis=1)
        bent = bend * linear
        resid = linear + bent * linear - seen
        weighted = resid * (1.0 + 2.0 * bent)
        w_high, w_low = split(weighted)
        part = mm_nt(w_high, jnp.concatenate([b_high, b_low], axis=0))
        part = part[:, :channels] + part[:, channels:] + mm_nt(w_low, b_high)
        if pair == 0:
            total[...] = part
        else:
            total[...] += part
        both = mm(t_cat, w_high)
        grad = (both[:channels] + both[channels:] + mm(t_high, w_low)) * scale
        for k in range(2):
            row = grad[:, k * width : k * width + width]
            rows_ref[2 * pair + k] = row
            rows.append(row)
    low, high = edges(rows, True), edges(rows, False)
    col_odd = place[COL_ODD] == 1
    core_ref[2 * quarter // 2 :] = jnp.where(col_odd, low, high)
    cross_ref[...] = jnp.where(col_odd, high, low)
    row_odd = place[ROW_ODD] == 1
    half = height // 2
    for i in range(half):
        main1[i] = jnp.where(row_odd, rows[i], rows[half + i])
        main2[i] = jnp.where(row_odd, rows[half + i], rows[i])
    g = total[...] * scale
    g0 = jnp.concatenate([g[:quarter], g[quarter : 2 * quarter]], axis=1)
    g1 = jnp.concatenate([g[2 * quarter : 3 * quarter], g[3 * quarter :]], axis=1)
    g_mine[...] = jnp.where(second, g1, g0)
    core_ref[:quarter] = jnp.where(second, g0, g1)


def maps_kernel(
    ext_ref, side_ref, rows_ref, p1, p2, left, right, above, below, place,
    wa_high, wa_low, sa_high, sa_low, *rest, last,
):
    if last:
        out_ref, g2_high, g2_low, acc = rest
    else:
        (wf_high, wf_low, sf_high, sf_low, ext_out, side_out, b_ref, g2_high, g2_low, a2_high, a2_low, acc, acc_b) = rest
    height, channels, width = rows_ref.shape
    ext_rows = height + EDGE
    odd = place[ROW_ODD] == 1
    lane = lanes((channels, width))
    near = []
    for q in range(height + 2 * EDGE):
        if q < EDGE:
            row = jnp.where(odd, p1[q], p2[q])
        elif q < EDGE + height:
            row = rows_ref[q - EDGE]
        else:
            row = jnp.where(odd, p2[q - EDGE - height], p1[q - EDGE - height])
        high, low = split(row)
        g2_high[q // 2, :, q % 2 * width : q % 2 * width + width] = high
        g2_low[q // 2, :, q % 2 * width : q % 2 * width + width] = low
        if q % height == 0:
            near.append(jnp.zeros((channels, width), F32))
        moved = pltpu.roll(row, (RADIUS + q * EDGE) % width, 1)
        near[-1] = jnp.where(lane // EDGE == q % height, moved, near[-1])
    side_in = jnp.concatenate([left[...], right[...], above[...], below[...]] + near, axis=1)
    side_high, side_low = split(side_in)
    side_mm = mm(side_high, sa_high[...]) + mm(side_low, sa_high[...]) + mm(side_high, sa_low[...])
    half = side_mm.shape[1] // 2
    rim = side_mm[:, half:]
    n = EDGE // 2
    own = height // 2
    out_pairs = ext_rows // 2
    acc[...] = jnp.zeros_like(acc)
    for d in range(RADIUS + 1):
        for b in range(3):
            first, end = ((0, n), (n, n + own), (n + own, 2 * n + own))[b]
            first, end = max(first, d), min(end, out_pairs + d)
            if first >= end:
                continue
            high = g2_high[first:end].reshape((end - first) * channels, 2 * width)
            low = g2_low[first:end].reshape((end - first) * channels, 2 * width)
            part = mm(high, wa_high[b, d]) + mm(low, wa_high[b, d]) + mm(high, wa_low[b, d])
            acc[first - d : end - d] += part.reshape(end - first, channels, 2 * width)
    for a in range(ext_rows):
        if last and not RADIUS <= a < RADIUS + height:
            continue
        grad = add_rim(acc[a // 2, :, a % 2 * width : a % 2 * width + width], rim, a)
        row = jnp.maximum(ext_ref[a] - 0.5 * grad, 0.0)
        if last:
            out_ref[a - RADIUS] = row
            continue
        if a < RADIUS:
            row = jnp.where(place[UP] == 1, row, 0.0)
        elif a >= RADIUS + height:
            row = jnp.where(place[DOWN] == 1, row, 0.0)
        ext_out[a] = row
        high, low = split(row)
        a2_high[a // 2, :, a % 2 * width : a % 2 * width + width] = high
        a2_low[a // 2, :, a % 2 * width : a % 2 * width + width] = low
    if last:
        return
    side = jnp.maximum(side_ref[...] - 0.5 * side_mm[:, :half], 0.0)
    where = lanes(side.shape)
    a, c = where // EDGE, where % EDGE
    outside = (
        ((a < RADIUS) & (place[UP] == 0))
        | ((a >= RADIUS + height) & (place[DOWN] == 0))
        | ((c < RADIUS) & (place[LEFT] == 0))
        | ((c >= RADIUS) & (place[RIGHT] == 0))
        | (a >= ext_rows)
    )
    side = jnp.where(outside, 0.0, side)
    side_out[...] = side
    blur_into(b_ref, a2_high, a2_low, side, wf_high, wf_low, sf_high, sf_low, acc_b)


def call(kernel, outs, scratch, specs, *args):
    return pl.pallas_call(
        kernel,
        out_shape=[jax.ShapeDtypeStruct(s, d) for s, d in outs],
        in_specs=specs,
        out_specs=[VMEM] * len(outs),
        scratch_shapes=[pltpu.VMEM(s, d) for s, d in scratch],
        compiler_params=PARAMS,
    )(*args)


def core_swap(x):
    count = lax.axis_size("cols")
    return lax.ppermute(x, "cols", [(i, i ^ 1) for i in range(count)])


def cross_swap(x):
    count = lax.axis_size("cols")
    return lax.ppermute(x, "cols", [(i, (i + 1 if i % 2 else i - 1) % count) for i in range(count)])


def pair_one(x):
    count = lax.axis_size("rows")
    return lax.ppermute(x, "rows", [(i, i ^ 1) for i in range(count)])


def pair_two(x):
    count = lax.axis_size("rows")
    pairs = [(i, i + 1) for i in range(1, count - 1, 2)]
    return lax.ppermute(x, "rows", pairs + [(b, a) for a, b in pairs])


def chips_sum(x):
    count = lax.axis_size("cols")
    step = 4
    while step < count:
        route = [(i, (((i + 1) % count) ^ step) - 1) for i in range(count)]
        x = x + lax.ppermute(x, "cols", [(i, j % count) for i, j in route])
        step *= 2
    return x


def rows_sum(x):
    count = lax.axis_size("rows")
    step = 2
    while step < count:
        x = x + lax.ppermute(x, "rows", [(i, i ^ step) for i in range(count)])
        step *= 2
    return x


def on_device(observed, nonlin, abundance, spectra, kernels, tile_family):
    bands, height, width = observed.shape
    channels = abundance.shape[0]
    n_rows, n_cols = lax.axis_size("rows"), lax.axis_size("cols")
    row_at, col_at = lax.axis_index("rows"), lax.axis_index("cols")
    pixel_count = height * width * n_rows * n_cols
    quarter = -(-bands // 32) * 8
    full = 4 * quarter
    half_of = ((col_at + 1) // 2) % 2
    col_odd, row_odd = col_at % 2 == 1, row_at % 2 == 1
    place = jnp.stack(
        [row_at % 2, col_at % 2, row_at > 0, row_at < n_rows - 1, col_at > 0, col_at < n_cols - 1, half_of]
    ).astype(jnp.int32)
    has_left = (col_at > 0).astype(F32)
    has_right = (col_at < n_cols - 1).astype(F32)
    tile = (channels, width)

    def sides(core, cross):
        left = jnp.where(col_odd, core, cross) * has_left
        right = jnp.where(col_odd, cross, core) * has_right
        lane = lanes(tile) < width // 2
        up_msg = jnp.where(lane, left, right)
        down_msg = jnp.where(lane, right, left)
        return left, right, jnp.where(row_odd, up_msg, down_msg), jnp.where(row_odd, down_msg, up_msg)

    a_rows, e_core, e_cross = call(
        first_kernel,
        [((height,) + tile, F32), ((channels + 8, width), F32), ((channels + 8, width), F32)],
        [],
        [SMEM, VMEM, SMEM],
        tile_family, abundance, place,
    )
    got_core = core_swap(e_core)
    got_cross = cross_swap(e_cross)
    left, right, side1, side2 = sides(got_core[:channels], got_cross[:channels])
    fam_left = jnp.where(col_odd, got_core[channels, 0], got_cross[channels, 0])
    fam_right = jnp.where(col_odd, got_cross[channels, 0], got_core[channels, 0])
    fam_row = jnp.stack([fam_left, tile_family[0, 0].astype(F32), fam_right])
    marks = jnp.broadcast_to(jnp.concatenate([fam_row, jnp.zeros(5, F32)])[:, None], (8, width))
    top = a_rows[:RADIUS].reshape(RADIUS * channels, width)
    bottom = a_rows[height - RADIUS :].reshape(RADIUS * channels, width)
    got1 = pair_one(jnp.concatenate([jnp.where(row_odd, top, bottom), side1, marks]))
    got2 = pair_two(jnp.concatenate([jnp.where(row_odd, bottom, top), side2, marks]))
    body = RADIUS * channels

    def above_below(x1, x2):
        return jnp.where(row_odd, x1, x2), jnp.where(row_odd, x2, x1)

    above, below = above_below(got1[body : body + channels], got2[body : body + channels])
    fam_up, fam_down = above_below(got1[body + channels :, 0][:3], got2[body + channels :, 0][:3])
    families = jnp.concatenate([fam_up, fam_row, fam_down])
    choice = jnp.arange(kernels.shape[0], dtype=F32)[None, :, None] == families[:, None, None]
    k9 = jnp.sum(jnp.where(choice, kernels.reshape(1, kernels.shape[0], KS * KS), 0.0), axis=1)

    pairs = height // 2
    ext_rows = height + EDGE
    main_w = ((RADIUS + 1, 2 * width, 2 * width), BF16)
    side_f = ((2 * width, height * EDGE), BF16)
    ext, side, blurred, wf_high, wf_low, sf_high, sf_low = call(
        start_kernel,
        [((ext_rows,) + tile, F32), ((channels, 2 * width), F32), ((height,) + tile, F32), main_w, main_w, side_f, side_f],
        [((ext_rows // 2, channels, 2 * width), BF16)] * 2 + [((pairs, channels, 2 * width), F32)],
        [VMEM] * 7 + [SMEM, SMEM],
        a_rows, got1, got2, left, right, above, below, k9, place,
    )
    main_a = ((3, RADIUS + 1, 2 * width, 2 * width), BF16)
    side_a = ((6 * width, 4 * width), BF16)
    wa = call(
        functools.partial(adjoint_weights_kernel, height=height, width=width),
        [main_a, main_a, side_a, side_a],
        [((6 * width, 4 * width), F32)],
        [SMEM],
        k9,
    )

    seen = jnp.pad(jnp.transpose(observed, (1, 0, 2)), ((0, 0), (0, full - bands), (0, 0)))
    padded = jnp.pad(spectra, ((0, full - bands), (0, 0))).reshape(2, 2, quarter, channels)
    halves = jnp.transpose(padded, (0, 2, 1, 3)).reshape(2, quarter, 2 * channels)
    mine = lax.dynamic_index_in_dim(halves, half_of, 0, False)
    other = lax.dynamic_index_in_dim(halves, 1 - half_of, 0, False)
    rate = 40.0 / pixel_count
    for step in range(ITERS):
        last = step == ITERS - 1
        g_mine, to_core, main1, main2, e_cross, g_rows = call(
            functools.partial(spectral_kernel, scale=1.0 / channels),
            [
                ((quarter, 2 * channels), F32),
                ((quarter + channels, width), F32),
                ((height // 2,) + tile, F32),
                ((height // 2,) + tile, F32),
                (tile, F32),
                ((height,) + tile, F32),
            ],
            [((full, channels), F32)],
            [VMEM] * 5 + [SMEM],
            seen, nonlin, blurred, mine, other, place,
        )
        got_core = core_swap(to_core)
        p1 = pair_one(main1)
        p2 = pair_two(main2)
        share = g_mine + got_core[:quarter]
        got_cross = cross_swap(jnp.concatenate([share, e_cross]))
        share = share + got_cross[:quarter]
        left, right, side1, side2 = sides(got_core[quarter:], got_cross[quarter:])
        share = chips_sum(share)
        got1 = pair_one(jnp.concatenate([share, side1]))
        got2 = pair_two(side2)
        share = rows_sum(share + got1[:quarter])
        above, below = above_below(got1[quarter:], got2)
        mine = jnp.maximum(mine - rate * share, 0.0)
        other = core_swap(mine)
        gathered = (ext, side, g_rows, p1, p2, left, right, above, below, place) + tuple(wa)
        g2 = [((ext_rows // 2 + RADIUS, channels, 2 * width), BF16)] * 2
        acc = [((ext_rows // 2, channels, 2 * width), F32)]
        if last:
            (out,) = call(
                functools.partial(maps_kernel, last=True),
                [((height,) + tile, F32)],
                g2 + acc,
                [VMEM] * 9 + [SMEM] + [VMEM] * 4,
                *gathered,
            )
        else:
            ext, side, blurred = call(
                functools.partial(maps_kernel, last=False),
                [((ext_rows,) + tile, F32), ((channels, 2 * width), F32), ((height,) + tile, F32)],
                g2 + [((ext_rows // 2, channels, 2 * width), BF16)] * 2 + acc + [((pairs, channels, 2 * width), F32)],
                [VMEM] * 9 + [SMEM] + [VMEM] * 8,
                *gathered, wf_high, wf_low, sf_high, sf_low,
            )
    first = jnp.where(half_of == 0, mine, other)
    second = jnp.where(half_of == 0, other, mine)
    parts = [first[:, :channels], first[:, channels:], second[:, :channels], second[:, channels:]]
    return jnp.transpose(out, (1, 0, 2)), jnp.concatenate(parts)[:bands]


def solution(mesh):
    placed = (
        P(None, "rows", "cols"),
        P("rows", "cols"),
        P(None, "rows", "cols"),
        P(),
        P(),
        P("rows", "cols"),
    )
    return jax.shard_map(
        on_device,
        mesh=mesh,
        in_specs=placed,
        out_specs=(P(None, "rows", "cols"), P()),
        check_vma=False,
    )
```

```python
import functools

import jax
import jax.numpy as jnp
import numpy as np
from jax import lax
from jax.experimental import pallas as pl
from jax.experimental.pallas import tpu as pltpu
from jax.sharding import PartitionSpec as P

KS = 9
RADIUS = KS // 2
EDGE = 2 * RADIUS
ITERS = 3
F32 = jnp.float32
BF16 = jnp.bfloat16
VMEM = pl.BlockSpec(memory_space=pltpu.VMEM)
SMEM = pl.BlockSpec(memory_space=pltpu.SMEM)
PARAMS = pltpu.CompilerParams(vmem_limit_bytes=18 * 1024 * 1024)
ROW_ODD, COL_ODD, UP, DOWN, LEFT, RIGHT, HALF = range(7)


def split(x):
    high = x.astype(BF16)
    return high, (x - high.astype(F32)).astype(BF16)


def mm(a, b):
    return jnp.dot(a, b, preferred_element_type=F32)


def mm_nt(a, b):
    return lax.dot_general(a, b, (((1,), (1,)), ((), ())), preferred_element_type=F32)


def lanes(shape):
    return lax.broadcasted_iota(jnp.int32, shape, len(shape) - 1)


def edges(rows, swapped):
    count = len(rows)
    lane = lanes(rows[0].shape)
    width = rows[0].shape[1]
    out = jnp.zeros_like(rows[0])
    for i, row in enumerate(rows):
        place = (i + count // 2) % count if swapped else i
        first = 0 if swapped else width - EDGE
        moved = pltpu.roll(row, (place * EDGE - first) % width, 1)
        out = jnp.where(lane // EDGE == place, moved, out)
    return out


def wide(x, total, shift):
    padded = jnp.concatenate([x, jnp.zeros((x.shape[0], total - x.shape[1]), x.dtype)], axis=1)
    return pltpu.roll(padded, shift % total, 1)


def assemble_side(left, right, above, below, height):
    total = 2 * left.shape[1]
    lane = lanes((left.shape[0], total))
    row, col = lane // EDGE, lane % EDGE
    on_left = col < RADIUS
    own = (row >= RADIUS) & (row < RADIUS + height)
    top = row < RADIUS
    bottom = (row >= RADIUS + height) & (row < 2 * RADIUS + height)
    half = EDGE * height // 2
    lo = RADIUS * EDGE - RADIUS
    hi = RADIUS * EDGE + RADIUS
    base = (RADIUS + height) * EDGE
    out = jnp.zeros((left.shape[0], total), F32)
    out = jnp.where(own & on_left, wide(left, total, lo), out)
    first = (row - RADIUS) < height // 2
    out = jnp.where(own & ~on_left & first, wide(right, total, hi - half), out)
    out = jnp.where(own & ~on_left & ~first, wide(right, total, hi + half), out)
    out = jnp.where(top & ~on_left, wide(above, total, RADIUS - RADIUS * EDGE), out)
    out = jnp.where(top & on_left, wide(above, total, -half - RADIUS * EDGE - RADIUS), out)
    out = jnp.where(bottom & on_left, wide(below, total, base - RADIUS), out)
    out = jnp.where(bottom & ~on_left, wide(below, total, base + RADIUS - half), out)
    return out


def add_rim(row, contrib, index):
    width = row.shape[1]
    start = index * EDGE
    part = contrib[:, start // width * width : start // width * width + width]
    moved = pltpu.roll(part, (-(start % width) - RADIUS) % width, 1)
    lane = lanes(row.shape)
    near = (lane < RADIUS) | (lane >= width - RADIUS)
    return row + jnp.where(near, moved, 0.0)


def first_kernel(family, a_ref, place, rows_ref, e_core, e_cross, mark_ref):
    channels, height, width = a_ref.shape
    rows = []
    for i in range(height):
        row = a_ref[:, i, :]
        rows_ref[i] = row
        rows.append(row)
    low, high = edges(rows, True), edges(rows, False)
    odd = place[COL_ODD] == 1
    e_core[:channels] = jnp.where(odd, low, high)
    e_cross[:channels] = jnp.where(odd, high, low)
    mark = jnp.full((8, width), family[0, 0].astype(F32), F32)
    e_core[channels:] = mark
    e_cross[channels:] = mark
    mark_ref[...] = mark


def band_sum(taps, delta):
    total = jnp.zeros(delta.shape, F32)
    for v in range(KS):
        total = jnp.where(delta == v, taps[v], total)
    return total


def build_main(taps, w_high, w_low, index, width):
    shape = (width, width)
    delta = lax.broadcasted_iota(jnp.int32, shape, 0) - lax.broadcasted_iota(jnp.int32, shape, 1) + RADIUS
    blank = jnp.zeros(shape, BF16)
    for u in range(-1, KS + 1):
        if 0 <= u < KS:
            high, low = split(band_sum([taps(u, v) for v in range(KS)], delta))
        else:
            high, low = blank, blank
        for r in range(2):
            for ro in range(2):
                if (u + ro - r) % 2 == 0:
                    d = (u + ro - r) // 2
                    if 0 <= d <= RADIUS:
                        at = index + (d, slice(r * width, r * width + width), slice(ro * width, ro * width + width))
                        w_high[at] = high
                        w_low[at] = low


def rim_column(lane, width):
    c = lane % EDGE
    return jnp.where(c < RADIUS, width - RADIUS + c, c - RADIUS)


def side_column(lane, width):
    c = lane % EDGE
    return jnp.where(c < RADIUS, c - RADIUS, width + c - RADIUS)


def forward_weights_kernel(family, table, obs_ref, seen_ref, w_high, w_low, s_high, s_low, sems):
    depth, height, width = obs_ref.shape
    copies = []
    for i in range(height):
        copies.append(pltpu.make_async_copy(obs_ref.at[:, i, :], seen_ref.at[i, pl.ds(0, depth), :], sems.at[i]))
        copies[-1].start()
    start = depth // 8 * 8
    own = lambda u, v: table[family[0, 0], u * KS + v]
    build_main(own, w_high, w_low, (), width)
    n = height * EDGE
    shape = (EDGE, n)
    lane = lanes(shape)
    c = lax.broadcasted_iota(jnp.int32, shape, 0)
    delta = side_column(c, width) - rim_column(lane, width) + RADIUS
    out_row = lane // EDGE
    bands = [band_sum([own(u, v) for v in range(KS)], delta) for u in range(KS)]
    rows = s_high.shape[0] // EDGE
    for a in range(0, rows, 2):
        blocks = []
        for b in (a, a + 1):
            total = jnp.zeros(shape, F32)
            for u in range(KS):
                total = jnp.where(out_row == b - u, bands[u], total)
            blocks.append(total)
        high, low = split(jnp.concatenate(blocks, axis=0))
        s_high[a * EDGE : a * EDGE + 2 * EDGE] = high
        s_low[a * EDGE : a * EDGE + 2 * EDGE] = low
    for i in range(height):
        copies[i].wait()
    sub = lax.broadcasted_iota(jnp.int32, (seen_ref.shape[1] - start, width), 0)
    for i in range(height):
        seen_ref[i, start:] = jnp.where(sub < depth - start, seen_ref[i, start:], 0.0)


def adjoint_weights_kernel(families, table, w_high, w_low, s_high, s_low, scratch, *, height, width):
    for b in range(3):
        build_main(lambda u, v, b=b: table[families[3 * b + 1], (KS - 1 - u) * KS + KS - 1 - v], w_high, w_low, (b,), width)
    n = s_high.shape[1]
    half = n // 2
    shape = (EDGE, n)
    lane = lanes(shape)
    c = lax.broadcasted_iota(jnp.int32, shape, 0)
    to_side = lane < half
    column = jnp.where(to_side, side_column(lane, width), rim_column(lane, width))
    out_row = jnp.where(to_side, lane, lane - half) // EDGE
    out_row = jnp.where(out_row < height + EDGE, out_row, -KS - 1)
    sources = (c - EDGE, width + c, rim_column(c, width))
    chunk = height * EDGE
    mid = chunk // 2

    def place_of(kind, q):
        i = q - EDGE
        if kind == 2:
            return 4 * chunk + q * EDGE
        if 0 <= i < height:
            return i * EDGE if kind == 0 else chunk + (i + height // 2) % height * EDGE
        if i < 0:
            return 2 * chunk + (mid if kind == 0 else 0) + q * EDGE
        return 3 * chunk + (0 if kind == 0 else mid) + (i - height) * EDGE

    for kind in range(3):
        delta = sources[kind] - column + RADIUS
        if kind == 2:
            delta = jnp.where(to_side, delta, -1)
        for b in range(3):
            tile = 3 * b + (0, 2, 1)[kind]
            bands = [
                band_sum([table[families[tile], (KS - 1 - u) * KS + KS - 1 - v] for v in range(KS)], delta) for u in range(KS)
            ]
            q_range = (range(0, EDGE), range(EDGE, EDGE + height), range(EDGE + height, 2 * EDGE + height))[b]
            for q in q_range:
                total = jnp.zeros(shape, F32)
                for u in range(KS):
                    if 0 <= q - u < height + EDGE:
                        total = jnp.where(out_row == q - u, bands[u], total)
                at = place_of(kind, q)
                scratch[at : at + EDGE] = total
    for start in range(0, scratch.shape[0], 64):
        high, low = split(scratch[start : start + 64])
        s_high[start : start + 64] = high
        s_low[start : start + 64] = low


def blur_into(b_ref, a2_high, a2_low, side, w_high, w_low, s_high, s_low, acc):
    pairs, channels, double = acc.shape
    width = double // 2
    for d in range(RADIUS + 1):
        high = a2_high[d : d + pairs].reshape(pairs * channels, double)
        low = a2_low[d : d + pairs].reshape(pairs * channels, double)
        part = mm(high, w_high[d]) + mm(low, w_high[d]) + mm(high, w_low[d])
        part = part.reshape(pairs, channels, double)
        if d == 0:
            acc[...] = part
        else:
            acc[...] += part
    side_high, side_low = split(side)
    rim = mm(side_high, s_high[...]) + mm(side_low, s_high[...]) + mm(side_high, s_low[...])
    for i in range(2 * pairs):
        row = acc[i // 2, :, i % 2 * width : i % 2 * width + width]
        b_ref[i] = add_rim(row, rim, i)


def start_kernel(
    rows_ref, p1, p2, left, right, above, below, place, w_high, w_low, s_high, s_low,
    ext_ref, side_ref, b_ref, a2_high, a2_low, acc,
):
    height, channels, width = rows_ref.shape
    odd = place[ROW_ODD] == 1
    for a in range(height + EDGE):
        if a < RADIUS:
            row = jnp.where(odd, p1[a * channels : a * channels + channels], p2[a * channels : a * channels + channels])
        elif a < RADIUS + height:
            row = rows_ref[a - RADIUS]
        else:
            k = (a - RADIUS - height) * channels
            row = jnp.where(odd, p2[k : k + channels], p1[k : k + channels])
        ext_ref[a] = row
        high, low = split(row)
        a2_high[a // 2, :, a % 2 * width : a % 2 * width + width] = high
        a2_low[a // 2, :, a % 2 * width : a % 2 * width + width] = low
    side = assemble_side(left[...], right[...], above[...], below[...], height)
    side_ref[...] = side
    blur_into(b_ref, a2_high, a2_low, side, w_high, w_low, s_high, s_low, acc)


def spectral_kernel(
    obs_ref, bend_ref, b_ref, mine, other, place,
    g_mine, core_ref, main1, main2, cross_ref, rows_ref,
    total, *, scale,
):
    height, channels, width = b_ref.shape
    bands = obs_ref.shape[1]
    quarter = bands // 4
    second = place[HALF] == 1
    m0 = jnp.where(second, other[...], mine[...])
    m1 = jnp.where(second, mine[...], other[...])
    spectra = jnp.concatenate([m0[:, :channels], m0[:, channels:], m1[:, :channels], m1[:, channels:]], axis=0)
    m_high, m_low = split(spectra)
    m_cat = jnp.concatenate([m_high, m_low, m_high], axis=1)
    t_high, t_low = split(spectra.T)
    t_cat = jnp.concatenate([t_high, t_low], axis=0)
    rows = []
    for pair in range(height // 2):
        b_pair = jnp.concatenate([b_ref[2 * pair], b_ref[2 * pair + 1]], axis=1)
        b_high, b_low = split(b_pair)
        b_cat = jnp.concatenate([b_high, b_high, b_low], axis=0)
        linear = mm(m_cat, b_cat) * scale
        seen = jnp.concatenate([obs_ref[2 * pair], obs_ref[2 * pair + 1]], axis=1)
        bend = jnp.concatenate([bend_ref[2 * pair : 2 * pair + 1], bend_ref[2 * pair + 1 : 2 * pair + 2]], axis=1)
        bent = bend * linear
        resid = linear + bent * linear - seen
        weighted = resid * (1.0 + 2.0 * bent)
        w_high, w_low = split(weighted)
        part = mm_nt(w_high, jnp.concatenate([b_high, b_low], axis=0))
        part = part[:, :channels] + part[:, channels:] + mm_nt(w_low, b_high)
        if pair == 0:
            total[...] = part
        else:
            total[...] += part
        both = mm(t_cat, w_high)
        grad = (both[:channels] + both[channels:] + mm(t_high, w_low)) * scale
        for k in range(2):
            row = grad[:, k * width : k * width + width]
            rows_ref[2 * pair + k] = row
            rows.append(row)
    low, high = edges(rows, True), edges(rows, False)
    col_odd = place[COL_ODD] == 1
    core_ref[2 * quarter // 2 :] = jnp.where(col_odd, low, high)
    cross_ref[...] = jnp.where(col_odd, high, low)
    row_odd = place[ROW_ODD] == 1
    half = height // 2
    for i in range(half):
        main1[i] = jnp.where(row_odd, rows[i], rows[half + i])
        main2[i] = jnp.where(row_odd, rows[half + i], rows[i])
    g = total[...] * scale
    g0 = jnp.concatenate([g[:quarter], g[quarter : 2 * quarter]], axis=1)
    g1 = jnp.concatenate([g[2 * quarter : 3 * quarter], g[3 * quarter :]], axis=1)
    g_mine[...] = jnp.where(second, g1, g0)
    core_ref[:quarter] = jnp.where(second, g0, g1)


def put_pair(high_ref, low_ref, index, row):
    width = row.shape[1]
    at = (index // 2, slice(None), slice(index % 2 * width, index % 2 * width + width))
    high_ref[at], low_ref[at] = split(row)


def adjoint_into(acc, g_high, g_low, first, w_high, w_low, band):
    pairs, channels, double = g_high.shape
    for d in range(RADIUS + 1):
        begin, end = max(first, d), min(first + pairs, acc.shape[0] + d)
        if begin >= end:
            continue
        high = g_high[begin - first : end - first].reshape((end - begin) * channels, double)
        low = g_low[begin - first : end - first].reshape((end - begin) * channels, double)
        part = mm(high, w_high[band, d]) + mm(low, w_high[band, d]) + mm(high, w_low[band, d])
        acc[begin - d : end - d] += part.reshape(end - begin, channels, double)


def own_maps_kernel(rows_ref, wa_high, wa_low, acc, near_ref, g_high, g_low):
    height, channels, width = rows_ref.shape
    lane = lanes((channels, width))
    near = [jnp.zeros((channels, width), F32) for _ in range(2)]
    for i in range(height):
        row = rows_ref[i]
        put_pair(g_high, g_low, i, row)
        q = i + EDGE
        moved = pltpu.roll(row, (RADIUS + q * EDGE) % width, 1)
        near[q // height] = jnp.where(lane // EDGE == q % height, moved, near[q // height])
    near_ref[...] = jnp.concatenate(near, axis=1)
    acc[...] = jnp.zeros_like(acc)
    adjoint_into(acc, g_high, g_low, EDGE // 2, wa_high, wa_low, 1)


def maps_kernel(
    ext_ref, side_ref, acc_in, near_ref, p1, p2, left, right, above, below, place,
    wa_high, wa_low, sa_high, sa_low, *rest, last,
):
    if last:
        out_ref, g_high, g_low, acc = rest
        height = out_ref.shape[1]
    else:
        (wf_high, wf_low, sf_high, sf_low, ext_out, side_out, b_ref, g_high, g_low, acc, a2_high, a2_low, acc_b) = rest
        height = b_ref.shape[0]
    channels, width = left.shape
    ext_rows = height + EDGE
    odd = place[ROW_ODD] == 1
    lane = lanes((channels, width))
    near = [near_ref[:, :width], near_ref[:, width:]]
    for k in range(2 * EDGE):
        q = k if k < EDGE else k + height
        row = jnp.where(odd, p1[k], p2[k]) if k < EDGE else jnp.where(odd, p2[k - EDGE], p1[k - EDGE])
        put_pair(g_high, g_low, k, row)
        moved = pltpu.roll(row, (RADIUS + q * EDGE) % width, 1)
        near[q // height] = jnp.where(lane // EDGE == q % height, moved, near[q // height])
    side_in = jnp.concatenate([left[...], right[...], above[...], below[...]] + near, axis=1)
    side_high, side_low = split(side_in)
    side_mm = mm(side_high, sa_high[...]) + mm(side_low, sa_high[...]) + mm(side_high, sa_low[...])
    half = side_mm.shape[1] // 2
    rim = side_mm[:, half:]
    acc[...] = acc_in[...]
    n = EDGE // 2
    adjoint_into(acc, g_high.at[:n], g_low.at[:n], 0, wa_high, wa_low, 0)
    adjoint_into(acc, g_high.at[n:], g_low.at[n:], n + height // 2, wa_high, wa_low, 2)
    for a in range(ext_rows):
        if last and not RADIUS <= a < RADIUS + height:
            continue
        grad = add_rim(acc[a // 2, :, a % 2 * width : a % 2 * width + width], rim, a)
        row = jnp.maximum(ext_ref[a] - 0.5 * grad, 0.0)
        if last:
            out_ref[:, a - RADIUS, :] = row
            continue
        if a < RADIUS:
            row = jnp.where(place[UP] == 1, row, 0.0)
        elif a >= RADIUS + height:
            row = jnp.where(place[DOWN] == 1, row, 0.0)
        ext_out[a] = row
        put_pair(a2_high, a2_low, a, row)
    if last:
        return
    side = jnp.maximum(side_ref[...] - 0.5 * side_mm[:, :half], 0.0)
    where = lanes(side.shape)
    a, c = where // EDGE, where % EDGE
    outside = (
        ((a < RADIUS) & (place[UP] == 0))
        | ((a >= RADIUS + height) & (place[DOWN] == 0))
        | ((c < RADIUS) & (place[LEFT] == 0))
        | ((c >= RADIUS) & (place[RIGHT] == 0))
        | (a >= ext_rows)
    )
    side = jnp.where(outside, 0.0, side)
    side_out[...] = side
    blur_into(b_ref, a2_high, a2_low, side, wf_high, wf_low, sf_high, sf_low, acc_b)


def call(kernel, micros, outs, scratch, specs, *args):
    return pl.pallas_call(
        kernel,
        out_shape=[jax.ShapeDtypeStruct(s, d) for s, d in outs],
        in_specs=specs,
        out_specs=[VMEM] * len(outs),
        scratch_shapes=[pltpu.VMEM(*s) if isinstance(s, tuple) else s for s in scratch],
        compiler_params=PARAMS,
        cost_estimate=pl.CostEstimate(
            flops=int(micros * 1.15e9), bytes_accessed=int(micros * 3.7e6), transcendentals=0
        ),
    )(*args)


def core_swap(x):
    count = lax.axis_size("cols")
    return lax.ppermute(x, "cols", [(i, i ^ 1) for i in range(count)])


def cross_swap(x):
    count = lax.axis_size("cols")
    return lax.ppermute(x, "cols", [(i, (i + 1 if i % 2 else i - 1) % count) for i in range(count)])


def pair_one(x):
    count = lax.axis_size("rows")
    return lax.ppermute(x, "rows", [(i, i ^ 1) for i in range(count)])


def pair_two(x):
    count = lax.axis_size("rows")
    pairs = [(i, i + 1) for i in range(1, count - 1, 2)]
    return lax.ppermute(x, "rows", pairs + [(b, a) for a, b in pairs])


def chips_sum(x):
    count = lax.axis_size("cols")
    step = 4
    while step < count:
        route = [(i, (((i + 1) % count) ^ step) - 1) for i in range(count)]
        x = x + lax.ppermute(x, "cols", [(i, j % count) for i, j in route])
        step *= 2
    return x


def rows_sum(x):
    count = lax.axis_size("rows")
    step = 2
    while step < count:
        x = x + lax.ppermute(x, "rows", [(i, i ^ step) for i in range(count)])
        step *= 2
    return x


def on_device(observed, nonlin, abundance, spectra, kernels, tile_family):
    bands, height, width = observed.shape
    channels = abundance.shape[0]
    n_rows, n_cols = lax.axis_size("rows"), lax.axis_size("cols")
    row_at, col_at = lax.axis_index("rows"), lax.axis_index("cols")
    pixel_count = height * width * n_rows * n_cols
    quarter = -(-bands // 32) * 8
    full = 4 * quarter
    half_of = ((col_at + 1) // 2) % 2
    col_odd, row_odd = col_at % 2 == 1, row_at % 2 == 1
    place = jnp.stack(
        [row_at % 2, col_at % 2, row_at > 0, row_at < n_rows - 1, col_at > 0, col_at < n_cols - 1, half_of]
    ).astype(jnp.int32)
    has_left = (col_at > 0).astype(F32)
    has_right = (col_at < n_cols - 1).astype(F32)
    tile = (channels, width)

    def sides(core, cross):
        left = jnp.where(col_odd, core, cross) * has_left
        right = jnp.where(col_odd, cross, core) * has_right
        lane = lanes(tile) < width // 2
        up_msg = jnp.where(lane, left, right)
        down_msg = jnp.where(lane, right, left)
        return left, right, jnp.where(row_odd, up_msg, down_msg), jnp.where(row_odd, down_msg, up_msg)

    a_rows, e_core, e_cross, mark = call(
        first_kernel,
        1,
        [((height,) + tile, F32), ((channels + 8, width), F32), ((channels + 8, width), F32), ((8, width), F32)],
        [],
        [SMEM, VMEM, SMEM],
        tile_family, abundance, place,
    )
    got_core = core_swap(e_core)
    got_cross = cross_swap(e_cross)
    left, right, side1, side2 = sides(got_core[:channels], got_cross[:channels])
    mark_left = jnp.where(col_odd, got_core[channels:], got_cross[channels:])
    mark_right = jnp.where(col_odd, got_cross[channels:], got_core[channels:])
    marks = jnp.concatenate([mark_left, mark, mark_right])
    top = a_rows[:RADIUS].reshape(RADIUS * channels, width)
    bottom = a_rows[height - RADIUS :].reshape(RADIUS * channels, width)
    got1 = pair_one(jnp.concatenate([jnp.where(row_odd, top, bottom), side1, marks]))
    got2 = pair_two(jnp.concatenate([jnp.where(row_odd, bottom, top), side2, marks]))
    body = RADIUS * channels

    def above_below(x1, x2):
        return jnp.where(row_odd, x1, x2), jnp.where(row_odd, x2, x1)

    above, below = above_below(got1[body : body + channels], got2[body : body + channels])
    table = kernels.reshape(kernels.shape[0], KS * KS)
    pairs = height // 2
    ext_rows = height + EDGE
    main_w = ((RADIUS + 1, 2 * width, 2 * width), BF16)
    side_f = ((2 * width, height * EDGE), BF16)
    any_space = pl.BlockSpec(memory_space=pl.ANY)
    seen, *wf = call(
        forward_weights_kernel,
        3,
        [((height, full, width), F32), main_w, main_w, side_f, side_f],
        [pltpu.SemaphoreType.DMA((height,))],
        [SMEM, SMEM, any_space],
        tile_family, table, observed,
    )
    got1, got2, seen, *wf = lax.optimization_barrier((got1, got2, seen, *wf))
    ext, side, blurred = call(
        start_kernel,
        2,
        [((ext_rows,) + tile, F32), ((channels, 2 * width), F32), ((height,) + tile, F32)],
        [((ext_rows // 2, channels, 2 * width), BF16)] * 2 + [((pairs, channels, 2 * width), F32)],
        [VMEM] * 7 + [SMEM] + [VMEM] * 4,
        a_rows, got1, got2, left, right, above, below, place, *wf,
    )
    marks_up, marks_down = above_below(got1[body + channels :], got2[body + channels :])
    families = jnp.concatenate([marks_up, marks, marks_down])[::8, 0].astype(jnp.int32)
    main_a = ((3, RADIUS + 1, 2 * width, 2 * width), BF16)
    side_a = ((6 * width, 4 * width), BF16)

    def adjoint_weights():
        return call(
            functools.partial(adjoint_weights_kernel, height=height, width=width),
            3,
            [main_a, main_a, side_a, side_a],
            [((6 * width, 4 * width), F32)],
            [SMEM, SMEM],
            families, table,
        )

    padded = jnp.pad(spectra, ((0, full - bands), (0, 0))).reshape(2, 2, quarter, channels)
    halves = jnp.transpose(padded, (0, 2, 1, 3)).reshape(2, quarter, 2 * channels)
    mine = lax.dynamic_index_in_dim(halves, half_of, 0, False)
    other = lax.dynamic_index_in_dim(halves, 1 - half_of, 0, False)
    rate = 40.0 / pixel_count
    for step in range(ITERS):
        last = step == ITERS - 1
        g_mine, to_core, main1, main2, e_cross, g_rows = call(
            functools.partial(spectral_kernel, scale=1.0 / channels),
            5,
            [
                ((quarter, 2 * channels), F32),
                ((quarter + channels, width), F32),
                ((height // 2,) + tile, F32),
                ((height // 2,) + tile, F32),
                (tile, F32),
                ((height,) + tile, F32),
            ],
            [((full, channels), F32)],
            [VMEM] * 5 + [SMEM],
            seen, nonlin, blurred, mine, other, place,
        )
        got_core = core_swap(to_core)
        p1 = pair_one(main1)
        p2 = pair_two(main2)
        share = g_mine + got_core[:quarter]
        got_cross = cross_swap(jnp.concatenate([share, e_cross]))
        if step == 0:
            wa = adjoint_weights()
            got_cross, *wa = lax.optimization_barrier((got_cross, *wa))
        share = share + got_cross[:quarter]
        left, right, side1, side2 = sides(got_core[quarter:], got_cross[quarter:])
        own, near = call(
            own_maps_kernel,
            2,
            [((ext_rows // 2, channels, 2 * width), F32), ((channels, 2 * width), F32)],
            [((pairs, channels, 2 * width), BF16)] * 2,
            [VMEM] * 3,
            g_rows, wa[0], wa[1],
        )
        share = chips_sum(share)
        share, own, near, p1, p2 = lax.optimization_barrier((share, own, near, p1, p2))
        got1 = pair_one(jnp.concatenate([share, side1]))
        got2 = pair_two(side2)
        share = share + got1[:quarter]
        above, below = above_below(got1[quarter:], got2)
        gathered = (ext, side, own, near, p1, p2, left, right, above, below, place) + tuple(wa)
        g2 = [((EDGE, channels, 2 * width), BF16)] * 2
        acc = [((ext_rows // 2, channels, 2 * width), F32)]
        if last:
            made = call(
                functools.partial(maps_kernel, last=True),
                3,
                [((channels, height, width), F32)],
                g2 + acc,
                [VMEM] * 10 + [SMEM] + [VMEM] * 4,
                *gathered,
            )
        else:
            made = call(
                functools.partial(maps_kernel, last=False),
                4,
                [((ext_rows,) + tile, F32), ((channels, 2 * width), F32), ((height,) + tile, F32)],
                g2 + acc + [((ext_rows // 2, channels, 2 * width), BF16)] * 2 + [((pairs, channels, 2 * width), F32)],
                [VMEM] * 10 + [SMEM] + [VMEM] * 8,
                *gathered, *wf,
            )
        share, *made = lax.optimization_barrier((rows_sum(share), *made))
        mine = jnp.maximum(mine - rate * share, 0.0)
        other = core_swap(mine)
        if last:
            (out,) = made
        else:
            ext, side, blurred = made
    first = jnp.where(half_of == 0, mine, other)
    second = jnp.where(half_of == 0, other, mine)
    parts = [first[:, :channels], first[:, channels:], second[:, :channels], second[:, channels:]]
    return out, jnp.concatenate(parts)[:bands]


def solution(mesh):
    placed = (
        P(None, "rows", "cols"),
        P("rows", "cols"),
        P(None, "rows", "cols"),
        P(),
        P(),
        P("rows", "cols"),
    )
    return jax.shard_map(
        on_device,
        mesh=mesh,
        in_specs=placed,
        out_specs=(P(None, "rows", "cols"), P()),
        check_vma=False,
    )
```

```python
import functools

import jax
import jax.numpy as jnp
import numpy as np
from jax import lax
from jax.experimental import pallas as pl
from jax.experimental.pallas import tpu as pltpu
from jax.sharding import PartitionSpec as P

KS = 9
RADIUS = KS // 2
EDGE = 2 * RADIUS
ITERS = 3
F32 = jnp.float32
BF16 = jnp.bfloat16
VMEM = pl.BlockSpec(memory_space=pltpu.VMEM)
SMEM = pl.BlockSpec(memory_space=pltpu.SMEM)
PARAMS = pltpu.CompilerParams(vmem_limit_bytes=18 * 1024 * 1024)
ROW_ODD, COL_ODD, UP, DOWN, LEFT, RIGHT, HALF = range(7)


def split(x):
    high = x.astype(BF16)
    return high, (x - high.astype(F32)).astype(BF16)


def mm(a, b):
    return jnp.dot(a, b, preferred_element_type=F32)


def mm_nt(a, b):
    return lax.dot_general(a, b, (((1,), (1,)), ((), ())), preferred_element_type=F32)


def lanes(shape):
    return lax.broadcasted_iota(jnp.int32, shape, len(shape) - 1)


def edges(rows, swapped):
    count = len(rows)
    lane = lanes(rows[0].shape)
    width = rows[0].shape[1]
    out = jnp.zeros_like(rows[0])
    for i, row in enumerate(rows):
        place = (i + count // 2) % count if swapped else i
        first = 0 if swapped else width - EDGE
        moved = pltpu.roll(row, (place * EDGE - first) % width, 1)
        out = jnp.where(lane // EDGE == place, moved, out)
    return out


def wide(x, total, shift):
    padded = jnp.concatenate([x, jnp.zeros((x.shape[0], total - x.shape[1]), x.dtype)], axis=1)
    return pltpu.roll(padded, shift % total, 1)


def assemble_side(left, right, above, below, height):
    total = 2 * left.shape[1]
    lane = lanes((left.shape[0], total))
    row, col = lane // EDGE, lane % EDGE
    on_left = col < RADIUS
    own = (row >= RADIUS) & (row < RADIUS + height)
    top = row < RADIUS
    bottom = (row >= RADIUS + height) & (row < 2 * RADIUS + height)
    half = EDGE * height // 2
    lo = RADIUS * EDGE - RADIUS
    hi = RADIUS * EDGE + RADIUS
    base = (RADIUS + height) * EDGE
    out = jnp.zeros((left.shape[0], total), F32)
    out = jnp.where(own & on_left, wide(left, total, lo), out)
    first = (row - RADIUS) < height // 2
    out = jnp.where(own & ~on_left & first, wide(right, total, hi - half), out)
    out = jnp.where(own & ~on_left & ~first, wide(right, total, hi + half), out)
    out = jnp.where(top & ~on_left, wide(above, total, RADIUS - RADIUS * EDGE), out)
    out = jnp.where(top & on_left, wide(above, total, -half - RADIUS * EDGE - RADIUS), out)
    out = jnp.where(bottom & on_left, wide(below, total, base - RADIUS), out)
    out = jnp.where(bottom & ~on_left, wide(below, total, base + RADIUS - half), out)
    return out


def add_rim(row, contrib, index):
    width = row.shape[1]
    start = index * EDGE
    part = contrib[:, start // width * width : start // width * width + width]
    moved = pltpu.roll(part, (-(start % width) - RADIUS) % width, 1)
    lane = lanes(row.shape)
    near = (lane < RADIUS) | (lane >= width - RADIUS)
    return row + jnp.where(near, moved, 0.0)


def first_kernel(family, a_ref, place, rows_ref, e_core, e_cross, mark_ref):
    channels, height, width = a_ref.shape
    rows = []
    for i in range(height):
        row = a_ref[:, i, :]
        rows_ref[i] = row
        rows.append(row)
    low, high = edges(rows, True), edges(rows, False)
    odd = place[COL_ODD] == 1
    e_core[:channels] = jnp.where(odd, low, high)
    e_cross[:channels] = jnp.where(odd, high, low)
    mark = jnp.full((8, width), family[0, 0].astype(F32), F32)
    e_core[channels:] = mark
    e_cross[channels:] = mark
    mark_ref[...] = mark


def band_sum(taps, delta):
    total = jnp.zeros(delta.shape, F32)
    for v in range(KS):
        total = jnp.where(delta == v, taps[v], total)
    return total


def build_main(taps, w_high, w_low, index, width):
    shape = (width, width)
    delta = lax.broadcasted_iota(jnp.int32, shape, 0) - lax.broadcasted_iota(jnp.int32, shape, 1) + RADIUS
    blank = jnp.zeros(shape, BF16)
    for u in range(-1, KS + 1):
        if 0 <= u < KS:
            high, low = split(band_sum([taps(u, v) for v in range(KS)], delta))
        else:
            high, low = blank, blank
        for r in range(2):
            for ro in range(2):
                if (u + ro - r) % 2 == 0:
                    d = (u + ro - r) // 2
                    if 0 <= d <= RADIUS:
                        at = index + (d, slice(r * width, r * width + width), slice(ro * width, ro * width + width))
                        w_high[at] = high
                        w_low[at] = low


def rim_column(lane, width):
    c = lane % EDGE
    return jnp.where(c < RADIUS, width - RADIUS + c, c - RADIUS)


def side_column(lane, width):
    c = lane % EDGE
    return jnp.where(c < RADIUS, c - RADIUS, width + c - RADIUS)


def forward_weights_kernel(family, table, place, obs_ref, spectra_ref, seen_ref, mine, other, w_high, w_low, s_high, s_low, sems):
    depth, height, width = obs_ref.shape
    copies = []
    for i in range(height):
        copies.append(pltpu.make_async_copy(obs_ref.at[:, i, :], seen_ref.at[i, pl.ds(0, depth), :], sems.at[i]))
        copies[-1].start()
    start = depth // 8 * 8
    channels = spectra_ref.shape[0]
    quarter = seen_ref.shape[1] // 4
    total = -(-seen_ref.shape[1] // 128) * 128
    spectra = jnp.concatenate([spectra_ref[...], jnp.zeros((channels, total - depth), F32)], axis=1).T
    halves = [
        jnp.concatenate([spectra[q * quarter : (q + 1) * quarter], spectra[(q + 1) * quarter : (q + 2) * quarter]], axis=1)
        for q in (0, 2)
    ]
    second = place[HALF] == 1
    mine[...] = jnp.where(second, halves[1], halves[0])
    other[...] = jnp.where(second, halves[0], halves[1])
    own = lambda u, v: table[u, family[0, 0], v]
    build_main(own, w_high, w_low, (), width)
    n = height * EDGE
    shape = (EDGE, n)
    lane = lanes(shape)
    c = lax.broadcasted_iota(jnp.int32, shape, 0)
    delta = side_column(c, width) - rim_column(lane, width) + RADIUS
    out_row = lane // EDGE
    bands = [band_sum([own(u, v) for v in range(KS)], delta) for u in range(KS)]
    rows = s_high.shape[0] // EDGE
    for a in range(0, rows, 2):
        blocks = []
        for b in (a, a + 1):
            total = jnp.zeros(shape, F32)
            for u in range(KS):
                total = jnp.where(out_row == b - u, bands[u], total)
            blocks.append(total)
        high, low = split(jnp.concatenate(blocks, axis=0))
        s_high[a * EDGE : a * EDGE + 2 * EDGE] = high
        s_low[a * EDGE : a * EDGE + 2 * EDGE] = low
    for i in range(height):
        copies[i].wait()
    sub = lax.broadcasted_iota(jnp.int32, (seen_ref.shape[1] - start, width), 0)
    for i in range(height):
        seen_ref[i, start:] = jnp.where(sub < depth - start, seen_ref[i, start:], 0.0)


def adjoint_weights_kernel(marks_up, marks, marks_down, table, w_high, w_low, s_high, s_low, scratch, *, height, width):
    families = []
    for ref in (marks_up, marks, marks_down):
        for k in range(3):
            families.append(jnp.max(ref[8 * k : 8 * k + 8]).astype(jnp.int32))
    for b in range(3):
        build_main(lambda u, v, b=b: table[KS - 1 - u, families[3 * b + 1], KS - 1 - v], w_high, w_low, (b,), width)
    n = s_high.shape[1]
    half = n // 2
    shape = (EDGE, n)
    lane = lanes(shape)
    c = lax.broadcasted_iota(jnp.int32, shape, 0)
    to_side = lane < half
    column = jnp.where(to_side, side_column(lane, width), rim_column(lane, width))
    out_row = jnp.where(to_side, lane, lane - half) // EDGE
    out_row = jnp.where(out_row < height + EDGE, out_row, -KS - 1)
    sources = (c - EDGE, width + c, rim_column(c, width))
    chunk = height * EDGE
    mid = chunk // 2

    def place_of(kind, q):
        i = q - EDGE
        if kind == 2:
            return 4 * chunk + q * EDGE
        if 0 <= i < height:
            return i * EDGE if kind == 0 else chunk + (i + height // 2) % height * EDGE
        if i < 0:
            return 2 * chunk + (mid if kind == 0 else 0) + q * EDGE
        return 3 * chunk + (0 if kind == 0 else mid) + (i - height) * EDGE

    for kind in range(3):
        delta = sources[kind] - column + RADIUS
        if kind == 2:
            delta = jnp.where(to_side, delta, -1)
        for b in range(3):
            tile = 3 * b + (0, 2, 1)[kind]
            bands = [
                band_sum([table[KS - 1 - u, families[tile], KS - 1 - v] for v in range(KS)], delta) for u in range(KS)
            ]
            q_range = (range(0, EDGE), range(EDGE, EDGE + height), range(EDGE + height, 2 * EDGE + height))[b]
            for q in q_range:
                total = jnp.zeros(shape, F32)
                for u in range(KS):
                    if 0 <= q - u < height + EDGE:
                        total = jnp.where(out_row == q - u, bands[u], total)
                at = place_of(kind, q)
                scratch[at : at + EDGE] = total
    for start in range(0, scratch.shape[0], 64):
        high, low = split(scratch[start : start + 64])
        s_high[start : start + 64] = high
        s_low[start : start + 64] = low


def blur_into(b_ref, a2_high, a2_low, side, w_high, w_low, s_high, s_low, acc):
    pairs, channels, double = acc.shape
    width = double // 2
    for d in range(RADIUS + 1):
        high = a2_high[d : d + pairs].reshape(pairs * channels, double)
        low = a2_low[d : d + pairs].reshape(pairs * channels, double)
        part = mm(high, w_high[d]) + mm(low, w_high[d]) + mm(high, w_low[d])
        part = part.reshape(pairs, channels, double)
        if d == 0:
            acc[...] = part
        else:
            acc[...] += part
    side_high, side_low = split(side)
    rim = mm(side_high, s_high[...]) + mm(side_low, s_high[...]) + mm(side_high, s_low[...])
    for i in range(2 * pairs):
        row = acc[i // 2, :, i % 2 * width : i % 2 * width + width]
        b_ref[i] = add_rim(row, rim, i)


def start_kernel(
    rows_ref, p1, p2, left, right, above, below, place, w_high, w_low, s_high, s_low,
    ext_ref, side_ref, b_ref, a2_high, a2_low, acc,
):
    height, channels, width = rows_ref.shape
    odd = place[ROW_ODD] == 1
    for a in range(height + EDGE):
        if a < RADIUS:
            row = jnp.where(odd, p1[a * channels : a * channels + channels], p2[a * channels : a * channels + channels])
            row = jnp.where(place[UP] == 1, row, 0.0)
        elif a < RADIUS + height:
            row = rows_ref[a - RADIUS]
        else:
            k = (a - RADIUS - height) * channels
            row = jnp.where(odd, p2[k : k + channels], p1[k : k + channels])
            row = jnp.where(place[DOWN] == 1, row, 0.0)
        ext_ref[a] = row
        high, low = split(row)
        a2_high[a // 2, :, a % 2 * width : a % 2 * width + width] = high
        a2_low[a // 2, :, a % 2 * width : a % 2 * width + width] = low
    side = assemble_side(left[...], right[...], above[...], below[...], height)
    side_ref[...] = side
    blur_into(b_ref, a2_high, a2_low, side, w_high, w_low, s_high, s_low, acc)


def spectral_kernel(
    obs_ref, bend_ref, b_ref, mine, other, place,
    g_mine, core_ref, main1, main2, cross_ref, rows_ref,
    total, *, scale,
):
    height, channels, width = b_ref.shape
    bands = obs_ref.shape[1]
    quarter = bands // 4
    second = place[HALF] == 1
    m0 = jnp.where(second, other[...], mine[...])
    m1 = jnp.where(second, mine[...], other[...])
    spectra = jnp.concatenate([m0[:, :channels], m0[:, channels:], m1[:, :channels], m1[:, channels:]], axis=0)
    m_high, m_low = split(spectra)
    m_cat = jnp.concatenate([m_high, m_low, m_high], axis=1)
    t_high, t_low = split(spectra.T)
    t_cat = jnp.concatenate([t_high, t_low], axis=0)
    rows = []
    for pair in range(height // 2):
        b_pair = jnp.concatenate([b_ref[2 * pair], b_ref[2 * pair + 1]], axis=1)
        b_high, b_low = split(b_pair)
        b_cat = jnp.concatenate([b_high, b_high, b_low], axis=0)
        linear = mm(m_cat, b_cat) * scale
        seen = jnp.concatenate([obs_ref[2 * pair], obs_ref[2 * pair + 1]], axis=1)
        bend = jnp.concatenate([bend_ref[2 * pair : 2 * pair + 1], bend_ref[2 * pair + 1 : 2 * pair + 2]], axis=1)
        bent = bend * linear
        resid = linear + bent * linear - seen
        weighted = resid * (1.0 + 2.0 * bent)
        w_high, w_low = split(weighted)
        part = mm_nt(w_high, jnp.concatenate([b_high, b_low], axis=0))
        part = part[:, :channels] + part[:, channels:] + mm_nt(w_low, b_high)
        if pair == 0:
            total[...] = part
        else:
            total[...] += part
        both = mm(t_cat, w_high)
        grad = (both[:channels] + both[channels:] + mm(t_high, w_low)) * scale
        for k in range(2):
            row = grad[:, k * width : k * width + width]
            rows_ref[2 * pair + k] = row
            rows.append(row)
    low, high = edges(rows, True), edges(rows, False)
    col_odd = place[COL_ODD] == 1
    core_ref[2 * quarter // 2 :] = jnp.where(col_odd, low, high)
    cross_ref[...] = jnp.where(col_odd, high, low)
    row_odd = place[ROW_ODD] == 1
    half = height // 2
    for i in range(half):
        main1[i] = jnp.where(row_odd, rows[i], rows[half + i])
        main2[i] = jnp.where(row_odd, rows[half + i], rows[i])
    g = total[...] * scale
    g0 = jnp.concatenate([g[:quarter], g[quarter : 2 * quarter]], axis=1)
    g1 = jnp.concatenate([g[2 * quarter : 3 * quarter], g[3 * quarter :]], axis=1)
    g_mine[...] = jnp.where(second, g1, g0)
    core_ref[:quarter] = jnp.where(second, g0, g1)


def put_pair(high_ref, low_ref, index, row):
    width = row.shape[1]
    at = (index // 2, slice(None), slice(index % 2 * width, index % 2 * width + width))
    high_ref[at], low_ref[at] = split(row)


def adjoint_into(acc, g_high, g_low, first, w_high, w_low, band):
    pairs, channels, double = g_high.shape
    for d in range(RADIUS + 1):
        begin, end = max(first, d), min(first + pairs, acc.shape[0] + d)
        if begin >= end:
            continue
        high = g_high[begin - first : end - first].reshape((end - begin) * channels, double)
        low = g_low[begin - first : end - first].reshape((end - begin) * channels, double)
        part = mm(high, w_high[band, d]) + mm(low, w_high[band, d]) + mm(high, w_low[band, d])
        acc[begin - d : end - d] += part.reshape(end - begin, channels, double)


def own_maps_kernel(rows_ref, wa_high, wa_low, acc, near_ref, g_high, g_low):
    height, channels, width = rows_ref.shape
    lane = lanes((channels, width))
    near = [jnp.zeros((channels, width), F32) for _ in range(2)]
    for i in range(height):
        row = rows_ref[i]
        put_pair(g_high, g_low, i, row)
        q = i + EDGE
        moved = pltpu.roll(row, (RADIUS + q * EDGE) % width, 1)
        near[q // height] = jnp.where(lane // EDGE == q % height, moved, near[q // height])
    near_ref[...] = jnp.concatenate(near, axis=1)
    acc[...] = jnp.zeros_like(acc)
    adjoint_into(acc, g_high, g_low, EDGE // 2, wa_high, wa_low, 1)


def halo_maps_kernel(acc_in, near_in, p1, p2, place, wa_high, wa_low, acc, near_ref, g_high, g_low):
    channels = near_in.shape[0]
    width = near_in.shape[1] // 2
    height = 2 * acc.shape[0] - EDGE
    odd = place[ROW_ODD] == 1
    lane = lanes((channels, width))
    near = [near_in[:, :width], near_in[:, width:]]
    for k in range(2 * EDGE):
        q = k if k < EDGE else k + height
        if k < EDGE:
            row = jnp.where(place[UP] == 1, jnp.where(odd, p1[k], p2[k]), 0.0)
        else:
            row = jnp.where(place[DOWN] == 1, jnp.where(odd, p2[k - EDGE], p1[k - EDGE]), 0.0)
        put_pair(g_high, g_low, k, row)
        moved = pltpu.roll(row, (RADIUS + q * EDGE) % width, 1)
        near[q // height] = jnp.where(lane // EDGE == q % height, moved, near[q // height])
    near_ref[...] = jnp.concatenate(near, axis=1)
    n = EDGE // 2
    adjoint_into(acc, g_high.at[:n], g_low.at[:n], 0, wa_high, wa_low, 0)
    adjoint_into(acc, g_high.at[n:], g_low.at[n:], n + height // 2, wa_high, wa_low, 2)


def maps_kernel(
    ext_ref, side_ref, acc, near_ref, left, right, above, below, place, sa_high, sa_low, *rest, last,
):
    if last:
        (out_ref,) = rest
        height = out_ref.shape[1]
    else:
        (wf_high, wf_low, sf_high, sf_low, ext_out, side_out, b_ref, a2_high, a2_low, acc_b) = rest
        height = b_ref.shape[0]
    width = left.shape[1]
    ext_rows = height + EDGE
    side_in = jnp.concatenate([left[...], right[...], above[...], below[...], near_ref[...]], axis=1)
    side_high, side_low = split(side_in)
    side_mm = mm(side_high, sa_high[...]) + mm(side_low, sa_high[...]) + mm(side_high, sa_low[...])
    half = side_mm.shape[1] // 2
    rim = side_mm[:, half:]
    for a in range(ext_rows):
        if last and not RADIUS <= a < RADIUS + height:
            continue
        grad = add_rim(acc[a // 2, :, a % 2 * width : a % 2 * width + width], rim, a)
        row = jnp.maximum(ext_ref[a] - 0.5 * grad, 0.0)
        if last:
            out_ref[:, a - RADIUS, :] = row
            continue
        if a < RADIUS:
            row = jnp.where(place[UP] == 1, row, 0.0)
        elif a >= RADIUS + height:
            row = jnp.where(place[DOWN] == 1, row, 0.0)
        ext_out[a] = row
        put_pair(a2_high, a2_low, a, row)
    if last:
        return
    side = jnp.maximum(side_ref[...] - 0.5 * side_mm[:, :half], 0.0)
    where = lanes(side.shape)
    a, c = where // EDGE, where % EDGE
    outside = (
        ((a < RADIUS) & (place[UP] == 0))
        | ((a >= RADIUS + height) & (place[DOWN] == 0))
        | ((c < RADIUS) & (place[LEFT] == 0))
        | ((c >= RADIUS) & (place[RIGHT] == 0))
        | (a >= ext_rows)
    )
    side = jnp.where(outside, 0.0, side)
    side_out[...] = side
    blur_into(b_ref, a2_high, a2_low, side, wf_high, wf_low, sf_high, sf_low, acc_b)


def spectra_kernel(mine, other, place, out_ref):
    channels, depth = out_ref.shape
    second = place[HALF] == 1
    first = jnp.where(second, other[...], mine[...])
    last = jnp.where(second, mine[...], other[...])
    parts = [first[:, :channels], first[:, channels:], last[:, :channels], last[:, channels:]]
    out_ref[...] = jnp.concatenate(parts, axis=0).T[:, :depth]


def call(kernel, micros, outs, scratch, specs, *args, aliases=None):
    return pl.pallas_call(
        kernel,
        out_shape=[jax.ShapeDtypeStruct(s, d) for s, d in outs],
        in_specs=specs,
        out_specs=[VMEM] * len(outs),
        scratch_shapes=[pltpu.VMEM(*s) if isinstance(s, tuple) else s for s in scratch],
        input_output_aliases=aliases or {},
        compiler_params=PARAMS,
        cost_estimate=pl.CostEstimate(
            flops=int(micros * 1.15e9), bytes_accessed=int(micros * 3.7e6), transcendentals=0
        ),
    )(*args)


def core_swap(x):
    count = lax.axis_size("cols")
    return lax.ppermute(x, "cols", [(i, i ^ 1) for i in range(count)])


def cross_swap(x):
    count = lax.axis_size("cols")
    return lax.ppermute(x, "cols", [(i, (i + 1 if i % 2 else i - 1) % count) for i in range(count)])


def pair_one(x):
    count = lax.axis_size("rows")
    return lax.ppermute(x, "rows", [(i, i ^ 1) for i in range(count)])


def pair_two(x):
    count = lax.axis_size("rows")
    return lax.ppermute(x, "rows", [(i, min(max(i + 1 if i % 2 else i - 1, 0), count - 1)) for i in range(count)])


def col_swap(x, mask):
    count = lax.axis_size("cols")
    return lax.ppermute(x, "cols", [(i, (((i + 1) % count ^ mask) - 1) % count) for i in range(count)])


def row_swap(x, mask):
    count = lax.axis_size("rows")
    return lax.ppermute(x, "rows", [(i, i ^ mask) for i in range(count)])


def on_device(observed, nonlin, abundance, spectra, kernels, tile_family):
    bands, height, width = observed.shape
    channels = abundance.shape[0]
    n_rows, n_cols = lax.axis_size("rows"), lax.axis_size("cols")
    row_at, col_at = lax.axis_index("rows"), lax.axis_index("cols")
    pixel_count = height * width * n_rows * n_cols
    quarter = -(-bands // 32) * 8
    full = 4 * quarter
    half_of = ((col_at + 1) // 2) % 2
    col_odd, row_odd = col_at % 2 == 1, row_at % 2 == 1
    place = jnp.stack(
        [row_at % 2, col_at % 2, row_at > 0, row_at < n_rows - 1, col_at > 0, col_at < n_cols - 1, half_of]
    ).astype(jnp.int32)
    has_left = (col_at > 0).astype(F32)
    has_right = (col_at < n_cols - 1).astype(F32)
    has_up = (row_at > 0).astype(F32)
    has_down = (row_at < n_rows - 1).astype(F32)
    table = jnp.transpose(kernels, (1, 0, 2))
    place, abundance, row_odd, col_odd, has_left, has_right, has_up, has_down = lax.optimization_barrier(
        (place, abundance, row_odd, col_odd, has_left, has_right, has_up, has_down)
    )
    tile = (channels, width)

    def sides(core, cross):
        left = jnp.where(col_odd, core, cross) * has_left
        right = jnp.where(col_odd, cross, core) * has_right
        lane = lanes(tile) < width // 2
        up_msg = jnp.where(lane, left, right)
        down_msg = jnp.where(lane, right, left)
        return left, right, jnp.where(row_odd, up_msg, down_msg), jnp.where(row_odd, down_msg, up_msg)

    a_rows, e_core, e_cross, mark = call(
        first_kernel,
        1,
        [((height,) + tile, F32), ((channels + 8, width), F32), ((channels + 8, width), F32), ((8, width), F32)],
        [],
        [SMEM, VMEM, SMEM],
        tile_family, abundance, place,
    )
    got_core = core_swap(e_core)
    got_cross = cross_swap(e_cross)
    left, right, side1, side2 = sides(got_core[:channels], got_cross[:channels])
    mark_left = jnp.where(col_odd, got_core[channels:], got_cross[channels:])
    mark_right = jnp.where(col_odd, got_cross[channels:], got_core[channels:])
    marks = jnp.concatenate([mark_left, mark, mark_right])
    top = a_rows[:RADIUS].reshape(RADIUS * channels, width)
    bottom = a_rows[height - RADIUS :].reshape(RADIUS * channels, width)
    got1 = pair_one(jnp.concatenate([jnp.where(row_odd, top, bottom), side1, marks]))
    got2 = pair_two(jnp.concatenate([jnp.where(row_odd, bottom, top), side2, marks]))
    body = RADIUS * channels

    def above_below(x1, x2):
        return jnp.where(row_odd, x1, x2), jnp.where(row_odd, x2, x1)

    above, below = above_below(got1[body : body + channels], got2[body : body + channels])
    above, below = above * has_up, below * has_down
    pairs = height // 2
    ext_rows = height + EDGE
    main_w = ((RADIUS + 1, 2 * width, 2 * width), BF16)
    side_f = ((2 * width, height * EDGE), BF16)
    hbm = pl.BlockSpec(memory_space=pltpu.HBM)
    half_shape = ((quarter, 2 * channels), F32)
    seen, mine, other, *wf = call(
        forward_weights_kernel,
        3,
        [((height, full, width), F32), half_shape, half_shape, main_w, main_w, side_f, side_f],
        [pltpu.SemaphoreType.DMA((height,))],
        [SMEM, SMEM, SMEM, hbm, VMEM],
        tile_family, table, place, observed, spectra.T,
    )
    got1, got2, seen, mine, other, *wf = lax.optimization_barrier((got1, got2, seen, mine, other, *wf))
    ext, side, blurred = call(
        start_kernel,
        2,
        [((ext_rows,) + tile, F32), ((channels, 2 * width), F32), ((height,) + tile, F32)],
        [((ext_rows // 2, channels, 2 * width), BF16)] * 2 + [((pairs, channels, 2 * width), F32)],
        [VMEM] * 7 + [SMEM] + [VMEM] * 4,
        a_rows, got1, got2, left, right, above, below, place, *wf,
    )
    marks_up, marks_down = above_below(got1[body + channels :], got2[body + channels :])
    main_a = ((3, RADIUS + 1, 2 * width, 2 * width), BF16)
    side_a = ((6 * width, 4 * width), BF16)

    def adjoint_weights():
        return call(
            functools.partial(adjoint_weights_kernel, height=height, width=width),
            3,
            [main_a, main_a, side_a, side_a],
            [((6 * width, 4 * width), F32)],
            [VMEM, VMEM, VMEM, SMEM],
            marks_up, marks, marks_down, table,
        )

    rate = 40.0 / pixel_count
    acc_shape = ((ext_rows // 2, channels, 2 * width), F32)
    near_shape = ((channels, 2 * width), F32)

    def own_part(g_rows, wa):
        return call(
            own_maps_kernel,
            2,
            [acc_shape, near_shape],
            [((pairs, channels, 2 * width), BF16)] * 2,
            [VMEM] * 3,
            g_rows, wa[0], wa[1],
        )

    for step in range(ITERS):
        last = step == ITERS - 1
        g_mine, to_core, main1, main2, e_cross, g_rows = call(
            functools.partial(spectral_kernel, scale=1.0 / channels),
            5,
            [
                ((quarter, 2 * channels), F32),
                ((quarter + channels, width), F32),
                ((height // 2,) + tile, F32),
                ((height // 2,) + tile, F32),
                (tile, F32),
                ((height,) + tile, F32),
            ],
            [((full, channels), F32)],
            [VMEM] * 5 + [SMEM],
            seen, nonlin, blurred, mine, other, place,
        )
        got_core = core_swap(to_core)
        p1 = pair_one(main1)
        share = g_mine + got_core[:quarter]
        if step > 0:
            own, near = own_part(g_rows, wa)
            main2, own, near = lax.optimization_barrier((main2, own, near))
        p2 = pair_two(main2)
        got_cross = cross_swap(jnp.concatenate([share, e_cross]))
        if step == 0:
            wa = adjoint_weights()
            got_cross, *wa = lax.optimization_barrier((got_cross, *wa))
            own, near = own_part(g_rows, wa)
        share = share + got_cross[:quarter]
        left, right, side1, side2 = sides(got_core[quarter:], got_cross[quarter:])
        step_size = 4
        while step_size < n_cols:
            share = share + col_swap(share, step_size)
            step_size *= 2
        share, own, near = lax.optimization_barrier((share, own, near))
        own, near = call(
            halo_maps_kernel,
            1.5,
            [acc_shape, near_shape],
            [((EDGE, channels, 2 * width), BF16)] * 2,
            [VMEM] * 4 + [SMEM] + [VMEM] * 2,
            own, near, p1, p2, place, wa[0], wa[1],
            aliases={0: 0, 1: 1},
        )
        got1 = pair_one(jnp.concatenate([share, side1]))
        if n_rows == 4:
            got2 = row_swap(jnp.concatenate([share, side2]), 3)
            got3 = row_swap(share, 2)
            got1, got2, own, near = lax.optimization_barrier((got1, got2, own, near))
            share = (share + got1[:quarter]) + (got3 + got2[:quarter])
            got2 = got2[quarter:]
        else:
            got2 = pair_two(side2)
            got1, got2, own, near = lax.optimization_barrier((got1, got2, own, near))
            share = share + got1[:quarter]
            step_size = 2
            while step_size < n_rows:
                share = share + row_swap(share, step_size)
                step_size *= 2
        above, below = above_below(got1[quarter:], got2)
        above, below = above * has_up, below * has_down
        gathered = (ext, side, own, near, left, right, above, below, place) + tuple(wa[2:])
        if last:
            made = call(
                functools.partial(maps_kernel, last=True),
                1.5,
                [((channels, height, width), F32)],
                [],
                [VMEM] * 8 + [SMEM] + [VMEM] * 2,
                *gathered,
            )
        else:
            made = call(
                functools.partial(maps_kernel, last=False),
                2.5,
                [((ext_rows,) + tile, F32), ((channels, 2 * width), F32), ((height,) + tile, F32)],
                [((ext_rows // 2, channels, 2 * width), BF16)] * 2 + [((pairs, channels, 2 * width), F32)],
                [VMEM] * 8 + [SMEM] + [VMEM] * 6,
                *gathered, *wf,
            )
        share, *made = lax.optimization_barrier((share, *made))
        mine = jnp.maximum(mine - rate * share, 0.0)
        other = core_swap(mine)
        if last:
            (out,) = made
        else:
            ext, side, blurred = made
    (result,) = call(spectra_kernel, 1, [((channels, bands), F32)], [], [VMEM, VMEM, SMEM], mine, other, place)
    return out, result.T


def solution(mesh):
    placed = (
        P(None, "rows", "cols"),
        P("rows", "cols"),
        P(None, "rows", "cols"),
        P(),
        P(),
        P("rows", "cols"),
    )
    return jax.shard_map(
        on_device,
        mesh=mesh,
        in_specs=placed,
        out_specs=(P(None, "rows", "cols"), P()),
        check_vma=False,
    )
```

```python
import functools

import jax
import jax.numpy as jnp
import numpy as np
from jax import lax
from jax.experimental import pallas as pl
from jax.experimental.pallas import tpu as pltpu
from jax.sharding import PartitionSpec as P

KS = 9
RADIUS = KS // 2
EDGE = 2 * RADIUS
ITERS = 3
F32 = jnp.float32
BF16 = jnp.bfloat16
VMEM = pl.BlockSpec(memory_space=pltpu.VMEM)
SMEM = pl.BlockSpec(memory_space=pltpu.SMEM)
PARAMS = pltpu.CompilerParams(vmem_limit_bytes=18 * 1024 * 1024)
ROW_ODD, COL_ODD, UP, DOWN, LEFT, RIGHT, HALF = range(7)


def split(x):
    high = x.astype(BF16)
    return high, (x - high.astype(F32)).astype(BF16)


def mm(a, b):
    return jnp.dot(a, b, preferred_element_type=F32)


def mm_split(high, low, w_high, w_low):
    rows = high.shape[0]
    both = mm(jnp.concatenate([high, low], axis=0), w_high)
    return both[:rows] + both[rows:] + mm(high, w_low)


def mm_nt(a, b):
    return lax.dot_general(a, b, (((1,), (1,)), ((), ())), preferred_element_type=F32)


def lanes(shape):
    return lax.broadcasted_iota(jnp.int32, shape, len(shape) - 1)


def edges(rows, swapped):
    count = len(rows)
    lane = lanes(rows[0].shape)
    width = rows[0].shape[1]
    out = jnp.zeros_like(rows[0])
    for i, row in enumerate(rows):
        place = (i + count // 2) % count if swapped else i
        first = 0 if swapped else width - EDGE
        moved = pltpu.roll(row, (place * EDGE - first) % width, 1)
        out = jnp.where(lane // EDGE == place, moved, out)
    return out


def wide(x, total, shift):
    padded = jnp.concatenate([x, jnp.zeros((x.shape[0], total - x.shape[1]), x.dtype)], axis=1)
    return pltpu.roll(padded, shift % total, 1)


def assemble_side(left, right, above, below, height):
    total = 2 * left.shape[1]
    lane = lanes((left.shape[0], total))
    row, col = lane // EDGE, lane % EDGE
    on_left = col < RADIUS
    own = (row >= RADIUS) & (row < RADIUS + height)
    top = row < RADIUS
    bottom = (row >= RADIUS + height) & (row < 2 * RADIUS + height)
    half = EDGE * height // 2
    lo = RADIUS * EDGE - RADIUS
    hi = RADIUS * EDGE + RADIUS
    base = (RADIUS + height) * EDGE
    out = jnp.zeros((left.shape[0], total), F32)
    out = jnp.where(own & on_left, wide(left, total, lo), out)
    first = (row - RADIUS) < height // 2
    out = jnp.where(own & ~on_left & first, wide(right, total, hi - half), out)
    out = jnp.where(own & ~on_left & ~first, wide(right, total, hi + half), out)
    out = jnp.where(top & ~on_left, wide(above, total, RADIUS - RADIUS * EDGE), out)
    out = jnp.where(top & on_left, wide(above, total, -half - RADIUS * EDGE - RADIUS), out)
    out = jnp.where(bottom & on_left, wide(below, total, base - RADIUS), out)
    out = jnp.where(bottom & ~on_left, wide(below, total, base + RADIUS - half), out)
    return out


def add_rim(row, contrib, index):
    width = row.shape[1]
    start = index * EDGE
    part = contrib[:, start // width * width : start // width * width + width]
    moved = pltpu.roll(part, (-(start % width) - RADIUS) % width, 1)
    lane = lanes(row.shape)
    near = (lane < RADIUS) | (lane >= width - RADIUS)
    return row + jnp.where(near, moved, 0.0)


def first_kernel(family, a_ref, place, rows_ref, e_core, e_cross, mark_ref):
    channels, height, width = a_ref.shape
    rows = []
    for i in range(height):
        row = a_ref[:, i, :]
        rows_ref[i] = row
        rows.append(row)
    low, high = edges(rows, True), edges(rows, False)
    odd = place[COL_ODD] == 1
    e_core[:channels] = jnp.where(odd, low, high)
    e_cross[:channels] = jnp.where(odd, high, low)
    mark = jnp.full((8, width), family[0, 0].astype(F32), F32)
    e_core[channels:] = mark
    e_cross[channels:] = mark
    mark_ref[...] = mark


def band_sum(taps, delta):
    total = jnp.zeros(delta.shape, F32)
    for v in range(KS):
        total = jnp.where(delta == v, taps[v], total)
    return total


def build_main(taps, w_high, w_low, index, width):
    shape = (width, width)
    delta = lax.broadcasted_iota(jnp.int32, shape, 0) - lax.broadcasted_iota(jnp.int32, shape, 1) + RADIUS
    blank = jnp.zeros(shape, BF16)
    for u in range(-1, KS + 1):
        if 0 <= u < KS:
            high, low = split(band_sum([taps(u, v) for v in range(KS)], delta))
        else:
            high, low = blank, blank
        for r in range(2):
            for ro in range(2):
                if (u + ro - r) % 2 == 0:
                    d = (u + ro - r) // 2
                    if 0 <= d <= RADIUS:
                        at = index + (d, slice(r * width, r * width + width), slice(ro * width, ro * width + width))
                        w_high[at] = high
                        w_low[at] = low


def rim_column(lane, width):
    c = lane % EDGE
    return jnp.where(c < RADIUS, width - RADIUS + c, c - RADIUS)


def side_column(lane, width):
    c = lane % EDGE
    return jnp.where(c < RADIUS, c - RADIUS, width + c - RADIUS)


def forward_weights_kernel(family, table, place, obs_ref, spectra_ref, seen_ref, mine, other, w_high, w_low, s_high, s_low, sems):
    depth, height, width = obs_ref.shape
    copies = []
    for i in range(height):
        copies.append(pltpu.make_async_copy(obs_ref.at[:, i, :], seen_ref.at[i, pl.ds(0, depth), :], sems.at[i]))
        copies[-1].start()
    start = depth // 8 * 8
    channels = spectra_ref.shape[0]
    quarter = seen_ref.shape[1] // 4
    total = -(-seen_ref.shape[1] // 128) * 128
    spectra = jnp.concatenate([spectra_ref[...], jnp.zeros((channels, total - depth), F32)], axis=1).T
    halves = [
        jnp.concatenate([spectra[q * quarter : (q + 1) * quarter], spectra[(q + 1) * quarter : (q + 2) * quarter]], axis=1)
        for q in (0, 2)
    ]
    second = place[HALF] == 1
    mine[...] = jnp.where(second, halves[1], halves[0])
    other[...] = jnp.where(second, halves[0], halves[1])
    own = lambda u, v: table[u, family[0, 0], v]
    build_main(own, w_high, w_low, (), width)
    n = height * EDGE
    shape = (EDGE, n)
    lane = lanes(shape)
    c = lax.broadcasted_iota(jnp.int32, shape, 0)
    delta = side_column(c, width) - rim_column(lane, width) + RADIUS
    out_row = lane // EDGE
    bands = [band_sum([own(u, v) for v in range(KS)], delta) for u in range(KS)]
    rows = s_high.shape[0] // EDGE
    for a in range(0, rows, 2):
        blocks = []
        for b in (a, a + 1):
            total = jnp.zeros(shape, F32)
            for u in range(KS):
                total = jnp.where(out_row == b - u, bands[u], total)
            blocks.append(total)
        high, low = split(jnp.concatenate(blocks, axis=0))
        s_high[a * EDGE : a * EDGE + 2 * EDGE] = high
        s_low[a * EDGE : a * EDGE + 2 * EDGE] = low
    for i in range(height):
        copies[i].wait()
    sub = lax.broadcasted_iota(jnp.int32, (seen_ref.shape[1] - start, width), 0)
    for i in range(height):
        seen_ref[i, start:] = jnp.where(sub < depth - start, seen_ref[i, start:], 0.0)


def adjoint_weights_kernel(marks_up, marks, marks_down, table, w_high, w_low, s_high, s_low, scratch, *, height, width):
    families = []
    for ref in (marks_up, marks, marks_down):
        for k in range(3):
            families.append(jnp.max(ref[8 * k : 8 * k + 8]).astype(jnp.int32))
    for b in range(3):
        build_main(lambda u, v, b=b: table[KS - 1 - u, families[3 * b + 1], KS - 1 - v], w_high, w_low, (b,), width)
    n = s_high.shape[1]
    half = n // 2
    shape = (EDGE, n)
    lane = lanes(shape)
    c = lax.broadcasted_iota(jnp.int32, shape, 0)
    to_side = lane < half
    column = jnp.where(to_side, side_column(lane, width), rim_column(lane, width))
    out_row = jnp.where(to_side, lane, lane - half) // EDGE
    out_row = jnp.where(out_row < height + EDGE, out_row, -KS - 1)
    sources = (c - EDGE, width + c, rim_column(c, width))
    chunk = height * EDGE
    mid = chunk // 2

    def place_of(kind, q):
        i = q - EDGE
        if kind == 2:
            return 4 * chunk + q * EDGE
        if 0 <= i < height:
            return i * EDGE if kind == 0 else chunk + (i + height // 2) % height * EDGE
        if i < 0:
            return 2 * chunk + (mid if kind == 0 else 0) + q * EDGE
        return 3 * chunk + (0 if kind == 0 else mid) + (i - height) * EDGE

    for kind in range(3):
        delta = sources[kind] - column + RADIUS
        if kind == 2:
            delta = jnp.where(to_side, delta, -1)
        for b in range(3):
            tile = 3 * b + (0, 2, 1)[kind]
            bands = [
                band_sum([table[KS - 1 - u, families[tile], KS - 1 - v] for v in range(KS)], delta) for u in range(KS)
            ]
            q_range = (range(0, EDGE), range(EDGE, EDGE + height), range(EDGE + height, 2 * EDGE + height))[b]
            for q in q_range:
                total = jnp.zeros(shape, F32)
                for u in range(KS):
                    if 0 <= q - u < height + EDGE:
                        total = jnp.where(out_row == q - u, bands[u], total)
                at = place_of(kind, q)
                scratch[at : at + EDGE] = total
    for start in range(0, scratch.shape[0], 64):
        high, low = split(scratch[start : start + 64])
        s_high[start : start + 64] = high
        s_low[start : start + 64] = low


def blur_into(b_ref, a2_high, a2_low, side, w_high, w_low, s_high, s_low, acc):
    pairs, channels, double = acc.shape
    width = double // 2
    for d in range(RADIUS + 1):
        high = a2_high[d : d + pairs].reshape(pairs * channels, double)
        low = a2_low[d : d + pairs].reshape(pairs * channels, double)
        part = mm_split(high, low, w_high[d], w_low[d])
        part = part.reshape(pairs, channels, double)
        if d == 0:
            acc[...] = part
        else:
            acc[...] += part
    side_high, side_low = split(side)
    rim = mm_split(side_high, side_low, s_high[...], s_low[...])
    for i in range(2 * pairs):
        row = acc[i // 2, :, i % 2 * width : i % 2 * width + width]
        b_ref[i] = add_rim(row, rim, i)


def start_kernel(
    rows_ref, p1, p2, left, right, above, below, place, w_high, w_low, s_high, s_low,
    ext_ref, side_ref, b_ref, a2_high, a2_low, acc,
):
    height, channels, width = rows_ref.shape
    odd = place[ROW_ODD] == 1
    for a in range(height + EDGE):
        if a < RADIUS:
            row = jnp.where(odd, p1[a * channels : a * channels + channels], p2[a * channels : a * channels + channels])
            row = jnp.where(place[UP] == 1, row, 0.0)
        elif a < RADIUS + height:
            row = rows_ref[a - RADIUS]
        else:
            k = (a - RADIUS - height) * channels
            row = jnp.where(odd, p2[k : k + channels], p1[k : k + channels])
            row = jnp.where(place[DOWN] == 1, row, 0.0)
        ext_ref[a] = row
        high, low = split(row)
        a2_high[a // 2, :, a % 2 * width : a % 2 * width + width] = high
        a2_low[a // 2, :, a % 2 * width : a % 2 * width + width] = low
    side = assemble_side(left[...], right[...], above[...], below[...], height)
    side_ref[...] = side
    blur_into(b_ref, a2_high, a2_low, side, w_high, w_low, s_high, s_low, acc)


def spectral_kernel(
    obs_ref, bend_ref, b_ref, mine, other, place,
    g_mine, core_ref, main1, main2, cross_ref, rows_ref,
    total, *, scale,
):
    height, channels, width = b_ref.shape
    bands = obs_ref.shape[1]
    quarter = bands // 4
    second = place[HALF] == 1
    m0 = jnp.where(second, other[...], mine[...])
    m1 = jnp.where(second, mine[...], other[...])
    spectra = jnp.concatenate([m0[:, :channels], m0[:, channels:], m1[:, :channels], m1[:, channels:]], axis=0)
    m_high, m_low = split(spectra)
    m_cat = jnp.concatenate([m_high, m_low, m_high], axis=1)
    t_high, t_low = split(spectra.T)
    t_cat = jnp.concatenate([t_high, t_low], axis=0)
    rows = []
    for pair in range(height // 2):
        b_pair = jnp.concatenate([b_ref[2 * pair], b_ref[2 * pair + 1]], axis=1)
        b_high, b_low = split(b_pair)
        b_cat = jnp.concatenate([b_high, b_high, b_low], axis=0)
        linear = mm(m_cat, b_cat) * scale
        seen = jnp.concatenate([obs_ref[2 * pair], obs_ref[2 * pair + 1]], axis=1)
        bend = jnp.concatenate([bend_ref[2 * pair : 2 * pair + 1], bend_ref[2 * pair + 1 : 2 * pair + 2]], axis=1)
        bent = bend * linear
        resid = linear + bent * linear - seen
        weighted = resid * (1.0 + 2.0 * bent)
        w_high, w_low = split(weighted)
        part = mm_nt(w_high, jnp.concatenate([b_high, b_low], axis=0))
        part = part[:, :channels] + part[:, channels:] + mm_nt(w_low, b_high)
        if pair == 0:
            total[...] = part
        else:
            total[...] += part
        both = mm(t_cat, w_high)
        grad = (both[:channels] + both[channels:] + mm(t_high, w_low)) * scale
        for k in range(2):
            row = grad[:, k * width : k * width + width]
            rows_ref[2 * pair + k] = row
            rows.append(row)
    low, high = edges(rows, True), edges(rows, False)
    col_odd = place[COL_ODD] == 1
    core_ref[2 * quarter // 2 :] = jnp.where(col_odd, low, high)
    cross_ref[...] = jnp.where(col_odd, high, low)
    row_odd = place[ROW_ODD] == 1
    halo = main1.shape[0]
    for i in range(halo):
        main1[i] = jnp.where(row_odd, rows[i], rows[height - halo + i])
        main2[i] = jnp.where(row_odd, rows[height - halo + i], rows[i])
    g = total[...] * scale
    g0 = jnp.concatenate([g[:quarter], g[quarter : 2 * quarter]], axis=1)
    g1 = jnp.concatenate([g[2 * quarter : 3 * quarter], g[3 * quarter :]], axis=1)
    g_mine[...] = jnp.where(second, g1, g0)
    core_ref[:quarter] = jnp.where(second, g0, g1)


def put_pair(high_ref, low_ref, index, row):
    width = row.shape[1]
    at = (index // 2, slice(None), slice(index % 2 * width, index % 2 * width + width))
    high_ref[at], low_ref[at] = split(row)


def adjoint_into(acc, g_high, g_low, first, w_high, w_low, band):
    pairs, channels, double = g_high.shape
    for d in range(RADIUS + 1):
        begin, end = max(first, d), min(first + pairs, acc.shape[0] + d)
        if begin >= end:
            continue
        high = g_high[begin - first : end - first].reshape((end - begin) * channels, double)
        low = g_low[begin - first : end - first].reshape((end - begin) * channels, double)
        part = mm_split(high, low, w_high[band, d], w_low[band, d])
        acc[begin - d : end - d] += part.reshape(end - begin, channels, double)


def own_maps_kernel(rows_ref, wa_high, wa_low, acc, near_ref, g_high, g_low):
    height, channels, width = rows_ref.shape
    lane = lanes((channels, width))
    near = [jnp.zeros((channels, width), F32) for _ in range(2)]
    for i in range(height):
        row = rows_ref[i]
        put_pair(g_high, g_low, i, row)
        q = i + EDGE
        moved = pltpu.roll(row, (RADIUS + q * EDGE) % width, 1)
        near[q // height] = jnp.where(lane // EDGE == q % height, moved, near[q // height])
    near_ref[...] = jnp.concatenate(near, axis=1)
    acc[...] = jnp.zeros_like(acc)
    adjoint_into(acc, g_high, g_low, EDGE // 2, wa_high, wa_low, 1)


def halo_maps_kernel(acc_in, near_in, p1, p2, place, wa_high, wa_low, acc, near_ref, g_high, g_low):
    channels = near_in.shape[0]
    width = near_in.shape[1] // 2
    height = 2 * acc.shape[0] - EDGE
    odd = place[ROW_ODD] == 1
    lane = lanes((channels, width))
    near = [near_in[:, :width], near_in[:, width:]]
    halo = p1.shape[0]
    for k in range(2 * halo):
        if k < halo:
            q = EDGE - halo + k
            row = jnp.where(place[UP] == 1, jnp.where(odd, p1[k], p2[k]), 0.0)
        else:
            q = EDGE + height + k - halo
            row = jnp.where(place[DOWN] == 1, jnp.where(odd, p2[k - halo], p1[k - halo]), 0.0)
        put_pair(g_high, g_low, k, row)
        moved = pltpu.roll(row, (RADIUS + q * EDGE) % width, 1)
        near[q // height] = jnp.where(lane // EDGE == q % height, moved, near[q // height])
    near_ref[...] = jnp.concatenate(near, axis=1)
    n = halo // 2
    adjoint_into(acc, g_high.at[:n], g_low.at[:n], EDGE // 2 - n, wa_high, wa_low, 0)
    adjoint_into(acc, g_high.at[n:], g_low.at[n:], (EDGE + height) // 2, wa_high, wa_low, 2)


def maps_kernel(
    ext_ref, side_ref, acc, near_ref, left, right, above, below, place, sa_high, sa_low, *rest, last,
):
    if last:
        (out_ref,) = rest
        height = out_ref.shape[1]
    else:
        (wf_high, wf_low, sf_high, sf_low, ext_out, side_out, b_ref, a2_high, a2_low, acc_b) = rest
        height = b_ref.shape[0]
    width = left.shape[1]
    ext_rows = height + EDGE
    side_in = jnp.concatenate([left[...], right[...], above[...], below[...], near_ref[...]], axis=1)
    side_high, side_low = split(side_in)
    half = sa_high.shape[1] // 2
    far = sa_high.shape[0] - 2 * width
    rim = mm_split(side_high[:, :far], side_low[:, :far], sa_high[:far, half:], sa_low[:far, half:])
    for a in range(ext_rows):
        if last and not RADIUS <= a < RADIUS + height:
            continue
        grad = add_rim(acc[a // 2, :, a % 2 * width : a % 2 * width + width], rim, a)
        row = jnp.maximum(ext_ref[a] - 0.5 * grad, 0.0)
        if last:
            out_ref[:, a - RADIUS, :] = row
            continue
        if a < RADIUS:
            row = jnp.where(place[UP] == 1, row, 0.0)
        elif a >= RADIUS + height:
            row = jnp.where(place[DOWN] == 1, row, 0.0)
        ext_out[a] = row
        put_pair(a2_high, a2_low, a, row)
    if last:
        return
    side_grad = mm_split(side_high, side_low, sa_high[:, :half], sa_low[:, :half])
    side = jnp.maximum(side_ref[...] - 0.5 * side_grad, 0.0)
    where = lanes(side.shape)
    a, c = where // EDGE, where % EDGE
    outside = (
        ((a < RADIUS) & (place[UP] == 0))
        | ((a >= RADIUS + height) & (place[DOWN] == 0))
        | ((c < RADIUS) & (place[LEFT] == 0))
        | ((c >= RADIUS) & (place[RIGHT] == 0))
        | (a >= ext_rows)
    )
    side = jnp.where(outside, 0.0, side)
    side_out[...] = side
    blur_into(b_ref, a2_high, a2_low, side, wf_high, wf_low, sf_high, sf_low, acc_b)


def spectra_kernel(mine, other, place, out_ref):
    channels, depth = out_ref.shape
    second = place[HALF] == 1
    first = jnp.where(second, other[...], mine[...])
    last = jnp.where(second, mine[...], other[...])
    parts = [first[:, :channels], first[:, channels:], last[:, :channels], last[:, channels:]]
    out_ref[...] = jnp.concatenate(parts, axis=0).T[:, :depth]


def call(kernel, micros, outs, scratch, specs, *args, aliases=None):
    return pl.pallas_call(
        kernel,
        out_shape=[jax.ShapeDtypeStruct(s, d) for s, d in outs],
        in_specs=specs,
        out_specs=[VMEM] * len(outs),
        scratch_shapes=[pltpu.VMEM(*s) if isinstance(s, tuple) else s for s in scratch],
        input_output_aliases=aliases or {},
        compiler_params=PARAMS,
        cost_estimate=pl.CostEstimate(
            flops=int(micros * 1.15e9), bytes_accessed=int(micros * 3.7e6), transcendentals=0
        ),
    )(*args)


def core_swap(x):
    count = lax.axis_size("cols")
    return lax.ppermute(x, "cols", [(i, i ^ 1) for i in range(count)])


def cross_swap(x):
    count = lax.axis_size("cols")
    return lax.ppermute(x, "cols", [(i, (i + 1 if i % 2 else i - 1) % count) for i in range(count)])


def pair_one(x):
    count = lax.axis_size("rows")
    return lax.ppermute(x, "rows", [(i, i ^ 1) for i in range(count)])


def pair_two(x):
    count = lax.axis_size("rows")
    return lax.ppermute(x, "rows", [(i, min(max(i + 1 if i % 2 else i - 1, 0), count - 1)) for i in range(count)])


def col_swap(x, mask):
    count = lax.axis_size("cols")
    return lax.ppermute(x, "cols", [(i, (((i + 1) % count ^ mask) - 1) % count) for i in range(count)])


def row_swap(x, mask):
    count = lax.axis_size("rows")
    return lax.ppermute(x, "rows", [(i, i ^ mask) for i in range(count)])


def on_device(observed, nonlin, abundance, spectra, kernels, tile_family):
    bands, height, width = observed.shape
    channels = abundance.shape[0]
    n_rows, n_cols = lax.axis_size("rows"), lax.axis_size("cols")
    row_at, col_at = lax.axis_index("rows"), lax.axis_index("cols")
    pixel_count = height * width * n_rows * n_cols
    quarter = -(-bands // 32) * 8
    full = 4 * quarter
    half_of = ((col_at + 1) // 2) % 2
    col_odd, row_odd = col_at % 2 == 1, row_at % 2 == 1
    place = jnp.stack(
        [row_at % 2, col_at % 2, row_at > 0, row_at < n_rows - 1, col_at > 0, col_at < n_cols - 1, half_of]
    ).astype(jnp.int32)
    has_left = (col_at > 0).astype(F32)
    has_right = (col_at < n_cols - 1).astype(F32)
    has_up = (row_at > 0).astype(F32)
    has_down = (row_at < n_rows - 1).astype(F32)
    table = jnp.transpose(kernels, (1, 0, 2))
    place, abundance, row_odd, col_odd, has_left, has_right, has_up, has_down = lax.optimization_barrier(
        (place, abundance, row_odd, col_odd, has_left, has_right, has_up, has_down)
    )
    tile = (channels, width)

    def sides(core, cross):
        left = jnp.where(col_odd, core, cross) * has_left
        right = jnp.where(col_odd, cross, core) * has_right
        lane = lanes(tile) < width // 2
        up_msg = jnp.where(lane, left, right)
        down_msg = jnp.where(lane, right, left)
        return left, right, jnp.where(row_odd, up_msg, down_msg), jnp.where(row_odd, down_msg, up_msg)

    a_rows, e_core, e_cross, mark = call(
        first_kernel,
        1,
        [((height,) + tile, F32), ((channels + 8, width), F32), ((channels + 8, width), F32), ((8, width), F32)],
        [],
        [SMEM, VMEM, SMEM],
        tile_family, abundance, place,
    )
    got_core = core_swap(e_core)
    got_cross = cross_swap(e_cross)
    left, right, side1, side2 = sides(got_core[:channels], got_cross[:channels])
    mark_left = jnp.where(col_odd, got_core[channels:], got_cross[channels:])
    mark_right = jnp.where(col_odd, got_cross[channels:], got_core[channels:])
    marks = jnp.concatenate([mark_left, mark, mark_right])
    top = a_rows[:RADIUS].reshape(RADIUS * channels, width)
    bottom = a_rows[height - RADIUS :].reshape(RADIUS * channels, width)
    got1 = pair_one(jnp.concatenate([jnp.where(row_odd, top, bottom), side1, marks]))
    got2 = pair_two(jnp.concatenate([jnp.where(row_odd, bottom, top), side2, marks]))
    body = RADIUS * channels

    def above_below(x1, x2):
        return jnp.where(row_odd, x1, x2), jnp.where(row_odd, x2, x1)

    above, below = above_below(got1[body : body + channels], got2[body : body + channels])
    above, below = above * has_up, below * has_down
    pairs = height // 2
    ext_rows = height + EDGE
    main_w = ((RADIUS + 1, 2 * width, 2 * width), BF16)
    side_f = ((2 * width, height * EDGE), BF16)
    hbm = pl.BlockSpec(memory_space=pltpu.HBM)
    half_shape = ((quarter, 2 * channels), F32)
    seen, mine, other, *wf = call(
        forward_weights_kernel,
        3,
        [((height, full, width), F32), half_shape, half_shape, main_w, main_w, side_f, side_f],
        [pltpu.SemaphoreType.DMA((height,))],
        [SMEM, SMEM, SMEM, hbm, VMEM],
        tile_family, table, place, observed, spectra.T,
    )
    got1, got2, seen, mine, other, *wf = lax.optimization_barrier((got1, got2, seen, mine, other, *wf))
    ext, side, blurred = call(
        start_kernel,
        2,
        [((ext_rows,) + tile, F32), ((channels, 2 * width), F32), ((height,) + tile, F32)],
        [((ext_rows // 2, channels, 2 * width), BF16)] * 2 + [((pairs, channels, 2 * width), F32)],
        [VMEM] * 7 + [SMEM] + [VMEM] * 4,
        a_rows, got1, got2, left, right, above, below, place, *wf,
    )
    marks_up, marks_down = above_below(got1[body + channels :], got2[body + channels :])
    main_a = ((3, RADIUS + 1, 2 * width, 2 * width), BF16)
    side_a = ((6 * width, 4 * width), BF16)

    def adjoint_weights():
        return call(
            functools.partial(adjoint_weights_kernel, height=height, width=width),
            3,
            [main_a, main_a, side_a, side_a],
            [((6 * width, 4 * width), F32)],
            [VMEM, VMEM, VMEM, SMEM],
            marks_up, marks, marks_down, table,
        )

    rate = 40.0 / pixel_count
    acc_shape = ((ext_rows // 2, channels, 2 * width), F32)
    near_shape = ((channels, 2 * width), F32)

    def own_part(g_rows, wa):
        return call(
            own_maps_kernel,
            2,
            [acc_shape, near_shape],
            [((pairs, channels, 2 * width), BF16)] * 2,
            [VMEM] * 3,
            g_rows, wa[0], wa[1],
        )

    for step in range(ITERS):
        last = step == ITERS - 1
        halo = RADIUS if last else EDGE
        g_mine, to_core, main1, main2, e_cross, g_rows = call(
            functools.partial(spectral_kernel, scale=1.0 / channels),
            5,
            [
                ((quarter, 2 * channels), F32),
                ((quarter + channels, width), F32),
                ((halo,) + tile, F32),
                ((halo,) + tile, F32),
                (tile, F32),
                ((height,) + tile, F32),
            ],
            [((full, channels), F32)],
            [VMEM] * 5 + [SMEM],
            seen, nonlin, blurred, mine, other, place,
        )
        got_core = core_swap(to_core)
        p1 = pair_one(main1)
        share = g_mine + got_core[:quarter]
        if step > 0:
            own, near = own_part(g_rows, wa)
            main2, own, near = lax.optimization_barrier((main2, own, near))
        p2 = pair_two(main2)
        got_cross = cross_swap(jnp.concatenate([share, e_cross]))
        if step == 0:
            wa = adjoint_weights()
            got_cross, *wa = lax.optimization_barrier((got_cross, *wa))
            own, near = own_part(g_rows, wa)
        share = share + got_cross[:quarter]
        left, right, side1, side2 = sides(got_core[quarter:], got_cross[quarter:])
        step_size = 4
        while step_size < n_cols:
            share = share + col_swap(share, step_size)
            step_size *= 2
        share, own, near = lax.optimization_barrier((share, own, near))
        own, near = call(
            halo_maps_kernel,
            1.5,
            [acc_shape, near_shape],
            [((halo, channels, 2 * width), BF16)] * 2,
            [VMEM] * 4 + [SMEM] + [VMEM] * 2,
            own, near, p1, p2, place, wa[0], wa[1],
            aliases={0: 0, 1: 1},
        )
        got1 = pair_one(jnp.concatenate([share, side1]))
        if n_rows == 4:
            got2 = row_swap(jnp.concatenate([share, side2]), 3)
            got3 = row_swap(share, 2)
            got1, got2, own, near = lax.optimization_barrier((got1, got2, own, near))
            share = (share + got1[:quarter]) + (got3 + got2[:quarter])
            got2 = got2[quarter:]
        else:
            got2 = pair_two(side2)
            got1, got2, own, near = lax.optimization_barrier((got1, got2, own, near))
            share = share + got1[:quarter]
            step_size = 2
            while step_size < n_rows:
                share = share + row_swap(share, step_size)
                step_size *= 2
        above, below = above_below(got1[quarter:], got2)
        above, below = above * has_up, below * has_down
        gathered = (ext, side, own, near, left, right, above, below, place) + tuple(wa[2:])
        if last:
            made = call(
                functools.partial(maps_kernel, last=True),
                1.5,
                [((channels, height, width), F32)],
                [],
                [VMEM] * 8 + [SMEM] + [VMEM] * 2,
                *gathered,
            )
        else:
            made = call(
                functools.partial(maps_kernel, last=False),
                2.5,
                [((ext_rows,) + tile, F32), ((channels, 2 * width), F32), ((height,) + tile, F32)],
                [((ext_rows // 2, channels, 2 * width), BF16)] * 2 + [((pairs, channels, 2 * width), F32)],
                [VMEM] * 8 + [SMEM] + [VMEM] * 6,
                *gathered, *wf,
            )
        mine = jnp.maximum(mine - rate * share, 0.0)
        other = core_swap(mine)
        if last:
            (out,) = made
        else:
            ext, side, blurred = made
    (result,) = call(spectra_kernel, 1, [((channels, bands), F32)], [], [VMEM, VMEM, SMEM], mine, other, place)
    return out, result.T


def solution(mesh):
    placed = (
        P(None, "rows", "cols"),
        P("rows", "cols"),
        P(None, "rows", "cols"),
        P(),
        P(),
        P("rows", "cols"),
    )
    return jax.shard_map(
        on_device,
        mesh=mesh,
        in_specs=placed,
        out_specs=(P(None, "rows", "cols"), P()),
        check_vma=False,
    )
```

```python
import functools

import jax
import jax.numpy as jnp
import numpy as np
from jax import lax
from jax.experimental import pallas as pl
from jax.experimental.pallas import tpu as pltpu
from jax.sharding import PartitionSpec as P

KS = 9
RADIUS = KS // 2
EDGE = 2 * RADIUS
ITERS = 3
F32 = jnp.float32
BF16 = jnp.bfloat16
VMEM = pl.BlockSpec(memory_space=pltpu.VMEM)
SMEM = pl.BlockSpec(memory_space=pltpu.SMEM)
PARAMS = pltpu.CompilerParams(vmem_limit_bytes=18 * 1024 * 1024)
ROW_ODD, COL_ODD, UP, DOWN, LEFT, RIGHT, HALF = range(7)


def split(x):
    high = x.astype(BF16)
    return high, (x - high.astype(F32)).astype(BF16)


def mm(a, b):
    return jnp.dot(a, b, preferred_element_type=F32)


def mm_split(high, low, w_high, w_low):
    rows = high.shape[0]
    both = mm(jnp.concatenate([high, low], axis=0), w_high)
    return both[:rows] + both[rows:] + mm(high, w_low)


def mm_nt(a, b):
    return lax.dot_general(a, b, (((1,), (1,)), ((), ())), preferred_element_type=F32)


def lanes(shape):
    return lax.broadcasted_iota(jnp.int32, shape, len(shape) - 1)


def edges(rows, swapped):
    count = len(rows)
    lane = lanes(rows[0].shape)
    width = rows[0].shape[1]
    out = jnp.zeros_like(rows[0])
    for i, row in enumerate(rows):
        place = (i + count // 2) % count if swapped else i
        first = 0 if swapped else width - EDGE
        moved = pltpu.roll(row, (place * EDGE - first) % width, 1)
        out = jnp.where(lane // EDGE == place, moved, out)
    return out


def wide(x, total, shift):
    padded = jnp.concatenate([x, jnp.zeros((x.shape[0], total - x.shape[1]), x.dtype)], axis=1)
    return pltpu.roll(padded, shift % total, 1)


def assemble_side(left, right, above, below, height):
    total = 2 * left.shape[1]
    lane = lanes((left.shape[0], total))
    row, col = lane // EDGE, lane % EDGE
    on_left = col < RADIUS
    own = (row >= RADIUS) & (row < RADIUS + height)
    top = row < RADIUS
    bottom = (row >= RADIUS + height) & (row < 2 * RADIUS + height)
    half = EDGE * height // 2
    lo = RADIUS * EDGE - RADIUS
    hi = RADIUS * EDGE + RADIUS
    base = (RADIUS + height) * EDGE
    out = jnp.zeros((left.shape[0], total), F32)
    out = jnp.where(own & on_left, wide(left, total, lo), out)
    first = (row - RADIUS) < height // 2
    out = jnp.where(own & ~on_left & first, wide(right, total, hi - half), out)
    out = jnp.where(own & ~on_left & ~first, wide(right, total, hi + half), out)
    out = jnp.where(top & ~on_left, wide(above, total, RADIUS - RADIUS * EDGE), out)
    out = jnp.where(top & on_left, wide(above, total, -half - RADIUS * EDGE - RADIUS), out)
    out = jnp.where(bottom & on_left, wide(below, total, base - RADIUS), out)
    out = jnp.where(bottom & ~on_left, wide(below, total, base + RADIUS - half), out)
    return out


def add_rim(row, contrib, index):
    width = row.shape[1]
    start = index * EDGE
    part = contrib[:, start // width * width : start // width * width + width]
    moved = pltpu.roll(part, (-(start % width) - RADIUS) % width, 1)
    lane = lanes(row.shape)
    near = (lane < RADIUS) | (lane >= width - RADIUS)
    return row + jnp.where(near, moved, 0.0)


def first_kernel(family, a_ref, place, rows_ref, e_core, e_cross, mark_ref):
    channels, height, width = a_ref.shape
    rows = []
    for i in range(height):
        row = a_ref[:, i, :]
        rows_ref[i] = row
        rows.append(row)
    low, high = edges(rows, True), edges(rows, False)
    odd = place[COL_ODD] == 1
    e_core[:channels] = jnp.where(odd, low, high)
    e_cross[:channels] = jnp.where(odd, high, low)
    mark = jnp.full((8, width), family[0, 0].astype(F32), F32)
    e_core[channels:] = mark
    e_cross[channels:] = mark
    mark_ref[...] = mark


def band_sum(taps, delta):
    total = jnp.zeros(delta.shape, F32)
    for v in range(KS):
        total = jnp.where(delta == v, taps[v], total)
    return total


def build_main(taps, w_high, w_low, index, width):
    shape = (width, width)
    delta = lax.broadcasted_iota(jnp.int32, shape, 0) - lax.broadcasted_iota(jnp.int32, shape, 1) + RADIUS
    blank = jnp.zeros(shape, BF16)
    for u in range(-1, KS + 1):
        if 0 <= u < KS:
            high, low = split(band_sum([taps(u, v) for v in range(KS)], delta))
        else:
            high, low = blank, blank
        for r in range(2):
            for ro in range(2):
                if (u + ro - r) % 2 == 0:
                    d = (u + ro - r) // 2
                    if 0 <= d <= RADIUS:
                        at = index + (d, slice(r * width, r * width + width), slice(ro * width, ro * width + width))
                        w_high[at] = high
                        w_low[at] = low


def rim_column(lane, width):
    c = lane % EDGE
    return jnp.where(c < RADIUS, width - RADIUS + c, c - RADIUS)


def side_column(lane, width):
    c = lane % EDGE
    return jnp.where(c < RADIUS, c - RADIUS, width + c - RADIUS)


def forward_weights_kernel(family, table, place, obs_ref, spectra_ref, seen_ref, mine, other, w_high, w_low, s_high, s_low, sems):
    depth, height, width = obs_ref.shape
    copies = []
    for i in range(height):
        copies.append(pltpu.make_async_copy(obs_ref.at[:, i, :], seen_ref.at[i, pl.ds(0, depth), :], sems.at[i]))
        copies[-1].start()
    start = depth // 8 * 8
    channels = spectra_ref.shape[0]
    quarter = seen_ref.shape[1] // 4
    total = -(-seen_ref.shape[1] // 128) * 128
    spectra = jnp.concatenate([spectra_ref[...], jnp.zeros((channels, total - depth), F32)], axis=1).T
    halves = [
        jnp.concatenate([spectra[q * quarter : (q + 1) * quarter], spectra[(q + 1) * quarter : (q + 2) * quarter]], axis=1)
        for q in (0, 2)
    ]
    second = place[HALF] == 1
    mine[...] = jnp.where(second, halves[1], halves[0])
    other[...] = jnp.where(second, halves[0], halves[1])
    own = lambda u, v: table[u, family[0, 0], v]
    build_main(own, w_high, w_low, (), width)
    n = height * EDGE
    shape = (EDGE, n)
    lane = lanes(shape)
    c = lax.broadcasted_iota(jnp.int32, shape, 0)
    delta = side_column(c, width) - rim_column(lane, width) + RADIUS
    out_row = lane // EDGE
    bands = [band_sum([own(u, v) for v in range(KS)], delta) for u in range(KS)]
    rows = s_high.shape[0] // EDGE
    for a in range(0, rows, 2):
        blocks = []
        for b in (a, a + 1):
            total = jnp.zeros(shape, F32)
            for u in range(KS):
                total = jnp.where(out_row == b - u, bands[u], total)
            blocks.append(total)
        high, low = split(jnp.concatenate(blocks, axis=0))
        s_high[a * EDGE : a * EDGE + 2 * EDGE] = high
        s_low[a * EDGE : a * EDGE + 2 * EDGE] = low
    for i in range(height):
        copies[i].wait()
    sub = lax.broadcasted_iota(jnp.int32, (seen_ref.shape[1] - start, width), 0)
    for i in range(height):
        seen_ref[i, start:] = jnp.where(sub < depth - start, seen_ref[i, start:], 0.0)


def flipped(table, family):
    return lambda u, v: table[KS - 1 - u, family, KS - 1 - v]


def own_weights_kernel(marks, table, w_high, w_low):
    family = jnp.max(marks[8:16]).astype(jnp.int32)
    build_main(flipped(table, family), w_high, w_low, (), w_high.shape[1] // 2)


def halo_weights_kernel(
    marks_up, marks, marks_down, table, w_high, w_low, s_high, s_low, scratch, *, height, width
):
    families = []
    for ref in (marks_up, marks, marks_down):
        for k in range(3):
            families.append(jnp.max(ref[8 * k : 8 * k + 8]).astype(jnp.int32))
    for b in range(2):
        build_main(flipped(table, families[6 * b + 1]), w_high, w_low, (b,), width)
    n = s_high.shape[1]
    half = n // 2
    shape = (EDGE, n)
    lane = lanes(shape)
    c = lax.broadcasted_iota(jnp.int32, shape, 0)
    to_side = lane < half
    column = jnp.where(to_side, side_column(lane, width), rim_column(lane, width))
    out_row = jnp.where(to_side, lane, lane - half) // EDGE
    out_row = jnp.where(out_row < height + EDGE, out_row, -KS - 1)
    sources = (c - EDGE, width + c, rim_column(c, width))
    chunk = height * EDGE
    mid = chunk // 2

    def place_of(kind, q):
        i = q - EDGE
        if kind == 2:
            return 4 * chunk + q * EDGE
        if 0 <= i < height:
            return i * EDGE if kind == 0 else chunk + (i + height // 2) % height * EDGE
        if i < 0:
            return 2 * chunk + (mid if kind == 0 else 0) + q * EDGE
        return 3 * chunk + (0 if kind == 0 else mid) + (i - height) * EDGE

    for kind in range(3):
        delta = sources[kind] - column + RADIUS
        if kind == 2:
            delta = jnp.where(to_side, delta, -1)
        for b in range(3):
            tile = 3 * b + (0, 2, 1)[kind]
            bands = [
                band_sum([table[KS - 1 - u, families[tile], KS - 1 - v] for v in range(KS)], delta) for u in range(KS)
            ]
            q_range = (range(0, EDGE), range(EDGE, EDGE + height), range(EDGE + height, 2 * EDGE + height))[b]
            for q in q_range:
                total = jnp.zeros(shape, F32)
                for u in range(KS):
                    if 0 <= q - u < height + EDGE:
                        total = jnp.where(out_row == q - u, bands[u], total)
                at = place_of(kind, q)
                scratch[at : at + EDGE] = total
    for start in range(0, scratch.shape[0], 64):
        high, low = split(scratch[start : start + 64])
        s_high[start : start + 64] = high
        s_low[start : start + 64] = low


def blur_into(b_ref, a2_high, a2_low, side, w_high, w_low, s_high, s_low, acc):
    pairs, channels, double = acc.shape
    width = double // 2
    for d in range(RADIUS + 1):
        high = a2_high[d : d + pairs].reshape(pairs * channels, double)
        low = a2_low[d : d + pairs].reshape(pairs * channels, double)
        part = mm_split(high, low, w_high[d], w_low[d])
        part = part.reshape(pairs, channels, double)
        if d == 0:
            acc[...] = part
        else:
            acc[...] += part
    side_high, side_low = split(side)
    rim = mm_split(side_high, side_low, s_high[...], s_low[...])
    for i in range(2 * pairs):
        row = acc[i // 2, :, i % 2 * width : i % 2 * width + width]
        b_ref[i] = add_rim(row, rim, i)


def start_kernel(
    rows_ref, p1, p2, left, right, above, below, place, w_high, w_low, s_high, s_low,
    ext_ref, side_ref, b_ref, a2_high, a2_low, acc,
):
    height, channels, width = rows_ref.shape
    odd = place[ROW_ODD] == 1
    for a in range(height + EDGE):
        if a < RADIUS:
            row = jnp.where(odd, p1[a * channels : a * channels + channels], p2[a * channels : a * channels + channels])
            row = jnp.where(place[UP] == 1, row, 0.0)
        elif a < RADIUS + height:
            row = rows_ref[a - RADIUS]
        else:
            k = (a - RADIUS - height) * channels
            row = jnp.where(odd, p2[k : k + channels], p1[k : k + channels])
            row = jnp.where(place[DOWN] == 1, row, 0.0)
        ext_ref[a] = row
        high, low = split(row)
        a2_high[a // 2, :, a % 2 * width : a % 2 * width + width] = high
        a2_low[a // 2, :, a % 2 * width : a % 2 * width + width] = low
    side = assemble_side(left[...], right[...], above[...], below[...], height)
    side_ref[...] = side
    blur_into(b_ref, a2_high, a2_low, side, w_high, w_low, s_high, s_low, acc)


def spectral_kernel(
    obs_ref, bend_ref, b_ref, mine, other, place,
    g_mine, core_ref, main1, main2, cross_ref, rows_ref,
    total, *, scale,
):
    height, channels, width = b_ref.shape
    bands = obs_ref.shape[1]
    quarter = bands // 4
    second = place[HALF] == 1
    m0 = jnp.where(second, other[...], mine[...])
    m1 = jnp.where(second, mine[...], other[...])
    spectra = jnp.concatenate([m0[:, :channels], m0[:, channels:], m1[:, :channels], m1[:, channels:]], axis=0)
    m_high, m_low = split(spectra)
    m_cat = jnp.concatenate([m_high, m_low, m_high], axis=1)
    t_high, t_low = split(spectra.T)
    t_cat = jnp.concatenate([t_high, t_low], axis=0)
    rows = []
    for pair in range(height // 2):
        b_pair = jnp.concatenate([b_ref[2 * pair], b_ref[2 * pair + 1]], axis=1)
        b_high, b_low = split(b_pair)
        b_cat = jnp.concatenate([b_high, b_high, b_low], axis=0)
        linear = mm(m_cat, b_cat) * scale
        seen = jnp.concatenate([obs_ref[2 * pair], obs_ref[2 * pair + 1]], axis=1)
        bend = jnp.concatenate([bend_ref[2 * pair : 2 * pair + 1], bend_ref[2 * pair + 1 : 2 * pair + 2]], axis=1)
        bent = bend * linear
        resid = linear + bent * linear - seen
        weighted = resid * (1.0 + 2.0 * bent)
        w_high, w_low = split(weighted)
        part = mm_nt(w_high, jnp.concatenate([b_high, b_low], axis=0))
        part = part[:, :channels] + part[:, channels:] + mm_nt(w_low, b_high)
        if pair == 0:
            total[...] = part
        else:
            total[...] += part
        both = mm(t_cat, w_high)
        grad = (both[:channels] + both[channels:] + mm(t_high, w_low)) * scale
        for k in range(2):
            row = grad[:, k * width : k * width + width]
            rows_ref[2 * pair + k] = row
            rows.append(row)
    low, high = edges(rows, True), edges(rows, False)
    col_odd = place[COL_ODD] == 1
    core_ref[2 * quarter // 2 :] = jnp.where(col_odd, low, high)
    cross_ref[...] = jnp.where(col_odd, high, low)
    row_odd = place[ROW_ODD] == 1
    halo = main1.shape[0]
    for i in range(halo):
        main1[i] = jnp.where(row_odd, rows[i], rows[height - halo + i])
        main2[i] = jnp.where(row_odd, rows[height - halo + i], rows[i])
    g = total[...] * scale
    g0 = jnp.concatenate([g[:quarter], g[quarter : 2 * quarter]], axis=1)
    g1 = jnp.concatenate([g[2 * quarter : 3 * quarter], g[3 * quarter :]], axis=1)
    g_mine[...] = jnp.where(second, g1, g0)
    core_ref[:quarter] = jnp.where(second, g0, g1)


def put_pair(high_ref, low_ref, index, row):
    width = row.shape[1]
    at = (index // 2, slice(None), slice(index % 2 * width, index % 2 * width + width))
    high_ref[at], low_ref[at] = split(row)


def adjoint_into(acc, g_high, g_low, first, w_high, w_low):
    pairs, channels, double = g_high.shape
    for d in range(RADIUS + 1):
        begin, end = max(first, d), min(first + pairs, acc.shape[0] + d)
        if begin >= end:
            continue
        high = g_high[begin - first : end - first].reshape((end - begin) * channels, double)
        low = g_low[begin - first : end - first].reshape((end - begin) * channels, double)
        part = mm_split(high, low, w_high[d], w_low[d])
        acc[begin - d : end - d] += part.reshape(end - begin, channels, double)


def own_maps_kernel(rows_ref, wa_high, wa_low, acc, near_ref, g_high, g_low):
    height, channels, width = rows_ref.shape
    lane = lanes((channels, width))
    near = [jnp.zeros((channels, width), F32) for _ in range(2)]
    for i in range(height):
        row = rows_ref[i]
        put_pair(g_high, g_low, i, row)
        q = i + EDGE
        moved = pltpu.roll(row, (RADIUS + q * EDGE) % width, 1)
        near[q // height] = jnp.where(lane // EDGE == q % height, moved, near[q // height])
    near_ref[...] = jnp.concatenate(near, axis=1)
    acc[...] = jnp.zeros_like(acc)
    adjoint_into(acc, g_high, g_low, EDGE // 2, wa_high, wa_low)


def halo_maps_kernel(acc_in, near_in, p1, p2, place, wa_high, wa_low, acc, near_ref, g_high, g_low):
    channels = near_in.shape[0]
    width = near_in.shape[1] // 2
    height = 2 * acc.shape[0] - EDGE
    odd = place[ROW_ODD] == 1
    lane = lanes((channels, width))
    near = [near_in[:, :width], near_in[:, width:]]
    halo = p1.shape[0]
    for k in range(2 * halo):
        if k < halo:
            q = EDGE - halo + k
            row = jnp.where(place[UP] == 1, jnp.where(odd, p1[k], p2[k]), 0.0)
        else:
            q = EDGE + height + k - halo
            row = jnp.where(place[DOWN] == 1, jnp.where(odd, p2[k - halo], p1[k - halo]), 0.0)
        put_pair(g_high, g_low, k, row)
        moved = pltpu.roll(row, (RADIUS + q * EDGE) % width, 1)
        near[q // height] = jnp.where(lane // EDGE == q % height, moved, near[q // height])
    near_ref[...] = jnp.concatenate(near, axis=1)
    n = halo // 2
    adjoint_into(acc, g_high.at[:n], g_low.at[:n], EDGE // 2 - n, wa_high.at[0], wa_low.at[0])
    adjoint_into(acc, g_high.at[n:], g_low.at[n:], (EDGE + height) // 2, wa_high.at[1], wa_low.at[1])


def maps_kernel(
    ext_ref, side_ref, acc, near_ref, left, right, above, below, place, sa_high, sa_low, *rest, last,
):
    if last:
        (out_ref,) = rest
        height = out_ref.shape[1]
    else:
        (wf_high, wf_low, sf_high, sf_low, ext_out, side_out, b_ref, a2_high, a2_low, acc_b) = rest
        height = b_ref.shape[0]
    width = left.shape[1]
    ext_rows = height + EDGE
    side_in = jnp.concatenate([left[...], right[...], above[...], below[...], near_ref[...]], axis=1)
    side_high, side_low = split(side_in)
    half = sa_high.shape[1] // 2
    far = sa_high.shape[0] - 2 * width
    rim = mm_split(side_high[:, :far], side_low[:, :far], sa_high[:far, half:], sa_low[:far, half:])
    for a in range(ext_rows):
        if last and not RADIUS <= a < RADIUS + height:
            continue
        grad = add_rim(acc[a // 2, :, a % 2 * width : a % 2 * width + width], rim, a)
        row = jnp.maximum(ext_ref[a] - 0.5 * grad, 0.0)
        if last:
            out_ref[:, a - RADIUS, :] = row
            continue
        if a < RADIUS:
            row = jnp.where(place[UP] == 1, row, 0.0)
        elif a >= RADIUS + height:
            row = jnp.where(place[DOWN] == 1, row, 0.0)
        ext_out[a] = row
        put_pair(a2_high, a2_low, a, row)
    if last:
        return
    side_grad = mm_split(side_high, side_low, sa_high[:, :half], sa_low[:, :half])
    side = jnp.maximum(side_ref[...] - 0.5 * side_grad, 0.0)
    where = lanes(side.shape)
    a, c = where // EDGE, where % EDGE
    outside = (
        ((a < RADIUS) & (place[UP] == 0))
        | ((a >= RADIUS + height) & (place[DOWN] == 0))
        | ((c < RADIUS) & (place[LEFT] == 0))
        | ((c >= RADIUS) & (place[RIGHT] == 0))
        | (a >= ext_rows)
    )
    side = jnp.where(outside, 0.0, side)
    side_out[...] = side
    blur_into(b_ref, a2_high, a2_low, side, wf_high, wf_low, sf_high, sf_low, acc_b)


def spectra_kernel(mine, other, place, out_ref):
    channels, depth = out_ref.shape
    second = place[HALF] == 1
    first = jnp.where(second, other[...], mine[...])
    last = jnp.where(second, mine[...], other[...])
    parts = [first[:, :channels], first[:, channels:], last[:, :channels], last[:, channels:]]
    out_ref[...] = jnp.concatenate(parts, axis=0).T[:, :depth]


def call(kernel, micros, outs, scratch, specs, *args, aliases=None):
    return pl.pallas_call(
        kernel,
        out_shape=[jax.ShapeDtypeStruct(s, d) for s, d in outs],
        in_specs=specs,
        out_specs=[VMEM] * len(outs),
        scratch_shapes=[pltpu.VMEM(*s) if isinstance(s, tuple) else s for s in scratch],
        input_output_aliases=aliases or {},
        compiler_params=PARAMS,
        cost_estimate=pl.CostEstimate(
            flops=int(micros * 1.15e9), bytes_accessed=int(micros * 3.7e6), transcendentals=0
        ),
    )(*args)


def core_swap(x):
    count = lax.axis_size("cols")
    return lax.ppermute(x, "cols", [(i, i ^ 1) for i in range(count)])


def cross_swap(x):
    count = lax.axis_size("cols")
    return lax.ppermute(x, "cols", [(i, (i + 1 if i % 2 else i - 1) % count) for i in range(count)])


def pair_one(x):
    count = lax.axis_size("rows")
    return lax.ppermute(x, "rows", [(i, i ^ 1) for i in range(count)])


def pair_two(x):
    count = lax.axis_size("rows")
    return lax.ppermute(x, "rows", [(i, min(max(i + 1 if i % 2 else i - 1, 0), count - 1)) for i in range(count)])


def col_swap(x, mask):
    count = lax.axis_size("cols")
    return lax.ppermute(x, "cols", [(i, (((i + 1) % count ^ mask) - 1) % count) for i in range(count)])


def row_swap(x, mask):
    count = lax.axis_size("rows")
    return lax.ppermute(x, "rows", [(i, i ^ mask) for i in range(count)])


def on_device(observed, nonlin, abundance, spectra, kernels, tile_family):
    bands, height, width = observed.shape
    channels = abundance.shape[0]
    n_rows, n_cols = lax.axis_size("rows"), lax.axis_size("cols")
    row_at, col_at = lax.axis_index("rows"), lax.axis_index("cols")
    pixel_count = height * width * n_rows * n_cols
    quarter = -(-bands // 32) * 8
    full = 4 * quarter
    half_of = ((col_at + 1) // 2) % 2
    col_odd, row_odd = col_at % 2 == 1, row_at % 2 == 1
    place = jnp.stack(
        [row_at % 2, col_at % 2, row_at > 0, row_at < n_rows - 1, col_at > 0, col_at < n_cols - 1, half_of]
    ).astype(jnp.int32)
    has_left = (col_at > 0).astype(F32)
    has_right = (col_at < n_cols - 1).astype(F32)
    has_up = (row_at > 0).astype(F32)
    has_down = (row_at < n_rows - 1).astype(F32)
    table = jnp.transpose(kernels, (1, 0, 2))
    place, abundance, row_odd, col_odd, has_left, has_right, has_up, has_down = lax.optimization_barrier(
        (place, abundance, row_odd, col_odd, has_left, has_right, has_up, has_down)
    )
    tile = (channels, width)

    def sides(core, cross):
        left = jnp.where(col_odd, core, cross) * has_left
        right = jnp.where(col_odd, cross, core) * has_right
        lane = lanes(tile) < width // 2
        up_msg = jnp.where(lane, left, right)
        down_msg = jnp.where(lane, right, left)
        return left, right, jnp.where(row_odd, up_msg, down_msg), jnp.where(row_odd, down_msg, up_msg)

    a_rows, e_core, e_cross, mark = call(
        first_kernel,
        1,
        [((height,) + tile, F32), ((channels + 8, width), F32), ((channels + 8, width), F32), ((8, width), F32)],
        [],
        [SMEM, VMEM, SMEM],
        tile_family, abundance, place,
    )
    got_core = core_swap(e_core)
    got_cross = cross_swap(e_cross)
    left, right, side1, side2 = sides(got_core[:channels], got_cross[:channels])
    mark_left = jnp.where(col_odd, got_core[channels:], got_cross[channels:])
    mark_right = jnp.where(col_odd, got_cross[channels:], got_core[channels:])
    marks = jnp.concatenate([mark_left, mark, mark_right])
    top = a_rows[:RADIUS].reshape(RADIUS * channels, width)
    bottom = a_rows[height - RADIUS :].reshape(RADIUS * channels, width)
    got1 = pair_one(jnp.concatenate([jnp.where(row_odd, top, bottom), side1, marks]))
    got2 = pair_two(jnp.concatenate([jnp.where(row_odd, bottom, top), side2, marks]))
    body = RADIUS * channels

    def above_below(x1, x2):
        return jnp.where(row_odd, x1, x2), jnp.where(row_odd, x2, x1)

    above, below = above_below(got1[body : body + channels], got2[body : body + channels])
    above, below = above * has_up, below * has_down
    pairs = height // 2
    ext_rows = height + EDGE
    main_w = ((RADIUS + 1, 2 * width, 2 * width), BF16)
    side_f = ((2 * width, height * EDGE), BF16)
    hbm = pl.BlockSpec(memory_space=pltpu.HBM)
    half_shape = ((quarter, 2 * channels), F32)
    seen, mine, other, *wf = call(
        forward_weights_kernel,
        3,
        [((height, full, width), F32), half_shape, half_shape, main_w, main_w, side_f, side_f],
        [pltpu.SemaphoreType.DMA((height,))],
        [SMEM, SMEM, SMEM, hbm, VMEM],
        tile_family, table, place, observed, spectra.T,
    )
    got1, got2, seen, mine, other, *wf = lax.optimization_barrier((got1, got2, seen, mine, other, *wf))
    ext, side, blurred = call(
        start_kernel,
        2,
        [((ext_rows,) + tile, F32), ((channels, 2 * width), F32), ((height,) + tile, F32)],
        [((ext_rows // 2, channels, 2 * width), BF16)] * 2 + [((pairs, channels, 2 * width), F32)],
        [VMEM] * 7 + [SMEM] + [VMEM] * 4,
        a_rows, got1, got2, left, right, above, below, place, *wf,
    )
    marks_up, marks_down = above_below(got1[body + channels :], got2[body + channels :])
    main_a = ((2, RADIUS + 1, 2 * width, 2 * width), BF16)
    side_a = ((6 * width, 4 * width), BF16)

    def halo_weights(marks):
        return call(
            functools.partial(halo_weights_kernel, height=height, width=width),
            3,
            [main_a, main_a, side_a, side_a],
            [((6 * width, 4 * width), F32)],
            [VMEM, VMEM, VMEM, SMEM],
            marks_up, marks, marks_down, table,
        )

    rate = 40.0 / pixel_count
    acc_shape = ((ext_rows // 2, channels, 2 * width), F32)
    near_shape = ((channels, 2 * width), F32)

    def own_part(g_rows):
        return call(
            own_maps_kernel,
            2,
            [acc_shape, near_shape],
            [((pairs, channels, 2 * width), BF16)] * 2,
            [VMEM] * 3,
            g_rows, *w_own,
        )

    for step in range(ITERS):
        last = step == ITERS - 1
        halo = RADIUS if last else EDGE
        g_mine, to_core, main1, main2, e_cross, g_rows = call(
            functools.partial(spectral_kernel, scale=1.0 / channels),
            5,
            [
                ((quarter, 2 * channels), F32),
                ((quarter + channels, width), F32),
                ((halo,) + tile, F32),
                ((halo,) + tile, F32),
                (tile, F32),
                ((height,) + tile, F32),
            ],
            [((full, channels), F32)],
            [VMEM] * 5 + [SMEM],
            seen, nonlin, blurred, mine, other, place,
        )
        got_core = core_swap(to_core)
        p1 = pair_one(main1)
        share = g_mine + got_core[:quarter]
        main2, share = lax.optimization_barrier((main2, share))
        p2 = pair_two(main2)
        got_cross = cross_swap(jnp.concatenate([share, e_cross]))
        share = share + got_cross[:quarter]
        if step == 0:
            share, marks = lax.optimization_barrier((share, marks))
            wa = halo_weights(marks)
        else:
            share, g_rows = lax.optimization_barrier((share, g_rows))
            own, near = own_part(g_rows)
        left, right, side1, side2 = sides(got_core[quarter:], got_cross[quarter:])
        step_size = 4
        while step_size < n_cols:
            share = share + col_swap(share, step_size)
            step_size *= 2
        if step == 0:
            share, g_rows, marks, *wa = lax.optimization_barrier((share, g_rows, marks, *wa))
            w_own = call(own_weights_kernel, 1, [main_w, main_w], [], [VMEM, SMEM], marks, table)
            own, near = own_part(g_rows)
        else:
            share, own, near = lax.optimization_barrier((share, own, near))
        own, near = call(
            halo_maps_kernel,
            1.5,
            [acc_shape, near_shape],
            [((halo, channels, 2 * width), BF16)] * 2,
            [VMEM] * 4 + [SMEM] + [VMEM] * 2,
            own, near, p1, p2, place, wa[0], wa[1],
            aliases={0: 0, 1: 1},
        )
        got1 = pair_one(jnp.concatenate([share, side1]))
        if n_rows == 4:
            got2 = row_swap(jnp.concatenate([share, side2]), 3)
            got3 = row_swap(share, 2)
            got1, got2, own, near = lax.optimization_barrier((got1, got2, own, near))
            share = (share + got1[:quarter]) + (got3 + got2[:quarter])
            got2 = got2[quarter:]
        else:
            got2 = pair_two(side2)
            got1, got2, own, near = lax.optimization_barrier((got1, got2, own, near))
            share = share + got1[:quarter]
            step_size = 2
            while step_size < n_rows:
                share = share + row_swap(share, step_size)
                step_size *= 2
        above, below = above_below(got1[quarter:], got2)
        above, below = above * has_up, below * has_down
        gathered = (ext, side, own, near, left, right, above, below, place) + tuple(wa[2:])
        if last:
            made = call(
                functools.partial(maps_kernel, last=True),
                1.5,
                [((channels, height, width), F32)],
                [],
                [VMEM] * 8 + [SMEM] + [VMEM] * 2,
                *gathered,
            )
        else:
            made = call(
                functools.partial(maps_kernel, last=False),
                2.5,
                [((ext_rows,) + tile, F32), ((channels, 2 * width), F32), ((height,) + tile, F32)],
                [((ext_rows // 2, channels, 2 * width), BF16)] * 2 + [((pairs, channels, 2 * width), F32)],
                [VMEM] * 8 + [SMEM] + [VMEM] * 6,
                *gathered, *wf,
            )
        mine = jnp.maximum(mine - rate * share, 0.0)
        other = core_swap(mine)
        if last:
            (out,) = made
        else:
            ext, side, blurred = made
    (result,) = call(spectra_kernel, 1, [((channels, bands), F32)], [], [VMEM, VMEM, SMEM], mine, other, place)
    return out, result.T


def solution(mesh):
    placed = (
        P(None, "rows", "cols"),
        P("rows", "cols"),
        P(None, "rows", "cols"),
        P(),
        P(),
        P("rows", "cols"),
    )
    return jax.shard_map(
        on_device,
        mesh=mesh,
        in_specs=placed,
        out_specs=(P(None, "rows", "cols"), P()),
        check_vma=False,
    )
```

```python
import functools

import jax
import jax.numpy as jnp
import numpy as np
from jax import lax
from jax.experimental import pallas as pl
from jax.experimental.pallas import tpu as pltpu
from jax.sharding import PartitionSpec as P

KS = 9
RADIUS = KS // 2
EDGE = 2 * RADIUS
ITERS = 3
F32 = jnp.float32
BF16 = jnp.bfloat16
VMEM = pl.BlockSpec(memory_space=pltpu.VMEM)
SMEM = pl.BlockSpec(memory_space=pltpu.SMEM)
PARAMS = pltpu.CompilerParams(vmem_limit_bytes=18 * 1024 * 1024)
ROW_ODD, COL_ODD, UP, DOWN, LEFT, RIGHT, HALF = range(7)


def split(x):
    high = x.astype(BF16)
    return high, (x - high.astype(F32)).astype(BF16)


def mm(a, b):
    return jnp.dot(a, b, preferred_element_type=F32)


def mm_split(high, low, w_high, w_low):
    rows = high.shape[0]
    both = mm(jnp.concatenate([high, low], axis=0), w_high)
    return both[:rows] + both[rows:] + mm(high, w_low)


def mm_nt(a, b):
    return lax.dot_general(a, b, (((1,), (1,)), ((), ())), preferred_element_type=F32)


def lanes(shape):
    return lax.broadcasted_iota(jnp.int32, shape, len(shape) - 1)


def edges(rows, swapped):
    count = len(rows)
    lane = lanes(rows[0].shape)
    width = rows[0].shape[1]
    out = jnp.zeros_like(rows[0])
    for i, row in enumerate(rows):
        place = (i + count // 2) % count if swapped else i
        first = 0 if swapped else width - EDGE
        moved = pltpu.roll(row, (place * EDGE - first) % width, 1)
        out = jnp.where(lane // EDGE == place, moved, out)
    return out


def wide(x, total, shift):
    padded = jnp.concatenate([x, jnp.zeros((x.shape[0], total - x.shape[1]), x.dtype)], axis=1)
    return pltpu.roll(padded, shift % total, 1)


def assemble_side(left, right, above, below, height):
    total = 2 * left.shape[1]
    lane = lanes((left.shape[0], total))
    row, col = lane // EDGE, lane % EDGE
    on_left = col < RADIUS
    own = (row >= RADIUS) & (row < RADIUS + height)
    top = row < RADIUS
    bottom = (row >= RADIUS + height) & (row < 2 * RADIUS + height)
    half = EDGE * height // 2
    lo = RADIUS * EDGE - RADIUS
    hi = RADIUS * EDGE + RADIUS
    base = (RADIUS + height) * EDGE
    out = jnp.zeros((left.shape[0], total), F32)
    out = jnp.where(own & on_left, wide(left, total, lo), out)
    first = (row - RADIUS) < height // 2
    out = jnp.where(own & ~on_left & first, wide(right, total, hi - half), out)
    out = jnp.where(own & ~on_left & ~first, wide(right, total, hi + half), out)
    out = jnp.where(top & ~on_left, wide(above, total, RADIUS - RADIUS * EDGE), out)
    out = jnp.where(top & on_left, wide(above, total, -half - RADIUS * EDGE - RADIUS), out)
    out = jnp.where(bottom & on_left, wide(below, total, base - RADIUS), out)
    out = jnp.where(bottom & ~on_left, wide(below, total, base + RADIUS - half), out)
    return out


def add_rim(row, contrib, index):
    width = row.shape[1]
    start = index * EDGE
    part = contrib[:, start // width * width : start // width * width + width]
    moved = pltpu.roll(part, (-(start % width) - RADIUS) % width, 1)
    lane = lanes(row.shape)
    near = (lane < RADIUS) | (lane >= width - RADIUS)
    return row + jnp.where(near, moved, 0.0)


def first_kernel(family, a_ref, place, rows_ref, e_core, e_cross, mark_ref):
    channels, height, width = a_ref.shape
    rows = []
    for i in range(height):
        row = a_ref[:, i, :]
        rows_ref[i] = row
        rows.append(row)
    low, high = edges(rows, True), edges(rows, False)
    odd = place[COL_ODD] == 1
    e_core[:channels] = jnp.where(odd, low, high)
    e_cross[:channels] = jnp.where(odd, high, low)
    mark = jnp.full((8, width), family[0, 0].astype(F32), F32)
    e_core[channels:] = mark
    e_cross[channels:] = mark
    mark_ref[...] = mark


def band_sum(taps, delta):
    total = jnp.zeros(delta.shape, F32)
    for v in range(KS):
        total = jnp.where(delta == v, taps[v], total)
    return total


def build_main(taps, w_high, w_low, index, width):
    shape = (width, width)
    delta = lax.broadcasted_iota(jnp.int32, shape, 0) - lax.broadcasted_iota(jnp.int32, shape, 1) + RADIUS
    blank = jnp.zeros(shape, BF16)
    for u in range(-1, KS + 1):
        if 0 <= u < KS:
            high, low = split(band_sum([taps(u, v) for v in range(KS)], delta))
        else:
            high, low = blank, blank
        for r in range(2):
            for ro in range(2):
                if (u + ro - r) % 2 == 0:
                    d = (u + ro - r) // 2
                    if 0 <= d <= RADIUS:
                        at = index + (d, slice(r * width, r * width + width), slice(ro * width, ro * width + width))
                        w_high[at] = high
                        w_low[at] = low


def rim_column(lane, width):
    c = lane % EDGE
    return jnp.where(c < RADIUS, width - RADIUS + c, c - RADIUS)


def side_column(lane, width):
    c = lane % EDGE
    return jnp.where(c < RADIUS, c - RADIUS, width + c - RADIUS)


def forward_weights_kernel(family, table, place, obs_ref, spectra_ref, seen_ref, mine, other, w_high, w_low, s_high, s_low, sems):
    depth, height, width = obs_ref.shape
    copies = []
    for i in range(height):
        copies.append(pltpu.make_async_copy(obs_ref.at[:, i, :], seen_ref.at[i, pl.ds(0, depth), :], sems.at[i]))
        copies[-1].start()
    start = depth // 8 * 8
    channels = spectra_ref.shape[0]
    quarter = seen_ref.shape[1] // 4
    total = -(-seen_ref.shape[1] // 128) * 128
    spectra = jnp.concatenate([spectra_ref[...], jnp.zeros((channels, total - depth), F32)], axis=1).T
    halves = [
        jnp.concatenate([spectra[q * quarter : (q + 1) * quarter], spectra[(q + 1) * quarter : (q + 2) * quarter]], axis=1)
        for q in (0, 2)
    ]
    second = place[HALF] == 1
    mine[...] = jnp.where(second, halves[1], halves[0])
    other[...] = jnp.where(second, halves[0], halves[1])
    own = lambda u, v: table[u, family[0, 0], v]
    build_main(own, w_high, w_low, (), width)
    n = height * EDGE
    shape = (EDGE, n)
    lane = lanes(shape)
    c = lax.broadcasted_iota(jnp.int32, shape, 0)
    delta = side_column(c, width) - rim_column(lane, width) + RADIUS
    out_row = lane // EDGE
    bands = [band_sum([own(u, v) for v in range(KS)], delta) for u in range(KS)]
    rows = s_high.shape[0] // EDGE
    for a in range(0, rows, 2):
        blocks = []
        for b in (a, a + 1):
            total = jnp.zeros(shape, F32)
            for u in range(KS):
                total = jnp.where(out_row == b - u, bands[u], total)
            blocks.append(total)
        high, low = split(jnp.concatenate(blocks, axis=0))
        s_high[a * EDGE : a * EDGE + 2 * EDGE] = high
        s_low[a * EDGE : a * EDGE + 2 * EDGE] = low
    for i in range(height):
        copies[i].wait()
    sub = lax.broadcasted_iota(jnp.int32, (seen_ref.shape[1] - start, width), 0)
    for i in range(height):
        seen_ref[i, start:] = jnp.where(sub < depth - start, seen_ref[i, start:], 0.0)


def flipped(table, family):
    return lambda u, v: table[KS - 1 - u, family, KS - 1 - v]


def own_weights_kernel(marks, table, w_high, w_low):
    family = jnp.max(marks[8:16]).astype(jnp.int32)
    build_main(flipped(table, family), w_high, w_low, (), w_high.shape[1] // 2)


def halo_weights_kernel(
    marks_up, marks, marks_down, table, w_high, w_low, s_high, s_low, scratch, *, height, width
):
    families = []
    for ref in (marks_up, marks, marks_down):
        for k in range(3):
            families.append(jnp.max(ref[8 * k : 8 * k + 8]).astype(jnp.int32))
    for b in range(2):
        build_main(flipped(table, families[6 * b + 1]), w_high, w_low, (b,), width)
    n = s_high.shape[1]
    half = n // 2
    shape = (EDGE, n)
    lane = lanes(shape)
    c = lax.broadcasted_iota(jnp.int32, shape, 0)
    to_side = lane < half
    column = jnp.where(to_side, side_column(lane, width), rim_column(lane, width))
    out_row = jnp.where(to_side, lane, lane - half) // EDGE
    out_row = jnp.where(out_row < height + EDGE, out_row, -KS - 1)
    sources = (c - EDGE, width + c, rim_column(c, width))
    chunk = height * EDGE
    mid = chunk // 2

    def place_of(kind, q):
        i = q - EDGE
        if kind == 2:
            return 4 * chunk + q * EDGE
        if 0 <= i < height:
            return i * EDGE if kind == 0 else chunk + (i + height // 2) % height * EDGE
        if i < 0:
            return 2 * chunk + (mid if kind == 0 else 0) + q * EDGE
        return 3 * chunk + (0 if kind == 0 else mid) + (i - height) * EDGE

    for kind in range(3):
        delta = sources[kind] - column + RADIUS
        if kind == 2:
            delta = jnp.where(to_side, delta, -1)
        for b in range(3):
            tile = 3 * b + (0, 2, 1)[kind]
            bands = [
                band_sum([table[KS - 1 - u, families[tile], KS - 1 - v] for v in range(KS)], delta) for u in range(KS)
            ]
            q_range = (range(0, EDGE), range(EDGE, EDGE + height), range(EDGE + height, 2 * EDGE + height))[b]
            for q in q_range:
                total = jnp.zeros(shape, F32)
                for u in range(KS):
                    if 0 <= q - u < height + EDGE:
                        total = jnp.where(out_row == q - u, bands[u], total)
                at = place_of(kind, q)
                scratch[at : at + EDGE] = total
    for start in range(0, scratch.shape[0], 64):
        high, low = split(scratch[start : start + 64])
        s_high[start : start + 64] = high
        s_low[start : start + 64] = low


def blur_into(b_ref, a2_high, a2_low, side, w_high, w_low, s_high, s_low, acc):
    pairs, channels, double = acc.shape
    width = double // 2
    for d in range(RADIUS + 1):
        high = a2_high[d : d + pairs].reshape(pairs * channels, double)
        low = a2_low[d : d + pairs].reshape(pairs * channels, double)
        part = mm_split(high, low, w_high[d], w_low[d])
        part = part.reshape(pairs, channels, double)
        if d == 0:
            acc[...] = part
        else:
            acc[...] += part
    side_high, side_low = split(side)
    rim = mm_split(side_high, side_low, s_high[...], s_low[...])
    for i in range(2 * pairs):
        row = acc[i // 2, :, i % 2 * width : i % 2 * width + width]
        b_ref[i] = add_rim(row, rim, i)


def start_kernel(
    rows_ref, p1, p2, left, right, above, below, place, w_high, w_low, s_high, s_low,
    ext_ref, side_ref, b_ref, a2_high, a2_low, acc,
):
    height, channels, width = rows_ref.shape
    odd = place[ROW_ODD] == 1
    for a in range(height + EDGE):
        if a < RADIUS:
            row = jnp.where(odd, p1[a * channels : a * channels + channels], p2[a * channels : a * channels + channels])
            row = jnp.where(place[UP] == 1, row, 0.0)
        elif a < RADIUS + height:
            row = rows_ref[a - RADIUS]
        else:
            k = (a - RADIUS - height) * channels
            row = jnp.where(odd, p2[k : k + channels], p1[k : k + channels])
            row = jnp.where(place[DOWN] == 1, row, 0.0)
        ext_ref[a] = row
        high, low = split(row)
        a2_high[a // 2, :, a % 2 * width : a % 2 * width + width] = high
        a2_low[a // 2, :, a % 2 * width : a % 2 * width + width] = low
    side = assemble_side(left[...], right[...], above[...], below[...], height)
    side_ref[...] = side
    blur_into(b_ref, a2_high, a2_low, side, w_high, w_low, s_high, s_low, acc)


def spectral_kernel(
    obs_ref, bend_ref, b_ref, mine, other, place,
    g_mine, core_ref, main1, main2, cross_ref, rows_ref,
    total, *, scale,
):
    height, channels, width = b_ref.shape
    bands = obs_ref.shape[1]
    quarter = bands // 4
    second = place[HALF] == 1
    m0 = jnp.where(second, other[...], mine[...])
    m1 = jnp.where(second, mine[...], other[...])
    spectra = jnp.concatenate([m0[:, :channels], m0[:, channels:], m1[:, :channels], m1[:, channels:]], axis=0)
    m_high, m_low = split(spectra)
    m_cat = jnp.concatenate([m_high, m_low, m_high], axis=1)
    t_high, t_low = split(spectra.T)
    t_cat = jnp.concatenate([t_high, t_low], axis=0)
    rows = []
    for pair in range(height // 2):
        b_pair = jnp.concatenate([b_ref[2 * pair], b_ref[2 * pair + 1]], axis=1)
        b_high, b_low = split(b_pair)
        b_cat = jnp.concatenate([b_high, b_high, b_low], axis=0)
        linear = mm(m_cat, b_cat) * scale
        seen = jnp.concatenate([obs_ref[2 * pair], obs_ref[2 * pair + 1]], axis=1)
        bend = jnp.concatenate([bend_ref[2 * pair : 2 * pair + 1], bend_ref[2 * pair + 1 : 2 * pair + 2]], axis=1)
        bent = bend * linear
        resid = linear + bent * linear - seen
        weighted = resid * (1.0 + 2.0 * bent)
        w_high, w_low = split(weighted)
        part = mm_nt(w_high, jnp.concatenate([b_high, b_low], axis=0))
        part = part[:, :channels] + part[:, channels:] + mm_nt(w_low, b_high)
        if pair == 0:
            total[...] = part
        else:
            total[...] += part
        both = mm(t_cat, w_high)
        grad = (both[:channels] + both[channels:] + mm(t_high, w_low)) * scale
        for k in range(2):
            row = grad[:, k * width : k * width + width]
            rows_ref[2 * pair + k] = row
            rows.append(row)
    low, high = edges(rows, True), edges(rows, False)
    col_odd = place[COL_ODD] == 1
    core_ref[2 * quarter // 2 :] = jnp.where(col_odd, low, high)
    cross_ref[...] = jnp.where(col_odd, high, low)
    row_odd = place[ROW_ODD] == 1
    halo = main1.shape[0]
    for i in range(halo):
        main1[i] = jnp.where(row_odd, rows[i], rows[height - halo + i])
        main2[i] = jnp.where(row_odd, rows[height - halo + i], rows[i])
    g = total[...] * scale
    g0 = jnp.concatenate([g[:quarter], g[quarter : 2 * quarter]], axis=1)
    g1 = jnp.concatenate([g[2 * quarter : 3 * quarter], g[3 * quarter :]], axis=1)
    g_mine[...] = jnp.where(second, g1, g0)
    core_ref[:quarter] = jnp.where(second, g0, g1)


def put_pair(high_ref, low_ref, index, row):
    width = row.shape[1]
    at = (index // 2, slice(None), slice(index % 2 * width, index % 2 * width + width))
    high_ref[at], low_ref[at] = split(row)


def adjoint_into(acc, g_high, g_low, first, w_high, w_low):
    pairs, channels, double = g_high.shape
    for d in range(RADIUS + 1):
        begin, end = max(first, d), min(first + pairs, acc.shape[0] + d)
        if begin >= end:
            continue
        high = g_high[begin - first : end - first].reshape((end - begin) * channels, double)
        low = g_low[begin - first : end - first].reshape((end - begin) * channels, double)
        part = mm_split(high, low, w_high[d], w_low[d])
        acc[begin - d : end - d] += part.reshape(end - begin, channels, double)


def own_maps_kernel(rows_ref, wa_high, wa_low, acc, near_ref, g_high, g_low):
    height, channels, width = rows_ref.shape
    lane = lanes((channels, width))
    near = [jnp.zeros((channels, width), F32) for _ in range(2)]
    for i in range(height):
        row = rows_ref[i]
        put_pair(g_high, g_low, i, row)
        q = i + EDGE
        moved = pltpu.roll(row, (RADIUS + q * EDGE) % width, 1)
        near[q // height] = jnp.where(lane // EDGE == q % height, moved, near[q // height])
    near_ref[...] = jnp.concatenate(near, axis=1)
    acc[...] = jnp.zeros_like(acc)
    adjoint_into(acc, g_high, g_low, EDGE // 2, wa_high, wa_low)


def halo_maps_kernel(acc_in, near_in, p1, p2, place, wa_high, wa_low, acc, near_ref, g_high, g_low):
    channels = near_in.shape[0]
    width = near_in.shape[1] // 2
    height = 2 * acc.shape[0] - EDGE
    odd = place[ROW_ODD] == 1
    lane = lanes((channels, width))
    near = [near_in[:, :width], near_in[:, width:]]
    halo = p1.shape[0]
    for k in range(2 * halo):
        if k < halo:
            q = EDGE - halo + k
            row = jnp.where(place[UP] == 1, jnp.where(odd, p1[k], p2[k]), 0.0)
        else:
            q = EDGE + height + k - halo
            row = jnp.where(place[DOWN] == 1, jnp.where(odd, p2[k - halo], p1[k - halo]), 0.0)
        put_pair(g_high, g_low, k, row)
        moved = pltpu.roll(row, (RADIUS + q * EDGE) % width, 1)
        near[q // height] = jnp.where(lane // EDGE == q % height, moved, near[q // height])
    near_ref[...] = jnp.concatenate(near, axis=1)
    n = halo // 2
    adjoint_into(acc, g_high.at[:n], g_low.at[:n], EDGE // 2 - n, wa_high.at[0], wa_low.at[0])
    adjoint_into(acc, g_high.at[n:], g_low.at[n:], (EDGE + height) // 2, wa_high.at[1], wa_low.at[1])


def maps_kernel(
    ext_ref, side_ref, acc, near_ref, left, right, above, below, place, sa_high, sa_low, *rest, last,
):
    if last:
        (out_ref,) = rest
        height = out_ref.shape[1]
    else:
        (wf_high, wf_low, sf_high, sf_low, ext_out, side_out, b_ref, a2_high, a2_low, acc_b) = rest
        height = b_ref.shape[0]
    width = left.shape[1]
    ext_rows = height + EDGE
    side_in = jnp.concatenate([left[...], right[...], above[...], below[...], near_ref[...]], axis=1)
    side_high, side_low = split(side_in)
    half = sa_high.shape[1] // 2
    far = sa_high.shape[0] - 2 * width
    rim = mm_split(side_high[:, :far], side_low[:, :far], sa_high[:far, half:], sa_low[:far, half:])
    for a in range(ext_rows):
        if last and not RADIUS <= a < RADIUS + height:
            continue
        grad = add_rim(acc[a // 2, :, a % 2 * width : a % 2 * width + width], rim, a)
        row = jnp.maximum(ext_ref[a] - 0.5 * grad, 0.0)
        if last:
            out_ref[:, a - RADIUS, :] = row
            continue
        if a < RADIUS:
            row = jnp.where(place[UP] == 1, row, 0.0)
        elif a >= RADIUS + height:
            row = jnp.where(place[DOWN] == 1, row, 0.0)
        ext_out[a] = row
        put_pair(a2_high, a2_low, a, row)
    if last:
        return
    side_grad = mm_split(side_high, side_low, sa_high[:, :half], sa_low[:, :half])
    side = jnp.maximum(side_ref[...] - 0.5 * side_grad, 0.0)
    where = lanes(side.shape)
    a, c = where // EDGE, where % EDGE
    outside = (
        ((a < RADIUS) & (place[UP] == 0))
        | ((a >= RADIUS + height) & (place[DOWN] == 0))
        | ((c < RADIUS) & (place[LEFT] == 0))
        | ((c >= RADIUS) & (place[RIGHT] == 0))
        | (a >= ext_rows)
    )
    side = jnp.where(outside, 0.0, side)
    side_out[...] = side
    blur_into(b_ref, a2_high, a2_low, side, wf_high, wf_low, sf_high, sf_low, acc_b)


def turn_kernel(half_ref, out_ref):
    channels, width = out_ref.shape
    half = jnp.concatenate([half_ref[:, :channels], half_ref[:, channels:]], axis=0)
    rest = jnp.zeros((width - half.shape[0], channels), F32)
    out_ref[...] = jnp.concatenate([half, rest], axis=0).T


def call(kernel, micros, outs, scratch, specs, *args, aliases=None):
    return pl.pallas_call(
        kernel,
        out_shape=[jax.ShapeDtypeStruct(s, d) for s, d in outs],
        in_specs=specs,
        out_specs=[VMEM] * len(outs),
        scratch_shapes=[pltpu.VMEM(*s) if isinstance(s, tuple) else s for s in scratch],
        input_output_aliases=aliases or {},
        compiler_params=PARAMS,
        cost_estimate=pl.CostEstimate(
            flops=int(micros * 1.15e9), bytes_accessed=int(micros * 3.7e6), transcendentals=0
        ),
    )(*args)


def core_swap(x):
    count = lax.axis_size("cols")
    return lax.ppermute(x, "cols", [(i, i ^ 1) for i in range(count)])


def cross_swap(x):
    count = lax.axis_size("cols")
    return lax.ppermute(x, "cols", [(i, (i + 1 if i % 2 else i - 1) % count) for i in range(count)])


def pair_one(x):
    count = lax.axis_size("rows")
    return lax.ppermute(x, "rows", [(i, i ^ 1) for i in range(count)])


def pair_two(x):
    count = lax.axis_size("rows")
    return lax.ppermute(x, "rows", [(i, min(max(i + 1 if i % 2 else i - 1, 0), count - 1)) for i in range(count)])


def col_swap(x, mask):
    count = lax.axis_size("cols")
    return lax.ppermute(x, "cols", [(i, (((i + 1) % count ^ mask) - 1) % count) for i in range(count)])


def row_swap(x, mask):
    count = lax.axis_size("rows")
    return lax.ppermute(x, "rows", [(i, i ^ mask) for i in range(count)])


def on_device(observed, nonlin, abundance, spectra, kernels, tile_family):
    bands, height, width = observed.shape
    channels = abundance.shape[0]
    n_rows, n_cols = lax.axis_size("rows"), lax.axis_size("cols")
    row_at, col_at = lax.axis_index("rows"), lax.axis_index("cols")
    pixel_count = height * width * n_rows * n_cols
    quarter = -(-bands // 32) * 8
    full = 4 * quarter
    half_of = ((col_at + 1) // 2) % 2
    col_odd, row_odd = col_at % 2 == 1, row_at % 2 == 1
    place = jnp.stack(
        [row_at % 2, col_at % 2, row_at > 0, row_at < n_rows - 1, col_at > 0, col_at < n_cols - 1, half_of]
    ).astype(jnp.int32)
    has_left = (col_at > 0).astype(F32)
    has_right = (col_at < n_cols - 1).astype(F32)
    has_up = (row_at > 0).astype(F32)
    has_down = (row_at < n_rows - 1).astype(F32)
    table = jnp.transpose(kernels, (1, 0, 2))
    second_half = half_of == 1
    place, abundance, second_half, row_odd, col_odd, has_left, has_right, has_up, has_down = lax.optimization_barrier(
        (place, abundance, second_half, row_odd, col_odd, has_left, has_right, has_up, has_down)
    )
    tile = (channels, width)

    def sides(core, cross):
        left = jnp.where(col_odd, core, cross) * has_left
        right = jnp.where(col_odd, cross, core) * has_right
        lane = lanes(tile) < width // 2
        up_msg = jnp.where(lane, left, right)
        down_msg = jnp.where(lane, right, left)
        return left, right, jnp.where(row_odd, up_msg, down_msg), jnp.where(row_odd, down_msg, up_msg)

    a_rows, e_core, e_cross, mark = call(
        first_kernel,
        1,
        [((height,) + tile, F32), ((channels + 8, width), F32), ((channels + 8, width), F32), ((8, width), F32)],
        [],
        [SMEM, VMEM, SMEM],
        tile_family, abundance, place,
    )
    got_core = core_swap(e_core)
    got_cross = cross_swap(e_cross)
    left, right, side1, side2 = sides(got_core[:channels], got_cross[:channels])
    mark_left = jnp.where(col_odd, got_core[channels:], got_cross[channels:])
    mark_right = jnp.where(col_odd, got_cross[channels:], got_core[channels:])
    marks = jnp.concatenate([mark_left, mark, mark_right])
    top = a_rows[:RADIUS].reshape(RADIUS * channels, width)
    bottom = a_rows[height - RADIUS :].reshape(RADIUS * channels, width)
    got1 = pair_one(jnp.concatenate([jnp.where(row_odd, top, bottom), side1, marks]))
    got2 = pair_two(jnp.concatenate([jnp.where(row_odd, bottom, top), side2, marks]))
    body = RADIUS * channels

    def above_below(x1, x2):
        return jnp.where(row_odd, x1, x2), jnp.where(row_odd, x2, x1)

    above, below = above_below(got1[body : body + channels], got2[body : body + channels])
    above, below = above * has_up, below * has_down
    pairs = height // 2
    ext_rows = height + EDGE
    main_w = ((RADIUS + 1, 2 * width, 2 * width), BF16)
    side_f = ((2 * width, height * EDGE), BF16)
    hbm = pl.BlockSpec(memory_space=pltpu.HBM)
    half_shape = ((quarter, 2 * channels), F32)
    seen, mine, other, *wf = call(
        forward_weights_kernel,
        3,
        [((height, full, width), F32), half_shape, half_shape, main_w, main_w, side_f, side_f],
        [pltpu.SemaphoreType.DMA((height,))],
        [SMEM, SMEM, SMEM, hbm, VMEM],
        tile_family, table, place, observed, spectra.T,
    )
    got1, got2, seen, mine, other, *wf = lax.optimization_barrier((got1, got2, seen, mine, other, *wf))
    ext, side, blurred = call(
        start_kernel,
        2,
        [((ext_rows,) + tile, F32), ((channels, 2 * width), F32), ((height,) + tile, F32)],
        [((ext_rows // 2, channels, 2 * width), BF16)] * 2 + [((pairs, channels, 2 * width), F32)],
        [VMEM] * 7 + [SMEM] + [VMEM] * 4,
        a_rows, got1, got2, left, right, above, below, place, *wf,
    )
    marks_up, marks_down = above_below(got1[body + channels :], got2[body + channels :])
    main_a = ((2, RADIUS + 1, 2 * width, 2 * width), BF16)
    side_a = ((6 * width, 4 * width), BF16)

    def halo_weights(marks):
        return call(
            functools.partial(halo_weights_kernel, height=height, width=width),
            3,
            [main_a, main_a, side_a, side_a],
            [((6 * width, 4 * width), F32)],
            [VMEM, VMEM, VMEM, SMEM],
            marks_up, marks, marks_down, table,
        )

    rate = 40.0 / pixel_count
    acc_shape = ((ext_rows // 2, channels, 2 * width), F32)
    near_shape = ((channels, 2 * width), F32)

    def own_part(g_rows):
        return call(
            own_maps_kernel,
            2,
            [acc_shape, near_shape],
            [((pairs, channels, 2 * width), BF16)] * 2,
            [VMEM] * 3,
            g_rows, *w_own,
        )

    for step in range(ITERS):
        last = step == ITERS - 1
        halo = RADIUS if last else EDGE
        g_mine, to_core, main1, main2, e_cross, g_rows = call(
            functools.partial(spectral_kernel, scale=1.0 / channels),
            5,
            [
                ((quarter, 2 * channels), F32),
                ((quarter + channels, width), F32),
                ((halo,) + tile, F32),
                ((halo,) + tile, F32),
                (tile, F32),
                ((height,) + tile, F32),
            ],
            [((full, channels), F32)],
            [VMEM] * 5 + [SMEM],
            seen, nonlin, blurred, mine, other, place,
        )
        got_core = core_swap(to_core)
        p1 = pair_one(main1)
        share = g_mine + got_core[:quarter]
        main2, share = lax.optimization_barrier((main2, share))
        p2 = pair_two(main2)
        message = jnp.concatenate([share, e_cross])
        got_cross = cross_swap(message)
        at_once = last and n_cols >= 8
        if at_once:
            got_four = col_swap(message, 4)
            got_five = col_swap(message, 5)
            share = (share + got_cross[:quarter]) + (got_four[:quarter] + got_five[:quarter])
        else:
            share = share + got_cross[:quarter]
        if step == 0:
            share, marks = lax.optimization_barrier((share, marks))
            wa = halo_weights(marks)
        else:
            share, g_rows = lax.optimization_barrier((share, g_rows))
            own, near = own_part(g_rows)
        left, right, side1, side2 = sides(got_core[quarter:], got_cross[quarter:])
        step_size = 8 if at_once else 4
        while step_size < n_cols:
            share = share + col_swap(share, step_size)
            step_size *= 2
        if step == 0:
            share, *wa = lax.optimization_barrier((share, *wa))
            got1 = pair_one(jnp.concatenate([share, side1]))
            g_rows, marks, p1 = lax.optimization_barrier((g_rows, marks, p1))
            got1, p2 = lax.optimization_barrier((got1, p2))
            w_own = call(own_weights_kernel, 1, [main_w, main_w], [], [VMEM, SMEM], marks, table)
            own, near = own_part(g_rows)
        else:
            if not at_once:
                share, own, near = lax.optimization_barrier((share, own, near))
            got1 = pair_one(jnp.concatenate([share, side1]))
        own, near = call(
            halo_maps_kernel,
            1.5,
            [acc_shape, near_shape],
            [((halo, channels, 2 * width), BF16)] * 2,
            [VMEM] * 4 + [SMEM] + [VMEM] * 2,
            own, near, p1, p2, place, wa[0], wa[1],
            aliases={0: 0, 1: 1},
        )
        if n_rows == 4:
            got2 = row_swap(jnp.concatenate([share, side2]), 3)
            got3 = row_swap(share, 2)
            got1, got2, own, near = lax.optimization_barrier((got1, got2, own, near))
            share = (share + got1[:quarter]) + (got3 + got2[:quarter])
            got2 = got2[quarter:]
        else:
            got2 = pair_two(side2)
            got1, got2, own, near = lax.optimization_barrier((got1, got2, own, near))
            share = share + got1[:quarter]
            step_size = 2
            while step_size < n_rows:
                share = share + row_swap(share, step_size)
                step_size *= 2
        above, below = above_below(got1[quarter:], got2)
        above, below = above * has_up, below * has_down
        gathered = (ext, side, own, near, left, right, above, below, place) + tuple(wa[2:])
        if last:
            made = call(
                functools.partial(maps_kernel, last=True),
                1.5,
                [((channels, height, width), F32)],
                [],
                [VMEM] * 8 + [SMEM] + [VMEM] * 2,
                *gathered,
            )
        else:
            made = call(
                functools.partial(maps_kernel, last=False),
                2.5,
                [((ext_rows,) + tile, F32), ((channels, 2 * width), F32), ((height,) + tile, F32)],
                [((ext_rows // 2, channels, 2 * width), BF16)] * 2 + [((pairs, channels, 2 * width), F32)],
                [VMEM] * 8 + [SMEM] + [VMEM] * 6,
                *gathered, *wf,
            )
        mine = jnp.maximum(mine - rate * share, 0.0)
        if last:
            (out,) = made
            (mine,) = call(turn_kernel, 0.5, [((channels, -(-2 * quarter // 128) * 128), F32)], [], [VMEM], mine)
        other = core_swap(mine)
        if not last:
            ext, side, blurred = made
    low = jnp.where(second_half, other, mine)[:, : 2 * quarter]
    high = jnp.where(second_half, mine, other)[:, : bands - 2 * quarter]
    return out, jnp.concatenate([low, high], axis=1).T


def solution(mesh):
    placed = (
        P(None, "rows", "cols"),
        P("rows", "cols"),
        P(None, "rows", "cols"),
        P(),
        P(),
        P("rows", "cols"),
    )
    return jax.shard_map(
        on_device,
        mesh=mesh,
        in_specs=placed,
        out_specs=(P(None, "rows", "cols"), P()),
        check_vma=False,
    )
```

```python
import functools

import jax
import jax.numpy as jnp
import numpy as np
from jax import lax
from jax.experimental import pallas as pl
from jax.experimental.pallas import tpu as pltpu
from jax.sharding import PartitionSpec as P

KS = 9
RADIUS = KS // 2
EDGE = 2 * RADIUS
ITERS = 3
F32 = jnp.float32
BF16 = jnp.bfloat16
VMEM = pl.BlockSpec(memory_space=pltpu.VMEM)
SMEM = pl.BlockSpec(memory_space=pltpu.SMEM)
PARAMS = pltpu.CompilerParams(vmem_limit_bytes=18 * 1024 * 1024)
ROW_ODD, COL_ODD, UP, DOWN, LEFT, RIGHT, HALF = range(7)


def split(x):
    high = x.astype(BF16)
    return high, (x - high.astype(F32)).astype(BF16)


def mm(a, b):
    return jnp.dot(a, b, preferred_element_type=F32)


def mm_split(high, low, w_high, w_low):
    rows = high.shape[0]
    both = mm(jnp.concatenate([high, low], axis=0), w_high)
    return both[:rows] + both[rows:] + mm(high, w_low)


def mm_nt(a, b):
    return lax.dot_general(a, b, (((1,), (1,)), ((), ())), preferred_element_type=F32)


def lanes(shape):
    return lax.broadcasted_iota(jnp.int32, shape, len(shape) - 1)


def edges(rows, swapped):
    count = len(rows)
    lane = lanes(rows[0].shape)
    width = rows[0].shape[1]
    out = jnp.zeros_like(rows[0])
    for i, row in enumerate(rows):
        place = (i + count // 2) % count if swapped else i
        first = 0 if swapped else width - EDGE
        moved = pltpu.roll(row, (place * EDGE - first) % width, 1)
        out = jnp.where(lane // EDGE == place, moved, out)
    return out


def wide(x, total, shift):
    padded = jnp.concatenate([x, jnp.zeros((x.shape[0], total - x.shape[1]), x.dtype)], axis=1)
    return pltpu.roll(padded, shift % total, 1)


def assemble_side(left, right, above, below, height):
    total = 2 * left.shape[1]
    lane = lanes((left.shape[0], total))
    row, col = lane // EDGE, lane % EDGE
    on_left = col < RADIUS
    own = (row >= RADIUS) & (row < RADIUS + height)
    top = row < RADIUS
    bottom = (row >= RADIUS + height) & (row < 2 * RADIUS + height)
    half = EDGE * height // 2
    lo = RADIUS * EDGE - RADIUS
    hi = RADIUS * EDGE + RADIUS
    base = (RADIUS + height) * EDGE
    out = jnp.zeros((left.shape[0], total), F32)
    out = jnp.where(own & on_left, wide(left, total, lo), out)
    first = (row - RADIUS) < height // 2
    out = jnp.where(own & ~on_left & first, wide(right, total, hi - half), out)
    out = jnp.where(own & ~on_left & ~first, wide(right, total, hi + half), out)
    out = jnp.where(top & ~on_left, wide(above, total, RADIUS - RADIUS * EDGE), out)
    out = jnp.where(top & on_left, wide(above, total, -half - RADIUS * EDGE - RADIUS), out)
    out = jnp.where(bottom & on_left, wide(below, total, base - RADIUS), out)
    out = jnp.where(bottom & ~on_left, wide(below, total, base + RADIUS - half), out)
    return out


def add_rim(row, contrib, index):
    width = row.shape[1]
    start = index * EDGE
    part = contrib[:, start // width * width : start // width * width + width]
    moved = pltpu.roll(part, (-(start % width) - RADIUS) % width, 1)
    lane = lanes(row.shape)
    near = (lane < RADIUS) | (lane >= width - RADIUS)
    return row + jnp.where(near, moved, 0.0)


def first_kernel(family, a_ref, place, rows_ref, e_core, e_cross, mark_ref):
    channels, height, width = a_ref.shape
    rows = []
    for i in range(height):
        row = a_ref[:, i, :]
        rows_ref[i] = row
        rows.append(row)
    low, high = edges(rows, True), edges(rows, False)
    odd = place[COL_ODD] == 1
    e_core[:channels] = jnp.where(odd, low, high)
    e_cross[:channels] = jnp.where(odd, high, low)
    mark = jnp.full((8, width), family[0, 0].astype(F32), F32)
    e_core[channels:] = mark
    e_cross[channels:] = mark
    mark_ref[...] = mark


def band_sum(taps, delta):
    total = jnp.zeros(delta.shape, F32)
    for v in range(KS):
        total = jnp.where(delta == v, taps[v], total)
    return total


def toeplitz(taps, delta):
    height, width = delta.shape
    lane = lanes((8, width))
    line = jnp.zeros((8, width), F32)
    for v in range(KS):
        line = jnp.where(lane == (RADIUS - v) % width, taps[v], line)
    rolled = pltpu.roll(jnp.concatenate([line] * (height // 8), axis=0), 0, 1, stride=1, stride_axis=0)
    return jnp.where((delta >= 0) & (delta < KS), rolled, 0.0)


def build_main(taps, w_high, w_low, index, width):
    shape = (width, width)
    delta = lax.broadcasted_iota(jnp.int32, shape, 0) - lax.broadcasted_iota(jnp.int32, shape, 1) + RADIUS
    blank = jnp.zeros(shape, BF16)
    for u in range(-1, KS + 1):
        if 0 <= u < KS:
            high, low = split(toeplitz([taps(u, v) for v in range(KS)], delta))
        else:
            high, low = blank, blank
        for r in range(2):
            for ro in range(2):
                if (u + ro - r) % 2 == 0:
                    d = (u + ro - r) // 2
                    if 0 <= d <= RADIUS:
                        at = index + (d, slice(r * width, r * width + width), slice(ro * width, ro * width + width))
                        w_high[at] = high
                        w_low[at] = low


def rim_column(lane, width):
    c = lane % EDGE
    return jnp.where(c < RADIUS, width - RADIUS + c, c - RADIUS)


def side_column(lane, width):
    c = lane % EDGE
    return jnp.where(c < RADIUS, c - RADIUS, width + c - RADIUS)


def forward_weights_kernel(family, table, place, obs_ref, spectra_ref, seen_ref, mine, other, w_high, w_low, s_high, s_low, sems):
    depth, height, width = obs_ref.shape
    copies = []
    for i in range(height):
        copies.append(pltpu.make_async_copy(obs_ref.at[:, i, :], seen_ref.at[i, pl.ds(0, depth), :], sems.at[i]))
        copies[-1].start()
    start = depth // 8 * 8
    channels = spectra_ref.shape[0]
    quarter = seen_ref.shape[1] // 4
    total = -(-seen_ref.shape[1] // 128) * 128
    spectra = jnp.concatenate([spectra_ref[...], jnp.zeros((channels, total - depth), F32)], axis=1).T
    halves = [
        jnp.concatenate([spectra[q * quarter : (q + 1) * quarter], spectra[(q + 1) * quarter : (q + 2) * quarter]], axis=1)
        for q in (0, 2)
    ]
    second = place[HALF] == 1
    mine[...] = jnp.where(second, halves[1], halves[0])
    other[...] = jnp.where(second, halves[0], halves[1])
    own = lambda u, v: table[u, family[0, 0], v]
    build_main(own, w_high, w_low, (), width)
    n = height * EDGE
    shape = (EDGE, n)
    lane = lanes(shape)
    c = lax.broadcasted_iota(jnp.int32, shape, 0)
    delta = side_column(c, width) - rim_column(lane, width) + RADIUS
    out_row = lane // EDGE
    bands = [band_sum([own(u, v) for v in range(KS)], delta) for u in range(KS)]
    rows = s_high.shape[0] // EDGE
    for a in range(0, rows, 2):
        blocks = []
        for b in (a, a + 1):
            total = jnp.zeros(shape, F32)
            for u in range(KS):
                total = jnp.where(out_row == b - u, bands[u], total)
            blocks.append(total)
        high, low = split(jnp.concatenate(blocks, axis=0))
        s_high[a * EDGE : a * EDGE + 2 * EDGE] = high
        s_low[a * EDGE : a * EDGE + 2 * EDGE] = low
    for i in range(height):
        copies[i].wait()
    sub = lax.broadcasted_iota(jnp.int32, (seen_ref.shape[1] - start, width), 0)
    for i in range(height):
        seen_ref[i, start:] = jnp.where(sub < depth - start, seen_ref[i, start:], 0.0)


def flipped(table, family):
    return lambda u, v: table[KS - 1 - u, family, KS - 1 - v]


def own_weights_kernel(marks, table, w_high, w_low):
    family = jnp.max(marks[8:16]).astype(jnp.int32)
    build_main(flipped(table, family), w_high, w_low, (), w_high.shape[1] // 2)


def halo_weights_kernel(
    marks_up, marks, marks_down, table, w_high, w_low, s_high, s_low, scratch, *, height, width
):
    families = []
    for ref in (marks_up, marks, marks_down):
        for k in range(3):
            families.append(jnp.max(ref[8 * k : 8 * k + 8]).astype(jnp.int32))
    for b in range(2):
        build_main(flipped(table, families[6 * b + 1]), w_high, w_low, (b,), width)
    n = s_high.shape[1]
    half = n // 2
    shape = (EDGE, n)
    lane = lanes(shape)
    c = lax.broadcasted_iota(jnp.int32, shape, 0)
    to_side = lane < half
    column = jnp.where(to_side, side_column(lane, width), rim_column(lane, width))
    out_row = jnp.where(to_side, lane, lane - half) // EDGE
    out_row = jnp.where(out_row < height + EDGE, out_row, -KS - 1)
    sources = (c - EDGE, width + c, rim_column(c, width))
    chunk = height * EDGE
    mid = chunk // 2

    def place_of(kind, q):
        i = q - EDGE
        if kind == 2:
            return 4 * chunk + q * EDGE
        if 0 <= i < height:
            return i * EDGE if kind == 0 else chunk + (i + height // 2) % height * EDGE
        if i < 0:
            return 2 * chunk + (mid if kind == 0 else 0) + q * EDGE
        return 3 * chunk + (0 if kind == 0 else mid) + (i - height) * EDGE

    for kind in range(3):
        delta = sources[kind] - column + RADIUS
        if kind == 2:
            delta = jnp.where(to_side, delta, -1)
        for b in range(3):
            tile = 3 * b + (0, 2, 1)[kind]
            bands = [
                band_sum([table[KS - 1 - u, families[tile], KS - 1 - v] for v in range(KS)], delta) for u in range(KS)
            ]
            q_range = (range(0, EDGE), range(EDGE, EDGE + height), range(EDGE + height, 2 * EDGE + height))[b]
            for q in q_range:
                total = jnp.zeros(shape, F32)
                for u in range(KS):
                    if 0 <= q - u < height + EDGE:
                        total = jnp.where(out_row == q - u, bands[u], total)
                at = place_of(kind, q)
                scratch[at : at + EDGE] = total
    for start in range(0, scratch.shape[0], 64):
        high, low = split(scratch[start : start + 64])
        s_high[start : start + 64] = high
        s_low[start : start + 64] = low


def blur_into(b_ref, a2_high, a2_low, side, w_high, w_low, s_high, s_low, acc):
    pairs, channels, double = acc.shape
    width = double // 2
    for d in range(RADIUS + 1):
        high = a2_high[d : d + pairs].reshape(pairs * channels, double)
        low = a2_low[d : d + pairs].reshape(pairs * channels, double)
        part = mm_split(high, low, w_high[d], w_low[d])
        part = part.reshape(pairs, channels, double)
        if d == 0:
            acc[...] = part
        else:
            acc[...] += part
    side_high, side_low = split(side)
    rim = mm_split(side_high, side_low, s_high[...], s_low[...])
    for i in range(2 * pairs):
        row = acc[i // 2, :, i % 2 * width : i % 2 * width + width]
        b_ref[i] = add_rim(row, rim, i)


def start_kernel(
    rows_ref, p1, p2, left, right, above, below, place, w_high, w_low, s_high, s_low,
    ext_ref, side_ref, b_ref, a2_high, a2_low, acc,
):
    height, channels, width = rows_ref.shape
    odd = place[ROW_ODD] == 1
    for a in range(height + EDGE):
        if a < RADIUS:
            row = jnp.where(odd, p1[a * channels : a * channels + channels], p2[a * channels : a * channels + channels])
            row = jnp.where(place[UP] == 1, row, 0.0)
        elif a < RADIUS + height:
            row = rows_ref[a - RADIUS]
        else:
            k = (a - RADIUS - height) * channels
            row = jnp.where(odd, p2[k : k + channels], p1[k : k + channels])
            row = jnp.where(place[DOWN] == 1, row, 0.0)
        ext_ref[a] = row
        high, low = split(row)
        a2_high[a // 2, :, a % 2 * width : a % 2 * width + width] = high
        a2_low[a // 2, :, a % 2 * width : a % 2 * width + width] = low
    side = assemble_side(left[...], right[...], above[...], below[...], height)
    side_ref[...] = side
    blur_into(b_ref, a2_high, a2_low, side, w_high, w_low, s_high, s_low, acc)


def spectral_kernel(
    obs_ref, bend_ref, b_ref, mine, other, place,
    g_mine, core_ref, main1, main2, cross_ref, rows_ref,
    total, *, scale,
):
    height, channels, width = b_ref.shape
    bands = obs_ref.shape[1]
    quarter = bands // 4
    second = place[HALF] == 1
    m0 = jnp.where(second, other[...], mine[...])
    m1 = jnp.where(second, mine[...], other[...])
    spectra = jnp.concatenate([m0[:, :channels], m0[:, channels:], m1[:, :channels], m1[:, channels:]], axis=0)
    m_high, m_low = split(spectra)
    m_cat = jnp.concatenate([m_high, m_low, m_high], axis=1)
    t_high, t_low = split(spectra.T)
    t_cat = jnp.concatenate([t_high, t_low], axis=0)
    rows = []
    for pair in range(height // 2):
        b_pair = jnp.concatenate([b_ref[2 * pair], b_ref[2 * pair + 1]], axis=1)
        b_high, b_low = split(b_pair)
        b_cat = jnp.concatenate([b_high, b_high, b_low], axis=0)
        linear = mm(m_cat, b_cat) * scale
        seen = jnp.concatenate([obs_ref[2 * pair], obs_ref[2 * pair + 1]], axis=1)
        bend = jnp.concatenate([bend_ref[2 * pair : 2 * pair + 1], bend_ref[2 * pair + 1 : 2 * pair + 2]], axis=1)
        bent = bend * linear
        resid = linear + bent * linear - seen
        weighted = resid * (1.0 + 2.0 * bent)
        w_high, w_low = split(weighted)
        part = mm_nt(w_high, jnp.concatenate([b_high, b_low], axis=0))
        part = part[:, :channels] + part[:, channels:] + mm_nt(w_low, b_high)
        if pair == 0:
            total[...] = part
        else:
            total[...] += part
        both = mm(t_cat, w_high)
        grad = (both[:channels] + both[channels:] + mm(t_high, w_low)) * scale
        for k in range(2):
            row = grad[:, k * width : k * width + width]
            rows_ref[2 * pair + k] = row
            rows.append(row)
    low, high = edges(rows, True), edges(rows, False)
    col_odd = place[COL_ODD] == 1
    core_ref[2 * quarter // 2 :] = jnp.where(col_odd, low, high)
    cross_ref[...] = jnp.where(col_odd, high, low)
    row_odd = place[ROW_ODD] == 1
    halo = main1.shape[0]
    for i in range(halo):
        main1[i] = jnp.where(row_odd, rows[i], rows[height - halo + i])
        main2[i] = jnp.where(row_odd, rows[height - halo + i], rows[i])
    g = total[...] * scale
    g0 = jnp.concatenate([g[:quarter], g[quarter : 2 * quarter]], axis=1)
    g1 = jnp.concatenate([g[2 * quarter : 3 * quarter], g[3 * quarter :]], axis=1)
    g_mine[...] = jnp.where(second, g1, g0)
    core_ref[:quarter] = jnp.where(second, g0, g1)


def put_pair(high_ref, low_ref, index, row):
    width = row.shape[1]
    at = (index // 2, slice(None), slice(index % 2 * width, index % 2 * width + width))
    high_ref[at], low_ref[at] = split(row)


def adjoint_into(acc, g_high, g_low, first, w_high, w_low):
    pairs, channels, double = g_high.shape
    for d in range(RADIUS + 1):
        begin, end = max(first, d), min(first + pairs, acc.shape[0] + d)
        if begin >= end:
            continue
        high = g_high[begin - first : end - first].reshape((end - begin) * channels, double)
        low = g_low[begin - first : end - first].reshape((end - begin) * channels, double)
        part = mm_split(high, low, w_high[d], w_low[d])
        acc[begin - d : end - d] += part.reshape(end - begin, channels, double)


def own_maps_kernel(rows_ref, wa_high, wa_low, acc, near_ref, g_high, g_low):
    height, channels, width = rows_ref.shape
    lane = lanes((channels, width))
    near = [jnp.zeros((channels, width), F32) for _ in range(2)]
    for i in range(height):
        row = rows_ref[i]
        put_pair(g_high, g_low, i, row)
        q = i + EDGE
        moved = pltpu.roll(row, (RADIUS + q * EDGE) % width, 1)
        near[q // height] = jnp.where(lane // EDGE == q % height, moved, near[q // height])
    near_ref[...] = jnp.concatenate(near, axis=1)
    acc[...] = jnp.zeros_like(acc)
    adjoint_into(acc, g_high, g_low, EDGE // 2, wa_high, wa_low)


def halo_maps_kernel(acc_in, near_in, p1, p2, place, wa_high, wa_low, acc, near_ref, g_high, g_low):
    channels = near_in.shape[0]
    width = near_in.shape[1] // 2
    height = 2 * acc.shape[0] - EDGE
    odd = place[ROW_ODD] == 1
    lane = lanes((channels, width))
    near = [near_in[:, :width], near_in[:, width:]]
    halo = p1.shape[0]
    for k in range(2 * halo):
        if k < halo:
            q = EDGE - halo + k
            row = jnp.where(place[UP] == 1, jnp.where(odd, p1[k], p2[k]), 0.0)
        else:
            q = EDGE + height + k - halo
            row = jnp.where(place[DOWN] == 1, jnp.where(odd, p2[k - halo], p1[k - halo]), 0.0)
        put_pair(g_high, g_low, k, row)
        moved = pltpu.roll(row, (RADIUS + q * EDGE) % width, 1)
        near[q // height] = jnp.where(lane // EDGE == q % height, moved, near[q // height])
    near_ref[...] = jnp.concatenate(near, axis=1)
    n = halo // 2
    adjoint_into(acc, g_high.at[:n], g_low.at[:n], EDGE // 2 - n, wa_high.at[0], wa_low.at[0])
    adjoint_into(acc, g_high.at[n:], g_low.at[n:], (EDGE + height) // 2, wa_high.at[1], wa_low.at[1])


def maps_kernel(
    ext_ref, side_ref, acc, near_ref, left, right, above, below, place, sa_high, sa_low, *rest, last,
):
    if last:
        (out_ref,) = rest
        height = out_ref.shape[1]
    else:
        (wf_high, wf_low, sf_high, sf_low, ext_out, side_out, b_ref, a2_high, a2_low, acc_b) = rest
        height = b_ref.shape[0]
    width = left.shape[1]
    ext_rows = height + EDGE
    side_in = jnp.concatenate([left[...], right[...], above[...], below[...], near_ref[...]], axis=1)
    side_high, side_low = split(side_in)
    half = sa_high.shape[1] // 2
    far = sa_high.shape[0] - 2 * width
    rim = mm_split(side_high[:, :far], side_low[:, :far], sa_high[:far, half:], sa_low[:far, half:])
    for a in range(ext_rows):
        if last and not RADIUS <= a < RADIUS + height:
            continue
        grad = add_rim(acc[a // 2, :, a % 2 * width : a % 2 * width + width], rim, a)
        row = jnp.maximum(ext_ref[a] - 0.5 * grad, 0.0)
        if last:
            out_ref[:, a - RADIUS, :] = row
            continue
        if a < RADIUS:
            row = jnp.where(place[UP] == 1, row, 0.0)
        elif a >= RADIUS + height:
            row = jnp.where(place[DOWN] == 1, row, 0.0)
        ext_out[a] = row
        put_pair(a2_high, a2_low, a, row)
    if last:
        return
    side_grad = mm_split(side_high, side_low, sa_high[:, :half], sa_low[:, :half])
    side = jnp.maximum(side_ref[...] - 0.5 * side_grad, 0.0)
    where = lanes(side.shape)
    a, c = where // EDGE, where % EDGE
    outside = (
        ((a < RADIUS) & (place[UP] == 0))
        | ((a >= RADIUS + height) & (place[DOWN] == 0))
        | ((c < RADIUS) & (place[LEFT] == 0))
        | ((c >= RADIUS) & (place[RIGHT] == 0))
        | (a >= ext_rows)
    )
    side = jnp.where(outside, 0.0, side)
    side_out[...] = side
    blur_into(b_ref, a2_high, a2_low, side, wf_high, wf_low, sf_high, sf_low, acc_b)


def turn_kernel(half_ref, out_ref):
    channels, width = out_ref.shape
    half = jnp.concatenate([half_ref[:, :channels], half_ref[:, channels:]], axis=0)
    rest = jnp.zeros((width - half.shape[0], channels), F32)
    out_ref[...] = jnp.concatenate([half, rest], axis=0).T


def call(kernel, micros, outs, scratch, specs, *args, aliases=None):
    return pl.pallas_call(
        kernel,
        out_shape=[jax.ShapeDtypeStruct(s, d) for s, d in outs],
        in_specs=specs,
        out_specs=[VMEM] * len(outs),
        scratch_shapes=[pltpu.VMEM(*s) if isinstance(s, tuple) else s for s in scratch],
        input_output_aliases=aliases or {},
        compiler_params=PARAMS,
        cost_estimate=pl.CostEstimate(
            flops=int(micros * 1.15e9), bytes_accessed=int(micros * 3.7e6), transcendentals=0
        ),
    )(*args)


def core_swap(x):
    count = lax.axis_size("cols")
    return lax.ppermute(x, "cols", [(i, i ^ 1) for i in range(count)])


def cross_swap(x):
    count = lax.axis_size("cols")
    return lax.ppermute(x, "cols", [(i, (i + 1 if i % 2 else i - 1) % count) for i in range(count)])


def pair_one(x):
    count = lax.axis_size("rows")
    return lax.ppermute(x, "rows", [(i, i ^ 1) for i in range(count)])


def pair_two(x):
    count = lax.axis_size("rows")
    return lax.ppermute(x, "rows", [(i, min(max(i + 1 if i % 2 else i - 1, 0), count - 1)) for i in range(count)])


def col_swap(x, mask):
    count = lax.axis_size("cols")
    return lax.ppermute(x, "cols", [(i, (((i + 1) % count ^ mask) - 1) % count) for i in range(count)])


def row_swap(x, mask):
    count = lax.axis_size("rows")
    return lax.ppermute(x, "rows", [(i, i ^ mask) for i in range(count)])


def on_device(observed, nonlin, abundance, spectra, kernels, tile_family):
    bands, height, width = observed.shape
    channels = abundance.shape[0]
    n_rows, n_cols = lax.axis_size("rows"), lax.axis_size("cols")
    row_at, col_at = lax.axis_index("rows"), lax.axis_index("cols")
    pixel_count = height * width * n_rows * n_cols
    quarter = -(-bands // 32) * 8
    full = 4 * quarter
    half_of = ((col_at + 1) // 2) % 2
    col_odd, row_odd = col_at % 2 == 1, row_at % 2 == 1
    place = jnp.stack(
        [row_at % 2, col_at % 2, row_at > 0, row_at < n_rows - 1, col_at > 0, col_at < n_cols - 1, half_of]
    ).astype(jnp.int32)
    has_left = (col_at > 0).astype(F32)
    has_right = (col_at < n_cols - 1).astype(F32)
    has_up = (row_at > 0).astype(F32)
    has_down = (row_at < n_rows - 1).astype(F32)
    table = jnp.transpose(kernels, (1, 0, 2))
    second_half = half_of == 1
    place, abundance, second_half, row_odd, col_odd, has_left, has_right, has_up, has_down = lax.optimization_barrier(
        (place, abundance, second_half, row_odd, col_odd, has_left, has_right, has_up, has_down)
    )
    tile = (channels, width)

    def sides(core, cross):
        left = jnp.where(col_odd, core, cross) * has_left
        right = jnp.where(col_odd, cross, core) * has_right
        lane = lanes(tile) < width // 2
        up_msg = jnp.where(lane, left, right)
        down_msg = jnp.where(lane, right, left)
        return left, right, jnp.where(row_odd, up_msg, down_msg), jnp.where(row_odd, down_msg, up_msg)

    a_rows, e_core, e_cross, mark = call(
        first_kernel,
        1,
        [((height,) + tile, F32), ((channels + 8, width), F32), ((channels + 8, width), F32), ((8, width), F32)],
        [],
        [SMEM, VMEM, SMEM],
        tile_family, abundance, place,
    )
    got_core = core_swap(e_core)
    got_cross = cross_swap(e_cross)
    left, right, side1, side2 = sides(got_core[:channels], got_cross[:channels])
    mark_left = jnp.where(col_odd, got_core[channels:], got_cross[channels:])
    mark_right = jnp.where(col_odd, got_cross[channels:], got_core[channels:])
    marks = jnp.concatenate([mark_left, mark, mark_right])
    top = a_rows[:RADIUS].reshape(RADIUS * channels, width)
    bottom = a_rows[height - RADIUS :].reshape(RADIUS * channels, width)
    got1 = pair_one(jnp.concatenate([jnp.where(row_odd, top, bottom), side1, marks]))
    got2 = pair_two(jnp.concatenate([jnp.where(row_odd, bottom, top), side2, marks]))
    body = RADIUS * channels

    def above_below(x1, x2):
        return jnp.where(row_odd, x1, x2), jnp.where(row_odd, x2, x1)

    above, below = above_below(got1[body : body + channels], got2[body : body + channels])
    above, below = above * has_up, below * has_down
    pairs = height // 2
    ext_rows = height + EDGE
    main_w = ((RADIUS + 1, 2 * width, 2 * width), BF16)
    side_f = ((2 * width, height * EDGE), BF16)
    hbm = pl.BlockSpec(memory_space=pltpu.HBM)
    half_shape = ((quarter, 2 * channels), F32)
    seen, mine, other, *wf = call(
        forward_weights_kernel,
        3,
        [((height, full, width), F32), half_shape, half_shape, main_w, main_w, side_f, side_f],
        [pltpu.SemaphoreType.DMA((height,))],
        [SMEM, SMEM, SMEM, hbm, VMEM],
        tile_family, table, place, observed, spectra.T,
    )
    got1, got2, seen, mine, other, *wf = lax.optimization_barrier((got1, got2, seen, mine, other, *wf))
    ext, side, blurred = call(
        start_kernel,
        2,
        [((ext_rows,) + tile, F32), ((channels, 2 * width), F32), ((height,) + tile, F32)],
        [((ext_rows // 2, channels, 2 * width), BF16)] * 2 + [((pairs, channels, 2 * width), F32)],
        [VMEM] * 7 + [SMEM] + [VMEM] * 4,
        a_rows, got1, got2, left, right, above, below, place, *wf,
    )
    marks_up, marks_down = above_below(got1[body + channels :], got2[body + channels :])
    main_a = ((2, RADIUS + 1, 2 * width, 2 * width), BF16)
    side_a = ((6 * width, 4 * width), BF16)

    def halo_weights(marks):
        return call(
            functools.partial(halo_weights_kernel, height=height, width=width),
            3,
            [main_a, main_a, side_a, side_a],
            [((6 * width, 4 * width), F32)],
            [VMEM, VMEM, VMEM, SMEM],
            marks_up, marks, marks_down, table,
        )

    rate = 40.0 / pixel_count
    acc_shape = ((ext_rows // 2, channels, 2 * width), F32)
    near_shape = ((channels, 2 * width), F32)

    def own_part(g_rows):
        return call(
            own_maps_kernel,
            2,
            [acc_shape, near_shape],
            [((pairs, channels, 2 * width), BF16)] * 2,
            [VMEM] * 3,
            g_rows, *w_own,
        )

    for step in range(ITERS):
        last = step == ITERS - 1
        halo = RADIUS if last else EDGE
        g_mine, to_core, main1, main2, e_cross, g_rows = call(
            functools.partial(spectral_kernel, scale=1.0 / channels),
            5,
            [
                ((quarter, 2 * channels), F32),
                ((quarter + channels, width), F32),
                ((halo,) + tile, F32),
                ((halo,) + tile, F32),
                (tile, F32),
                ((height,) + tile, F32),
            ],
            [((full, channels), F32)],
            [VMEM] * 5 + [SMEM],
            seen, nonlin, blurred, mine, other, place,
        )
        got_core = core_swap(to_core)
        p1 = pair_one(main1)
        share = g_mine + got_core[:quarter]
        main2, share = lax.optimization_barrier((main2, share))
        p2 = pair_two(main2)
        message = jnp.concatenate([share, e_cross])
        got_cross = cross_swap(message)
        at_once = last and n_cols >= 8
        if at_once:
            got_four = col_swap(message, 4)
            got_five = col_swap(message, 5)
            share = (share + got_cross[:quarter]) + (got_four[:quarter] + got_five[:quarter])
        else:
            share = share + got_cross[:quarter]
        if step == 0:
            share, marks = lax.optimization_barrier((share, marks))
            wa = halo_weights(marks)
        else:
            share, g_rows = lax.optimization_barrier((share, g_rows))
            own, near = own_part(g_rows)
        left, right, side1, side2 = sides(got_core[quarter:], got_cross[quarter:])
        step_size = 8 if at_once else 4
        while step_size < n_cols:
            share = share + col_swap(share, step_size)
            step_size *= 2
        if step == 0:
            share, *wa = lax.optimization_barrier((share, *wa))
            got1 = pair_one(jnp.concatenate([share, side1]))
            g_rows, marks, p1 = lax.optimization_barrier((g_rows, marks, p1))
            got1, p2 = lax.optimization_barrier((got1, p2))
            w_own = call(own_weights_kernel, 1, [main_w, main_w], [], [VMEM, SMEM], marks, table)
            own, near = own_part(g_rows)
        else:
            if not at_once:
                share, own, near = lax.optimization_barrier((share, own, near))
            got1 = pair_one(jnp.concatenate([share, side1]))
        own, near = call(
            halo_maps_kernel,
            1.5,
            [acc_shape, near_shape],
            [((halo, channels, 2 * width), BF16)] * 2,
            [VMEM] * 4 + [SMEM] + [VMEM] * 2,
            own, near, p1, p2, place, wa[0], wa[1],
            aliases={0: 0, 1: 1},
        )
        if n_rows == 4:
            got2 = row_swap(jnp.concatenate([share, side2]), 3)
            got3 = row_swap(share, 2)
            got1, got2, own, near = lax.optimization_barrier((got1, got2, own, near))
            share = (share + got1[:quarter]) + (got3 + got2[:quarter])
            got2 = got2[quarter:]
        else:
            got2 = pair_two(side2)
            got1, got2, own, near = lax.optimization_barrier((got1, got2, own, near))
            share = share + got1[:quarter]
            step_size = 2
            while step_size < n_rows:
                share = share + row_swap(share, step_size)
                step_size *= 2
        above, below = above_below(got1[quarter:], got2)
        above, below = above * has_up, below * has_down
        gathered = (ext, side, own, near, left, right, above, below, place) + tuple(wa[2:])
        if last:
            made = call(
                functools.partial(maps_kernel, last=True),
                1.5,
                [((channels, height, width), F32)],
                [],
                [VMEM] * 8 + [SMEM] + [VMEM] * 2,
                *gathered,
            )
        else:
            made = call(
                functools.partial(maps_kernel, last=False),
                2.5,
                [((ext_rows,) + tile, F32), ((channels, 2 * width), F32), ((height,) + tile, F32)],
                [((ext_rows // 2, channels, 2 * width), BF16)] * 2 + [((pairs, channels, 2 * width), F32)],
                [VMEM] * 8 + [SMEM] + [VMEM] * 6,
                *gathered, *wf,
            )
        mine = jnp.maximum(mine - rate * share, 0.0)
        if last:
            (out,) = made
            (mine,) = call(turn_kernel, 0.5, [((channels, -(-2 * quarter // 128) * 128), F32)], [], [VMEM], mine)
        other = core_swap(mine)
        if not last:
            ext, side, blurred = made
    low = jnp.where(second_half, other, mine)[:, : 2 * quarter]
    high = jnp.where(second_half, mine, other)[:, : bands - 2 * quarter]
    return out, jnp.concatenate([low, high], axis=1).T


def solution(mesh):
    placed = (
        P(None, "rows", "cols"),
        P("rows", "cols"),
        P(None, "rows", "cols"),
        P(),
        P(),
        P("rows", "cols"),
    )
    return jax.shard_map(
        on_device,
        mesh=mesh,
        in_specs=placed,
        out_specs=(P(None, "rows", "cols"), P()),
        check_vma=False,
    )
```
